32 devices in a mesh: dp: 16 (over z, y, x), fsdp: 2 (over core).
Axes of the slice: x: 2, y: 2, z: 4, core: 2. Of those that a mesh axis runs over, the one named last changes fastest.
Arguments:
- features: bfloat16 [32, 576, 1024], P(('dp', 'fsdp')), may hold values from -6 to 6
- grid_live: int32 [32], P(('dp', 'fsdp')), may hold values 0 or 1
- pos_embed: bfloat16 [576, 1024], P(None, ('dp', 'fsdp')), may hold values from -3 to 3
- w_in: bfloat16 [2, 1024, 1024], P(None, ('dp', 'fsdp')), may hold values from -0.1875 to 0.1875
- w_mid: bfloat16 [2, 9216, 1024], P(None, ('dp', 'fsdp')), may hold values from -0.0625 to 0.0625
- w_out: bfloat16 [2, 1024, 1024], P(None, ('dp', 'fsdp')), may hold values from -0.1875 to 0.1875
- norm_gain: bfloat16 [2, 3, 1024], P(None, None, ('dp', 'fsdp')), may hold values from 0.099609375 to 1.8984375
- norm_bias: bfloat16 [2, 3, 1024], P(None, None, ('dp', 'fsdp')), may hold values from -1.5 to 1.5
- readout_w: bfloat16 [1024, 4096], P(('dp', 'fsdp')), may hold values from -0.1875 to 0.1875
- readout_b: bfloat16 [4096], P(('dp', 'fsdp')), may hold values from -1.5 to 1.5
- cotangent: bfloat16 [32, 144, 4096], P(('dp', 'fsdp')), may hold values from -6 to 6
Outputs:
- output: bfloat16 [32, 144, 4096], P(('dp', 'fsdp'))
- input_grad: float32 [32, 576, 1024], P(('dp', 'fsdp'))
- pos_grad: float32 [576, 1024], P(None, ('dp', 'fsdp'))
- w_in_grad: float32 [2, 1024, 1024], P(None, ('dp', 'fsdp'))
- w_mid_grad: float32 [2, 9216, 1024], P(None, ('dp', 'fsdp'))
- w_out_grad: float32 [2, 1024, 1024], P(None, ('dp', 'fsdp'))
- gain_grad: float32 [2, 3, 1024], P(None, None, ('dp', 'fsdp'))
- bias_grad: float32 [2, 3, 1024], P(None, None, ('dp', 'fsdp'))
- readout_w_grad: float32 [1024, 4096], P(('dp', 'fsdp'))
- readout_b_grad: float32 [4096], P(('dp', 'fsdp'))
The draws below stay inside these ranges and needn't reach their ends.
All inputs are finite; a program needn't handle non-finite values. No bound on the sum of `grid_live` on one device may be relied on, other than what follows from the above.
Results may differ from the reference program's by a relative error of at most 0.018.
Values may be sent and summed in bfloat16 or wider, within the bound.
No kernel may reach another device: no remote copies, remote signals or barrier semaphores. Data moves between devices by JAX's collectives and lax.ppermute only.
A program may use at most 448 MiB of HBM per device.

```python
import jax
import jax.numpy as jnp
from jax import lax

C = 1024
R = 4096
G = 24
PATCHES = 576
POOLED = 144
SLOTS = 32


def touch_ends(drawn, key, smallest, top_value):
    extent = drawn.shape
    index_at = [jax.random.randint(jax.random.fold_in(key, axis), (), 0, extent[axis]) for axis in range(len(extent))]
    drawn = drawn.at[tuple(index_at)].set(smallest)
    longest = extent.index(max(extent))
    index_at[longest] = (index_at[longest] + 1) % extent[longest]
    return drawn.at[tuple(index_at)].set(top_value)


def spiked(values, own_key, source, target, shards_of, factor):
    owner, partner = [(jnp.arange(values.shape[position]) // (values.shape[position] // shards_of)).reshape([-1 if axis == position else 1 for axis in range(values.ndim)]) for position in (source, target)]
    chosen = jax.random.permutation(own_key, shards_of)[partner]
    strong = (owner == chosen) | (owner == (partner + shards_of // 2) % shards_of)
    return jnp.where(strong, factor * values, values)


def levels(own_key, extent, cuts, low, largest):
    factor_of = 1.0
    for axis_at, blocks in cuts:
        heights = jax.random.uniform(jax.random.fold_in(jax.random.fold_in(own_key, 6), axis_at), (blocks,), jnp.float32, low / len(cuts), largest / len(cuts))
        factor_of = factor_of * jnp.repeat(jnp.exp(heights), extent[axis_at] // blocks).reshape((-1,) + (1,) * (len(extent) - 1 - axis_at))
    return factor_of


def scatter_about(own_key, shape, deviation, limit, split=(), held_as=jnp.bfloat16):
    loudness = levels(own_key, shape, split, -0.22, 0.18) if split else 1.0
    values = jax.random.normal(own_key, shape, jnp.float32) * deviation * loudness
    return jnp.minimum(jnp.maximum(values, -limit), limit).astype(held_as)


def heavy_noise(rng, dims, scale, most, split, heavy, dtype=jnp.bfloat16):
    values = scale * jax.random.normal(rng, dims, jnp.float32)
    if split:
        values = values * levels(rng, dims, split, -0.22, 0.18)
    return jnp.clip(spiked(values, jax.random.fold_in(rng, 3), *heavy), -most, most).astype(dtype)


def setup_inputs(seed: int = 0) -> dict:
    key_of = jax.random.split(jax.random.key(seed), 12)
    return {
        "features": heavy_noise(key_of[0], (SLOTS, PATCHES, C), 1.0, 6.0, ((0, 32),), (0, 2, 32, 2.75)),
        "grid_live": touch_ends((jax.random.randint(key_of[1], (SLOTS,), 0, 8) < 5).astype(jnp.int32), jax.random.fold_in(key_of[1], 1), 0, 1),
        "pos_embed": scatter_about(key_of[2], (PATCHES, C), 0.5, 3.0, ((1, 32),)),
        "w_in": scatter_about(key_of[3], (2, C, C), C ** -0.5, 0.1875, ((1, 32),)),
        "w_mid": scatter_about(key_of[4], (2, 9 * C, C), (9 * C) ** -0.5, 0.0625, ((1, 32),)),
        "w_out": scatter_about(key_of[5], (2, C, C), C ** -0.5, 0.1875, ((1, 32),)),
        "norm_gain": jnp.clip(1.0 + 0.18 * jax.random.normal(key_of[6], (2, 3, C), jnp.float32), 0.099609375, 1.8984375).astype(jnp.bfloat16),
        "norm_bias": scatter_about(key_of[7], (2, 3, C), 0.3, 1.5, ((2, 32),)),
        "readout_w": scatter_about(key_of[8], (C, R), C ** -0.5, 0.1875, ((0, 32),)),
        "readout_b": scatter_about(key_of[9], (R,), 0.3, 1.5, ((0, 32),)),
        "cotangent": scatter_about(key_of[10], (SLOTS, POOLED, R), 1.0, 6.0, ((0, 32),)),
    }


@jax.custom_vjp
def low(v):
    return lax.optimization_barrier(v.astype(jnp.bfloat16)).astype(jnp.float32)

@jax.custom_vjp
def low_back(v):
    return v

def low_keep(v):
    return (low(v), None)

def low_pass(kept, grad):
    return (grad,)

def back_keep(v):
    return (v, None)

def back_low(kept, grad):
    return (low(grad),)
low.defvjp(low_keep, low_pass)
low_back.defvjp(back_keep, back_low)

def layer_norm(hidden, gain_vec, bias_vec):
    center = hidden - lax.optimization_barrier(jnp.mean(hidden, axis=-1, keepdims=True))
    spread = lax.optimization_barrier(jnp.mean(center * center, axis=-1, keepdims=True))
    return center * lax.rsqrt(spread + 1e-05) * gain_vec + bias_vec

def columns(values, grid_side):
    leading = values.shape[:-2]
    channels = values.shape[-1]
    grid_vals = values.reshape(leading + (grid_side, grid_side, channels))
    padded = jnp.pad(grid_vals, [(0, 0)] * len(leading) + [(1, 1), (1, 1), (0, 0)])
    pieces = [padded[..., row_tap:row_tap + grid_side, col_tap:col_tap + grid_side, :] for row_tap in range(3) for col_tap in range(3)]
    return jnp.concatenate(pieces, axis=-1).reshape(leading + (grid_side * grid_side, 9 * channels))

def project(values, weight):
    return jnp.einsum('spk,kn->spn', values, weight, precision=lax.Precision.HIGHEST)

def block(stream, weights, grid_side):
    w_first, w_middle, w_last, gain_rows, bias_rows = weights
    pre_first = low_back(project(low(stream), w_first))
    act_first = jax.nn.silu(layer_norm(pre_first, gain_rows[0], bias_rows[0]))
    pre_middle = low_back(project(columns(low(act_first), grid_side), w_middle))
    act_middle = jax.nn.silu(layer_norm(pre_middle, gain_rows[1], bias_rows[1]))
    pre_last = low_back(project(low(act_middle), w_last))
    return jax.nn.silu(stream + layer_norm(pre_last, gain_rows[2], bias_rows[2]))

def pool_grid(stream, grid_side):
    half_side = grid_side // 2
    shaped = stream.reshape(stream.shape[0], half_side, 2, half_side, 2, stream.shape[-1])
    return lax.optimization_barrier(jnp.mean(shaped, axis=(2, 4))).reshape(stream.shape[0], half_side * half_side, stream.shape[-1])

def forward(group_feats, live_mask, pos_embed, w_in, w_mid, w_out, norm_gain, norm_bias, readout_w, readout_b):
    stream = group_feats + pos_embed
    stream = block(stream, (w_in[0], w_mid[0], w_out[0], norm_gain[0], norm_bias[0]), G)
    stream = pool_grid(stream, G)
    stream = block(stream, (w_in[1], w_mid[1], w_out[1], norm_gain[1], norm_bias[1]), G // 2)
    logits = low_back(project(low(stream), readout_w) + readout_b)
    return jax.nn.gelu(logits, approximate=False) * live_mask[:, None, None]

def reference(features, grid_live, pos_embed, w_in, w_mid, w_out, norm_gain, norm_bias, readout_w, readout_b, cotangent):
    params = tuple((tensor.astype(jnp.float32) for tensor in (pos_embed, w_in, w_mid, w_out, norm_gain, norm_bias, readout_w, readout_b)))
    groups = SLOTS // 4
    inputs = features.astype(jnp.float32).reshape(groups, 4, PATCHES, C)
    mask_rows = grid_live.astype(jnp.float32).reshape(groups, 4)
    cot_rows = cotangent.astype(jnp.float32).reshape(groups, 4, POOLED, R)

    def one_group(summed, entries):
        group_in, group_mask, group_cot = entries

        def run_group(group_feats, *weights):
            return forward(group_feats, group_mask, *weights)
        result, pullback = jax.vjp(run_group, group_in, *params)
        gradients = pullback(group_cot)
        summed = tuple((before + added for before, added in zip(summed, gradients[1:])))
        return (summed, (result, gradients[0]))
    initial = tuple((jnp.zeros(tensor.shape, jnp.float32) for tensor in params))
    summed, (results, input_grads) = lax.scan(one_group, initial, (inputs, mask_rows, cot_rows))
    return (results.reshape(SLOTS, POOLED, R).astype(jnp.bfloat16), input_grads.reshape(SLOTS, PATCHES, C), summed[0], summed[1], summed[2], summed[3], summed[4], summed[5], summed[6], summed[7])
```

```python
import functools

import jax
import jax.numpy as jnp
from jax import lax
from jax.experimental import pallas as pl
from jax.experimental.pallas import tpu as pltpu
from jax.sharding import PartitionSpec as P

C = 1024
G = 24


def product(left, right):
    return jnp.dot(left, right, preferred_element_type=jnp.float32)


def times_transposed(left, right):
    return lax.dot_general(
        left, right, (((1,), (1,)), ((), ())), preferred_element_type=jnp.float32
    )


def outer_sum(left, right):
    return lax.dot_general(
        left, right, (((0,), (0,)), ((), ())), preferred_element_type=jnp.float32
    )


def layer_norm(hidden, gain_vec, bias_vec):
    center = hidden - jnp.mean(hidden, axis=-1, keepdims=True)
    spread = jnp.mean(center * center, axis=-1, keepdims=True)
    return center * lax.rsqrt(spread + 1e-05) * gain_vec + bias_vec


def norm_act(hidden, gain_vec, bias_vec):
    return jax.nn.silu(layer_norm(hidden, gain_vec, bias_vec))


def closing(stream, hidden, gain_vec, bias_vec):
    return jax.nn.silu(stream + layer_norm(hidden, gain_vec, bias_vec))


def columns(values, grid_side):
    channels = values.shape[-1]
    padded = jnp.pad(values.reshape(grid_side, grid_side, channels), ((1, 1), (1, 1), (0, 0)))
    pieces = [
        padded[row_tap : row_tap + grid_side, col_tap : col_tap + grid_side, :]
        for row_tap in range(3)
        for col_tap in range(3)
    ]
    return jnp.concatenate(pieces, axis=-1).reshape(grid_side * grid_side, 9 * channels)


def back_columns(values, grid_side):
    channels = values.shape[-1]
    padded = jnp.pad(values.reshape(grid_side, grid_side, channels), ((1, 1), (1, 1), (0, 0)))
    pieces = [
        padded[2 - row_tap : 2 - row_tap + grid_side, 2 - col_tap : 2 - col_tap + grid_side, :]
        for row_tap in range(3)
        for col_tap in range(3)
    ]
    return jnp.concatenate(pieces, axis=-1).reshape(grid_side * grid_side, 9 * channels)


def block_forward(stream, weights, grid_side):
    w_first, w_middle, w_last, gain_rows, bias_rows = weights
    low_in = stream.astype(jnp.bfloat16)
    pre_first = product(low_in, w_first)
    act_first = norm_act(pre_first, gain_rows[0], bias_rows[0]).astype(jnp.bfloat16)
    taps_in = columns(act_first, grid_side)
    pre_middle = product(taps_in, w_middle)
    act_middle = norm_act(pre_middle, gain_rows[1], bias_rows[1]).astype(jnp.bfloat16)
    pre_last = product(act_middle, w_last)
    result = closing(stream, pre_last, gain_rows[2], bias_rows[2])
    return (result, (low_in, pre_first, taps_in, pre_middle, act_middle, pre_last))


def block_backward(grad_out, stream, kept, weights, grid_side):
    low_in, pre_first, taps_in, pre_middle, act_middle, pre_last = kept
    w_first, w_middle, w_last, gain_rows, bias_rows = weights
    unused, pullback = jax.vjp(closing, stream, pre_last, gain_rows[2], bias_rows[2])
    grad_stream, grad_last, gain_last, bias_last = pullback(grad_out)
    grad_last = grad_last.astype(jnp.bfloat16)
    grad_act = times_transposed(grad_last, w_last)
    wgrad_last = outer_sum(act_middle, grad_last)
    unused, pullback = jax.vjp(norm_act, pre_middle, gain_rows[1], bias_rows[1])
    grad_middle, gain_middle, bias_middle = pullback(grad_act)
    grad_middle = grad_middle.astype(jnp.bfloat16)
    tapped = back_columns(grad_middle, grid_side).reshape(-1, 9, C)
    grad_act_first = lax.dot_general(
        tapped,
        w_middle.reshape(9, C, C),
        (((1, 2), (0, 2)), ((), ())),
        preferred_element_type=jnp.float32,
    )
    wgrad_middle = outer_sum(taps_in, grad_middle)
    unused, pullback = jax.vjp(norm_act, pre_first, gain_rows[0], bias_rows[0])
    grad_first, gain_first, bias_first = pullback(grad_act_first)
    grad_first = grad_first.astype(jnp.bfloat16)
    grad_stream = grad_stream + times_transposed(grad_first, w_first)
    wgrad_first = outer_sum(low_in, grad_first)
    gain_grads = jnp.stack([gain_first, gain_middle, gain_last], axis=1)
    bias_grads = jnp.stack([bias_first, bias_middle, bias_last], axis=1)
    return (grad_stream, (wgrad_first, wgrad_middle, wgrad_last, gain_grads, bias_grads))

PLANE = 4


class Movement:
    def __init__(self, mesh):
        self.dp = mesh.shape["dp"]
        self.cores = mesh.shape["fsdp"]
        self.line = self.dp // PLANE

    def flip(self, value, bits):
        return lax.ppermute(value, "dp", [(i, i ^ bits) for i in range(self.dp)])

    def up(self, value, first, last):
        pairs = [(i, i + PLANE) for i in range(self.dp - PLANE) if first <= i // PLANE <= last]
        return lax.ppermute(value, "dp", pairs)

    def down(self, value, first, last):
        pairs = [(i, i - PLANE) for i in range(PLANE, self.dp) if first <= i // PLANE <= last]
        return lax.ppermute(value, "dp", pairs)

    def turn(self, value, step):
        return lax.ppermute(value, "fsdp", [(i, (i + step) % self.cores) for i in range(self.cores)])

    def place(self):
        index = lax.axis_index("dp")
        return index // PLANE, index % PLANE, lax.axis_index("fsdp")

    def gather_line(self, own):
        line = self.line
        height = self.place()[0]
        rising, falling, above, below = own, own, [], []
        for step in range(1, line):
            rising = self.up(rising, step - 1, line - 2)
            falling = self.down(falling, 1, line - step)
            below.append(rising)
            above.append(falling)
        stacked = jnp.stack(below[::-1] + [own] + above)
        return lax.dynamic_slice_in_dim(stacked, line - 1 - height, line)

    def gather_pieces(self, own):
        held = self.gather_line(own)
        half = held.shape[-1] // 2
        first = self.flip(held, 1)
        second = self.flip(held, 2)
        far = (self.flip(first[..., :half], 2), self.flip(second[..., half:], 1))
        pieces = [(0, 0, (held,)), (1, 0, (first,)), (2, 0, (second,)), (3, 0, far)]
        for step in range(1, self.cores):
            pieces += [(chip, step, tuple(self.turn(part, step) for part in parts)) for chip, _, parts in pieces[:4]]
        return pieces

    def gather(self, own_parts):
        gathered = [self.gather_pieces(part) for part in own_parts]
        columns = own_parts[0].shape[-1]
        rows = [part.shape[0] for part in own_parts]
        total = sum(rows)
        operands, plan, start = [], [], 0
        for pieces, count in zip(gathered, rows):
            for chip, step, parts in pieces:
                left = 0
                for part in parts:
                    operands.append(part)
                    plan.append((chip, step, start, count, left, part.shape[-1]))
                    left += part.shape[-1]
            start += count
        cores = self.cores

        def kernel(*refs):
            sources, target, arrived = refs[:-2], refs[-2], refs[-1]
            near = lax.rem(lax.axis_index("dp"), PLANE)
            core = lax.axis_index("fsdp")
            copies = []
            for number, (chip, step, start, count, left, width) in enumerate(plan):
                across = near if chip == 0 else lax.bitwise_xor(near, chip)
                turned = lax.rem(core + (cores - step), cores)
                copies.append(
                    pltpu.make_async_copy(
                        sources[number],
                        target.at[:, across, turned, pl.ds(start, count), pl.ds(left, width)],
                        arrived.at[number],
                    )
                )
            for copy in copies:
                copy.start()
            for copy in copies:
                copy.wait()

        shape = (self.line, PLANE, cores, total, columns)
        whole = pl.pallas_call(
            kernel,
            out_shape=jax.ShapeDtypeStruct(shape, own_parts[0].dtype),
            in_specs=[pl.BlockSpec(memory_space=pl.ANY)] * len(operands),
            out_specs=pl.BlockSpec(memory_space=pl.ANY),
            scratch_shapes=[pltpu.SemaphoreType.DMA((len(operands),))],
            cost_estimate=pl.CostEstimate(
                flops=0,
                bytes_accessed=4 * self.dp * cores * total * columns,
                transcendentals=0,
            ),
        )(*operands)
        return whole

    def scatter(self, terms):
        line, cores = self.line, self.cores
        height, near, core = self.place()
        columns = terms.shape[-1]
        terms = terms.reshape(line, PLANE, cores, -1, columns)
        half = columns // 2

        def of_core(step):
            return lax.dynamic_index_in_dim(terms, (core + step) % cores, 2, keepdims=False)

        summed = of_core(0).astype(jnp.float32)
        for step in range(1, cores):
            summed = summed + self.turn(of_core(step), step).astype(jnp.float32)

        def of_chip(bits):
            return lax.dynamic_index_in_dim(summed, near ^ bits, 1, keepdims=False)

        low = jnp.bfloat16
        far = of_chip(3).astype(low)
        far_first = self.flip(far[..., :half], 2).astype(jnp.float32)
        far_second = self.flip(far[..., half:], 1).astype(jnp.float32)
        first = of_chip(1)
        first = jnp.concatenate([first[..., :half] + far_first, first[..., half:]], -1)
        second = of_chip(2)
        second = jnp.concatenate([second[..., :half], second[..., half:] + far_second], -1)
        first = self.flip(first.astype(low), 1).astype(jnp.float32)
        second = self.flip(second.astype(low), 2).astype(jnp.float32)
        held = of_chip(0) + first + second

        def of_line(distance):
            return lax.dynamic_index_in_dim(held, jnp.clip(height + distance, 0, line - 1), 0, keepdims=False)

        rising = falling = None
        for distance in range(line - 1, 0, -1):
            to_up, to_down = of_line(distance), of_line(-distance)
            if rising is not None:
                to_up, to_down = to_up + rising, to_down + falling
            rising = self.up(to_up.astype(low), 0, line - 1 - distance).astype(jnp.float32)
            falling = self.down(to_down.astype(low), distance, line - 1).astype(jnp.float32)
        return of_line(0) + rising + falling


def local(
    move,
    features,
    grid_live,
    pos_embed,
    w_in,
    w_mid,
    w_out,
    norm_gain,
    norm_bias,
    readout_w,
    readout_b,
    cotangent,
):
    devices = move.dp * move.cores
    low = jnp.bfloat16
    own_rows = w_in.shape[1]
    width = norm_gain.shape[-1]
    wide = readout_b.shape[0]
    cells = pos_embed.shape[0]
    scales = jnp.concatenate([norm_gain.reshape(-1), norm_bias.reshape(-1), readout_b])
    small = jnp.concatenate([pos_embed.T.reshape(-1), scales])
    small_rows = -(-small.shape[0] // (16 * C)) * 16
    small = jnp.pad(small, (0, small_rows * C - small.shape[0])).reshape(small_rows, C)
    thirds = w_mid.shape[1] // 3
    small_all = move.gather([small]).reshape(devices, -1)
    w_in_0 = move.gather([w_in[0]]).reshape(C, C)

    def middle(block):
        if thirds % 16:
            return move.gather([w_mid[block]]).reshape(9 * C, C)
        return move.gather([w_mid[block, i * thirds : (i + 1) * thirds] for i in range(3)]).reshape(9 * C, C)

    w_mid_0 = middle(0)
    w_out_0 = move.gather([w_out[0]]).reshape(C, C)
    w_in_1 = move.gather([w_in[1]]).reshape(C, C)
    w_mid_1 = middle(1)
    w_out_1 = move.gather([w_out[1]]).reshape(C, C)
    readout_all = move.gather([readout_w]).reshape(C, -1)
    pos_all = small_all[:, : cells * width].reshape(C, cells).T
    at = cells * width
    count = 6 * width
    gains = small_all[:, at : at + count].reshape(devices, 2, 3, width)
    gains = jnp.moveaxis(gains, 0, 2).reshape(2, 3, C).astype(jnp.float32)
    biases = small_all[:, at + count : at + 2 * count].reshape(devices, 2, 3, width)
    biases = jnp.moveaxis(biases, 0, 2).reshape(2, 3, C).astype(jnp.float32)
    readout_bias = small_all[:, at + 2 * count : at + 2 * count + wide].reshape(-1).astype(jnp.float32)

    first_block = (w_in_0, w_mid_0, w_out_0, gains[0], biases[0])
    second_block = (w_in_1, w_mid_1, w_out_1, gains[1], biases[1])
    stream_in = features[0].astype(jnp.float32) + pos_all.astype(jnp.float32)
    stream_mid, first_kept = block_forward(stream_in, first_block, G)
    half_side = G // 2
    pooled = jnp.mean(stream_mid.reshape(half_side, 2, half_side, 2, C), axis=(1, 3)).reshape(
        half_side * half_side, C
    )
    stream_out, second_kept = block_forward(pooled, second_block, half_side)
    low_out = stream_out.astype(jnp.bfloat16)
    live_value = grid_live[0].astype(jnp.float32)

    def readout_act(logits):
        return jax.nn.gelu(logits, approximate=False) * live_value

    logits = product(low_out, readout_all) + readout_bias
    output = readout_act(logits).astype(jnp.bfloat16)
    unused, pullback = jax.vjp(readout_act, logits)
    grad_logits = pullback(cotangent[0].astype(jnp.float32))[0].astype(jnp.bfloat16)
    grad_readout_w = outer_sum(low_out, grad_logits).astype(low)
    grad_readout_b = jnp.sum(grad_logits.astype(jnp.float32), axis=0)
    grad_top = times_transposed(grad_logits, readout_all)
    readout_owned = move.scatter(grad_readout_w)
    grad_pooled, second_grads = block_backward(
        grad_top, pooled, second_kept, second_block, half_side
    )
    top_first, top_middle, top_last, top_gain, top_bias = second_grads
    last_owned_1 = move.scatter(top_last.astype(low))
    middle_owned_1 = move.scatter(top_middle.astype(low))
    first_owned_1 = move.scatter(top_first.astype(low))
    grad_mid = jnp.broadcast_to(
        (grad_pooled * 0.25).reshape(half_side, 1, half_side, 1, C), (half_side, 2, half_side, 2, C)
    ).reshape(G * G, C)
    grad_in, first_grads = block_backward(grad_mid, stream_in, first_kept, first_block, G)
    low_first, low_middle, low_last, low_gain, low_bias = first_grads
    last_owned_0 = move.scatter(low_last.astype(low))
    middle_owned_0 = move.scatter(low_middle.astype(low))
    first_owned_0 = move.scatter(low_first.astype(low))
    gain_terms = jnp.stack([low_gain, top_gain]).reshape(2, devices, width, 3)
    bias_terms = jnp.stack([low_bias, top_bias]).reshape(2, devices, width, 3)
    small_terms = jnp.concatenate(
        [
            grad_in.T.reshape(devices, -1),
            gain_terms.transpose(1, 0, 3, 2).reshape(devices, -1),
            bias_terms.transpose(1, 0, 3, 2).reshape(devices, -1),
            grad_readout_b.reshape(devices, -1),
        ],
        axis=1,
    ).astype(low)
    rest = small_rows * C - small_terms.shape[1]
    small_terms = jnp.pad(small_terms, ((0, 0), (0, rest))).reshape(devices * small_rows, C)
    small_owned = move.scatter(small_terms).reshape(-1)
    pos_owned = small_owned[:at].reshape(width, cells).T
    return (
        output[None],
        grad_in[None],
        pos_owned,
        jnp.stack([first_owned_0, first_owned_1]),
        jnp.stack([middle_owned_0, middle_owned_1]),
        jnp.stack([last_owned_0, last_owned_1]),
        small_owned[at : at + count].reshape(2, 3, width),
        small_owned[at + count : at + 2 * count].reshape(2, 3, width),
        readout_owned,
        small_owned[at + 2 * count : at + 2 * count + wide],
    )


def solution(mesh):
    return jax.shard_map(
        functools.partial(local, Movement(mesh)),
        mesh=mesh,
        in_specs=(
            P(("dp", "fsdp"), None, None),
            P(("dp", "fsdp")),
            P(None, ("dp", "fsdp")),
            P(None, ("dp", "fsdp"), None),
            P(None, ("dp", "fsdp"), None),
            P(None, ("dp", "fsdp"), None),
            P(None, None, ("dp", "fsdp")),
            P(None, None, ("dp", "fsdp")),
            P(("dp", "fsdp"), None),
            P(("dp", "fsdp")),
            P(("dp", "fsdp"), None, None),
        ),
        out_specs=(
            P(("dp", "fsdp"), None, None),
            P(("dp", "fsdp"), None, None),
            P(None, ("dp", "fsdp")),
            P(None, ("dp", "fsdp"), None),
            P(None, ("dp", "fsdp"), None),
            P(None, ("dp", "fsdp"), None),
            P(None, None, ("dp", "fsdp")),
            P(None, None, ("dp", "fsdp")),
            P(("dp", "fsdp"), None),
            P(("dp", "fsdp")),
        ),
        check_vma=False,
    )
```

```python
import functools

import jax
import jax.numpy as jnp
from jax import lax
from jax.experimental import pallas as pl
from jax.experimental.pallas import tpu as pltpu
from jax.sharding import PartitionSpec as P

C = 1024
G = 24
PLANE = 4
TILE = 256
ROWS = 48
PAD = 24
MISC = 16
HEAD = 1664
VMEM = 60 * 1024 * 1024


def low(value):
    return value.astype(jnp.bfloat16)


def wide(value):
    return value.astype(jnp.float32)


def dot(left, right):
    return jnp.dot(left, right, preferred_element_type=jnp.float32)


def dot_rows(left, right):
    return lax.dot_general(left, right, (((1,), (1,)), ((), ())), preferred_element_type=jnp.float32)


def dot_sums(left, right):
    return lax.dot_general(left, right, (((0,), (0,)), ((), ())), preferred_element_type=jnp.float32)


def sigmoid(value):
    return 1.0 / (1.0 + jnp.exp(-value))


def centered(value):
    center = value - jnp.mean(value, axis=-1, keepdims=True)
    spread = jnp.mean(center * center, axis=-1, keepdims=True)
    scale = lax.rsqrt(spread + 1e-05)
    return center * scale, scale


def norm_back(grad, normal, scale, gain):
    inner = grad * gain
    first = jnp.mean(inner, axis=-1, keepdims=True)
    second = jnp.mean(inner * normal, axis=-1, keepdims=True)
    return scale * (inner - first - normal * second)


def silu_back(value):
    gate = sigmoid(value)
    return gate * (1.0 + value * (1.0 - gate))


def tiles(extent, size, body):
    def step(i, carry):
        body(pl.ds(pl.multiple_of(i * size, size), size))
        return carry

    lax.fori_loop(0, extent // size, step, 0)


def fold(value):
    return jnp.sum(value.reshape(-1, 8, value.shape[-1]), axis=0)


def columns_of(cells, side, lanes):
    index = lax.broadcasted_iota(jnp.int32, (cells, lanes), 0).astype(jnp.float32)
    return index - side * jnp.floor((index + 0.5) * (1.0 / side))


def beside(value, side, step):
    cells = value.shape[0]
    column = columns_of(cells, side, value.shape[1])
    inside = column < side - 1 if step > 0 else column > 0
    return jnp.where(inside, pltpu.roll(value, (cells - step) % cells, 0), 0.0)


class Blocks:
    def __init__(self, parts, block_rows, columns=slice(None)):
        self.parts = parts
        self.block_rows = block_rows
        self.columns = columns
        self.operands = [array for part in parts for array in part[0]]
        self.copies = sum(array.shape[0] for array in self.operands)

    def bind(self, refs, places, matrix, sems, to_blocks=False, base=0):
        made = []
        number = 0
        for arrays, source, rows, target in self.parts:
            offset = 0
            for array in arrays:
                count = array.shape[0]
                for i in range(count):
                    at = target
                    if count > 1:
                        at = pl.multiple_of(places[offset + i] * self.block_rows + target, 16)
                    inside = matrix.at[pl.ds(at, rows), :]
                    outside = refs[number].at[i, pl.ds(source, rows), self.columns]
                    pair = (inside, outside) if to_blocks else (outside, inside)
                    made.append(pltpu.make_async_copy(*pair, sems.at[base + len(made)]))
                offset += count
                number += 1
        return made


def start(copies):
    for copy in copies:
        copy.start()


def wait(copies):
    for copy in copies:
        copy.wait()


ANY = pl.BlockSpec(memory_space=pl.ANY)
IN = pl.BlockSpec(memory_space=pltpu.VMEM)
SMEM = pl.BlockSpec(memory_space=pltpu.SMEM)


def call(kernel, name, ins, in_specs, outs, out_specs, scratch, flops, moved):
    return pl.pallas_call(
        kernel,
        name=name,
        out_shape=outs,
        in_specs=in_specs,
        out_specs=out_specs,
        scratch_shapes=scratch,
        compiler_params=pltpu.CompilerParams(vmem_limit_bytes=VMEM),
        cost_estimate=pl.CostEstimate(flops=int(flops), bytes_accessed=int(moved), transcendentals=0),
    )(*ins)


def shaped(*shape, dtype=jnp.float32):
    return jax.ShapeDtypeStruct(shape, dtype)


def forward_block(places, number, side, stream, features, misc, w_first, w_middle, w_last):
    cells = side * side
    opening = features is not None
    n_first, n_middle, n_last = len(w_first.operands), len(w_middle.operands), len(w_last.operands)
    given = [features] if opening else [stream, misc]
    given_count = len(given)
    bf16 = jnp.bfloat16

    def kernel(places_ref, *refs):
        refs = list(refs)
        heads = [refs.pop(0) for _ in range(given_count)]
        firsts = [refs.pop(0) for _ in range(n_first)]
        middles = [refs.pop(0) for _ in range(n_middle)]
        lasts = [refs.pop(0) for _ in range(n_last)]
        if opening:
            misc_ref, u_ref = refs.pop(0), refs.pop(0)
        else:
            u_ref, misc_ref = heads
        result_ref, pre1, pre2, pre3, act1 = [refs.pop(0) for _ in range(5)]
        wi, wm, wo, taps, lowered, above, below, work, pairs, sems = refs
        first_copies = w_first.bind(firsts, places_ref, wi, sems)
        middle_copies = w_middle.bind(middles, places_ref, wm, sems, base=len(first_copies))
        last_copies = w_last.bind(lasts, places_ref, wo, sems, base=len(first_copies) + len(middle_copies))
        start(first_copies)
        start(middle_copies)
        start(last_copies)
        wait(first_copies)
        if opening:

            def place(cut):
                turned = jnp.transpose(wide(wi[cut, C:HEAD]))
                u_ref[:, cut] = wide(heads[0][:, cut]) + turned[:cells]
                misc_ref[:, cut] = turned[cells : cells + MISC]

            tiles(C, 128, place)

        def lower(rows):
            lowered[rows, :] = low(u_ref[rows, :])

        tiles(cells, ROWS, lower)

        def first(cut):
            pre1[:, cut] = dot(lowered[...], wi[:, cut])

        tiles(C, TILE, first)

        def norm_act(source, target, norm):
            gain = misc_ref[3 * number + norm : 3 * number + norm + 1, :]
            bias = misc_ref[6 + 3 * number + norm : 7 + 3 * number + norm, :]

            def rows_of(rows):
                normal, _ = centered(source[rows, :])
                hidden = normal * gain + bias
                target[rows, :] = hidden * sigmoid(hidden)

            tiles(cells, ROWS, rows_of)

        norm_act(pre1, work, 0)

        def spread(i, carry):
            cut = pl.ds(pl.multiple_of(i * 128, 128), 128)
            value = work[:, cut]
            act1[:, cut] = low(value)
            taps[:, pl.ds(pl.multiple_of(i * 128, 128), 128)] = low(beside(value, side, -1))
            taps[:, pl.ds(pl.multiple_of(C + i * 128, 128), 128)] = low(value)
            taps[:, pl.ds(pl.multiple_of(2 * C + i * 128, 128), 128)] = low(beside(value, side, 1))
            return carry

        lax.fori_loop(0, C // 128, spread, 0)
        zeros = jnp.zeros((PAD, TILE), jnp.float32)
        for ref in (above, below):
            ref[:PAD, :] = zeros
            ref[PAD + cells :, :] = zeros
        wait(middle_copies)

        def middle(cut):
            above[PAD : PAD + cells, :] = dot(taps[...], wm[0 : 3 * C, cut])
            below[PAD : PAD + cells, :] = dot(taps[...], wm[6 * C : 9 * C, cut])
            same = dot(taps[...], wm[3 * C : 6 * C, cut])
            pre2[:, cut] = same + above[PAD - side : PAD - side + cells, :] + below[PAD + side : PAD + side + cells, :]

        tiles(C, TILE, middle)
        norm_act(pre2, work, 1)

        def lower_second(rows):
            lowered[rows, :] = low(work[rows, :])

        tiles(cells, ROWS, lower_second)
        wait(last_copies)

        def last(cut):
            pre3[:, cut] = dot(lowered[...], wo[:, cut])

        tiles(C, TILE, last)
        gain = misc_ref[3 * number + 2 : 3 * number + 3, :]
        bias = misc_ref[8 + 3 * number : 9 + 3 * number, :]

        def close(rows):
            normal, _ = centered(pre3[rows, :])
            total = u_ref[rows, :] + (normal * gain + bias)
            value = total * sigmoid(total)
            if opening:
                work[rows, :] = value
            else:
                result_ref[rows, :] = low(value)

        tiles(cells, ROWS, close)
        if opening:
            half = side // 2

            def pool(cut):
                value = work[:, cut].reshape(half, 2, side, 128)
                pairs[...] = (value[:, 0] + value[:, 1]).reshape(half * side, 128)
                result_ref[:, cut] = 0.25 * (
                    pairs[pl.ds(0, half * half, 2), :] + pairs[pl.ds(1, half * half, 2), :]
                )

            tiles(C, 128, pool)

    outs, out_specs = [], []
    if opening:
        outs += [shaped(MISC, C), shaped(cells, C), shaped(cells // 4, C)]
    else:
        outs += [shaped(cells, C, dtype=bf16)]
    outs += [shaped(cells, C)] * 3 + [shaped(cells, C, dtype=bf16)]
    copies = w_first.copies + w_middle.copies + w_last.copies
    scratch = [
        pltpu.VMEM((C, HEAD if opening else C), bf16),
        pltpu.VMEM((9 * C, C), bf16),
        pltpu.VMEM((C, C), bf16),
        pltpu.VMEM((cells, 3 * C), bf16),
        pltpu.VMEM((cells, C), bf16),
        pltpu.VMEM((cells + 2 * PAD, TILE), jnp.float32),
        pltpu.VMEM((cells + 2 * PAD, TILE), jnp.float32),
        pltpu.VMEM((cells, C), jnp.float32),
        pltpu.VMEM((cells // 2, 128), jnp.float32),
        pltpu.SemaphoreType.DMA((copies,)),
    ]
    weights = w_first.operands + w_middle.operands + w_last.operands
    return call(
        kernel,
        "forward_block",
        [places] + given + weights,
        [SMEM] + [IN] * given_count + [ANY] * len(weights),
        outs,
        [IN] * len(outs),
        scratch,
        2 * cells * 11 * C * C,
        22 * C * C + 20 * cells * C,
    )


def readout(places, live, lowered, bias, cotangent, weights, out_blocks):
    cells, columns = cotangent.shape
    n_weights, n_outs = len(weights.operands), len(out_blocks.operands)
    bf16 = jnp.bfloat16
    cut_size = 512

    def kernel(places_in, places_out, live_ref, low_ref, bias_ref, cot_ref, *refs):
        refs = list(refs)
        sources = [refs.pop(0) for _ in range(n_weights)]
        output, grad_stream, grad_bias = refs.pop(0), refs.pop(0), refs.pop(0)
        targets = [refs.pop(0) for _ in range(n_outs)]
        matrix, grad, turned, sems = refs
        copies = weights.bind(sources, places_in, matrix, sems)
        start(copies)
        factor = wide(live_ref[0])
        grad_stream[...] = jnp.zeros((cells, C), jnp.float32)
        turned[...] = low(jnp.transpose(wide(low_ref[...])))
        wait(copies)

        def part(cut):
            logits = dot(low_ref[...], matrix[:, cut]) + bias_ref[:, cut]
            share = 0.5 * (1.0 + lax.erf(logits * (0.5**0.5)))
            output[:, cut] = low(logits * share * factor)
            slope = share + logits * (jnp.exp(-0.5 * logits * logits) * (0.5 / jnp.pi) ** 0.5)
            grad_logits = low(wide(cot_ref[:, cut]) * factor * slope)
            grad_bias[:, cut] = jnp.sum(wide(grad_logits), axis=0, keepdims=True)
            grad[:, cut] = low(dot(turned[...], grad_logits))
            grad_stream[...] += dot_rows(grad_logits, matrix[:, cut])

        tiles(columns, cut_size, part)
        out_copies = out_blocks.bind(targets, places_out, grad, sems, to_blocks=True)
        start(out_copies)
        wait(out_copies)

    outs = [shaped(cells, columns, dtype=bf16), shaped(cells, C), shaped(1, columns)]
    outs += [shaped(*array.shape, dtype=bf16) for array in out_blocks.operands]
    scratch = [
        pltpu.VMEM((C, columns), bf16),
        pltpu.VMEM((C, columns), bf16),
        pltpu.VMEM((C, cells), bf16),
        pltpu.SemaphoreType.DMA((max(weights.copies, out_blocks.copies),)),
    ]
    return call(
        kernel,
        "readout",
        [places[0], places[1], live, lowered, bias, cotangent] + weights.operands,
        [SMEM] * 3 + [IN] * 3 + [ANY] * n_weights,
        outs,
        [IN] * 3 + [ANY] * n_outs,
        scratch,
        6 * cells * C * columns,
        4 * C * columns + 4 * cells * columns,
    )


def back_last(places, number, side, grad_out, stream, pre3, pre2, misc, w_last, out_blocks):
    cells = side * side
    n_weights, n_outs = len(w_last.operands), len(out_blocks.operands)
    bf16 = jnp.bfloat16

    def kernel(places_in, places_out, grad_ref, u_ref, pre3_ref, pre2_ref, misc_ref, *refs):
        refs = list(refs)
        sources = [refs.pop(0) for _ in range(n_weights)]
        direct, grad_pre2, sums = refs.pop(0), refs.pop(0), refs.pop(0)
        targets = [refs.pop(0) for _ in range(n_outs)]
        matrix, grad, grad_pre3, act2, work, parts, sems = refs
        copies = w_last.bind(sources, places_in, matrix, sems)
        start(copies)
        parts[...] = jnp.zeros_like(parts)
        gain = misc_ref[3 * number + 2 : 3 * number + 3, :]
        bias = misc_ref[8 + 3 * number : 9 + 3 * number, :]

        def close(rows):
            normal, scale = centered(pre3_ref[rows, :])
            total = u_ref[rows, :] + (normal * gain + bias)
            inner = grad_ref[rows, :] * silu_back(total)
            direct[rows, :] = inner
            parts[0:8, :] += fold(inner * normal)
            parts[8:16, :] += fold(inner)
            grad_pre3[rows, :] = low(norm_back(inner, normal, scale, gain))

        tiles(cells, ROWS, close)
        gain = misc_ref[3 * number + 1 : 3 * number + 2, :]
        bias = misc_ref[7 + 3 * number : 8 + 3 * number, :]

        def again(rows):
            normal, _ = centered(pre2_ref[rows, :])
            hidden = normal * gain + bias
            act2[rows, :] = low(hidden * sigmoid(hidden))

        tiles(cells, ROWS, again)

        def weight_term(cut):
            grad[cut, :] = low(dot_sums(act2[:, cut], grad_pre3[...]))

        tiles(C, TILE, weight_term)
        wait(copies)
        out_copies = out_blocks.bind(targets, places_out, grad, sems, to_blocks=True)
        start(out_copies)

        def last(cut):
            work[:, cut] = dot_rows(grad_pre3[...], matrix[cut, :])

        tiles(C, TILE, last)

        def norm(rows):
            normal, scale = centered(pre2_ref[rows, :])
            hidden = normal * gain + bias
            inner = work[rows, :] * silu_back(hidden)
            parts[16:24, :] += fold(inner * normal)
            parts[24:32, :] += fold(inner)
            grad_pre2[rows, :] = low(norm_back(inner, normal, scale, gain))

        tiles(cells, ROWS, norm)
        sums[...] = jnp.sum(parts[...].reshape(4, 8, C), axis=1)
        wait(out_copies)

    outs = [shaped(cells, C), shaped(cells, C, dtype=bf16), shaped(4, C)]
    outs += [shaped(*array.shape, dtype=bf16) for array in out_blocks.operands]
    scratch = [
        pltpu.VMEM((C, C), bf16),
        pltpu.VMEM((C, C), bf16),
        pltpu.VMEM((cells, C), bf16),
        pltpu.VMEM((cells, C), bf16),
        pltpu.VMEM((cells, C), jnp.float32),
        pltpu.VMEM((32, C), jnp.float32),
        pltpu.SemaphoreType.DMA((max(w_last.copies, out_blocks.copies),)),
    ]
    return call(
        kernel,
        "back_last",
        [places[0], places[1], grad_out, stream, pre3, pre2, misc] + w_last.operands,
        [SMEM] * 2 + [IN] * 5 + [ANY] * n_weights,
        outs,
        [IN] * 3 + [ANY] * n_outs,
        scratch,
        4 * cells * C * C,
        8 * C * C + 24 * cells * C,
    )


def back_middle(places, side, act1, grad_pre2, out_blocks):
    cells = side * side
    n_outs = len(out_blocks.operands)
    bf16 = jnp.bfloat16

    def kernel(places_out, act_ref, grad_ref, *refs):
        refs = list(refs)
        targets = [refs.pop(0) for _ in range(n_outs)]
        grad, taps, shifted, padded, sems = refs
        copies = out_blocks.bind(targets, places_out, grad, sems, to_blocks=True)
        padded[:PAD, :] = jnp.zeros((PAD, 128), jnp.float32)
        padded[PAD + cells :, :] = jnp.zeros((PAD, 128), jnp.float32)

        def spread(i, carry):
            cut = pl.ds(pl.multiple_of(i * 128, 128), 128)
            value = wide(act_ref[:, cut])
            taps[:, cut] = low(beside(value, side, -1))
            taps[:, pl.ds(pl.multiple_of(C + i * 128, 128), 128)] = act_ref[:, cut]
            taps[:, pl.ds(pl.multiple_of(2 * C + i * 128, 128), 128)] = low(beside(value, side, 1))
            padded[PAD : PAD + cells, :] = wide(grad_ref[:, cut])
            shifted[0, :, cut] = low(padded[PAD + side : PAD + side + cells, :])
            shifted[1, :, cut] = grad_ref[:, cut]
            shifted[2, :, cut] = low(padded[PAD - side : PAD - side + cells, :])
            return carry

        lax.fori_loop(0, C // 128, spread, 0)
        for row_tap in range(3):

            def part(i, carry, row_tap=row_tap):
                cut = pl.ds(pl.multiple_of(i * TILE, TILE), TILE)
                target = pl.ds(pl.multiple_of(row_tap * 3 * C + i * TILE, TILE), TILE)
                grad[target, :] = low(dot_sums(taps[:, cut], shifted[row_tap]))
                return carry

            lax.fori_loop(0, 3 * C // TILE, part, 0)
        start(copies)
        wait(copies)

    outs = [shaped(*array.shape, dtype=bf16) for array in out_blocks.operands]
    scratch = [
        pltpu.VMEM((9 * C, C), bf16),
        pltpu.VMEM((cells, 3 * C), bf16),
        pltpu.VMEM((3, cells, C), bf16),
        pltpu.VMEM((cells + 2 * PAD, 128), jnp.float32),
        pltpu.SemaphoreType.DMA((out_blocks.copies,)),
    ]
    return call(
        kernel,
        "back_middle",
        [places[1], act1, grad_pre2],
        [SMEM] + [IN] * 2,
        outs,
        [ANY] * n_outs,
        scratch,
        2 * cells * 9 * C * C,
        18 * C * C + 4 * cells * C,
    )


def back_first(places, number, side, grad_pre2, pre1, stream, direct, misc, rest, w_middle, w_first, out_blocks):
    cells = side * side
    closing = rest is not None
    n_middle, n_first, n_outs = len(w_middle.operands), len(w_first.operands), len(out_blocks.operands)
    bf16 = jnp.bfloat16
    extra = [rest] if closing else []

    def kernel(places_in, places_out, grad_ref, pre1_ref, u_ref, direct_ref, misc_ref, *refs):
        refs = list(refs)
        rest_ref = refs.pop(0) if closing else None
        middles = [refs.pop(0) for _ in range(n_middle)]
        firsts = [refs.pop(0) for _ in range(n_first)]
        grad_u, sums = refs.pop(0), refs.pop(0)
        targets = [refs.pop(0) for _ in range(n_outs)]
        wm, wi, grad, taps, above, below, work, lowered, grad_pre1, parts, sems = refs
        middle_copies = w_middle.bind(middles, places_in, wm, sems)
        first_copies = w_first.bind(firsts, places_in, wi, sems, base=len(middle_copies))
        start(middle_copies)
        start(first_copies)
        parts[...] = jnp.zeros_like(parts)
        zeros = jnp.zeros((PAD, TILE), jnp.float32)
        for ref in (above, below):
            ref[:PAD, :] = zeros
            ref[PAD + cells :, :] = zeros

        def spread(i, carry):
            cut = pl.ds(pl.multiple_of(i * 128, 128), 128)
            value = wide(grad_ref[:, cut])
            taps[:, cut] = low(beside(value, side, 1))
            taps[:, pl.ds(pl.multiple_of(C + i * 128, 128), 128)] = grad_ref[:, cut]
            taps[:, pl.ds(pl.multiple_of(2 * C + i * 128, 128), 128)] = low(beside(value, side, -1))
            return carry

        lax.fori_loop(0, C // 128, spread, 0)

        def lower(rows):
            lowered[rows, :] = low(u_ref[rows, :])

        tiles(cells, ROWS, lower)
        wait(middle_copies)

        def middle(i, carry):
            def row(tap):
                total = None
                for column in range(3):
                    source = pl.ds(pl.multiple_of((3 * tap + column) * C + i * TILE, TILE), TILE)
                    term = dot_rows(taps[:, column * C : (column + 1) * C], wm[source, :])
                    total = term if total is None else total + term
                return total

            above[PAD : PAD + cells, :] = row(0)
            below[PAD : PAD + cells, :] = row(2)
            cut = pl.ds(pl.multiple_of(i * TILE, TILE), TILE)
            work[:, cut] = (
                row(1) + above[PAD + side : PAD + side + cells, :] + below[PAD - side : PAD - side + cells, :]
            )
            return carry

        lax.fori_loop(0, C // TILE, middle, 0)
        gain = misc_ref[3 * number : 3 * number + 1, :]
        bias = misc_ref[6 + 3 * number : 7 + 3 * number, :]

        def norm(rows):
            normal, scale = centered(pre1_ref[rows, :])
            hidden = normal * gain + bias
            inner = work[rows, :] * silu_back(hidden)
            parts[0:8, :] += fold(inner * normal)
            parts[8:16, :] += fold(inner)
            grad_pre1[rows, :] = low(norm_back(inner, normal, scale, gain))

        tiles(cells, ROWS, norm)
        sums[...] = jnp.sum(parts[...].reshape(2, 8, C), axis=1)

        def weight_term(cut):
            grad[cut, :C] = low(dot_sums(lowered[:, cut], grad_pre1[...]))

        tiles(C, TILE, weight_term)
        wait(first_copies)

        def first(cut):
            grad_u[:, cut] = direct_ref[:, cut] + dot_rows(grad_pre1[...], wi[cut, :])

        tiles(C, TILE, first)
        if closing:

            def turn(cut):
                stacked = jnp.concatenate(
                    [
                        grad_u[:, cut],
                        sums[0:1, cut],
                        rest_ref[1:6, cut],
                        sums[1:2, cut],
                        rest_ref[7:MISC, cut],
                        jnp.zeros((HEAD - C - cells - MISC, 128), jnp.float32),
                    ]
                )
                grad[cut, C:HEAD] = low(jnp.transpose(stacked))

            tiles(C, 128, turn)
        out_copies = out_blocks.bind(targets, places_out, grad, sems, to_blocks=True)
        start(out_copies)
        wait(out_copies)

    outs = [shaped(cells, C), shaped(2, C)]
    outs += [shaped(*array.shape, dtype=bf16) for array in out_blocks.operands]
    scratch = [
        pltpu.VMEM((9 * C, C), bf16),
        pltpu.VMEM((C, C), bf16),
        pltpu.VMEM((C, HEAD if closing else C), bf16),
        pltpu.VMEM((cells, 3 * C), bf16),
        pltpu.VMEM((cells + 2 * PAD, TILE), jnp.float32),
        pltpu.VMEM((cells + 2 * PAD, TILE), jnp.float32),
        pltpu.VMEM((cells, C), jnp.float32),
        pltpu.VMEM((cells, C), bf16),
        pltpu.VMEM((cells, C), bf16),
        pltpu.VMEM((16, C), jnp.float32),
        pltpu.SemaphoreType.DMA((max(w_middle.copies + w_first.copies, out_blocks.copies),)),
    ]
    weights = w_middle.operands + w_first.operands
    return call(
        kernel,
        "back_first",
        [places[0], places[1], grad_pre2, pre1, stream, direct, misc] + extra + weights,
        [SMEM] * 2 + [IN] * (5 + len(extra)) + [ANY] * len(weights),
        outs,
        [IN] * 2 + [ANY] * n_outs,
        scratch,
        2 * cells * 11 * C * C,
        24 * C * C + 24 * cells * C,
    )


def after(value, *earlier):
    return lax.optimization_barrier((value, earlier))[0]


class Movement:
    def __init__(self, mesh):
        self.dp = mesh.shape["dp"]
        self.cores = mesh.shape["fsdp"]
        self.line = self.dp // PLANE
        self.devices = self.dp * self.cores
        self.ring = [0] + list(range(1, self.line, 2)) + list(range(2, self.line, 2))[::-1]
        self.paired = self.cores == 2 and self.line == 4

    def flip(self, value, bits):
        return lax.ppermute(value, "dp", [(i, i ^ bits) for i in range(self.dp)])

    def along(self, value):
        pairs = []
        for position, level in enumerate(self.ring):
            following = self.ring[(position + 1) % self.line]
            pairs += [(level * PLANE + near, following * PLANE + near) for near in range(PLANE)]
        return lax.ppermute(value, "dp", pairs)

    def swap(self, value):
        return lax.ppermute(value, "fsdp", [(0, 1), (1, 0)])

    def places(self, direction):
        if not self.paired:
            return jnp.zeros((1,), jnp.int32)
        index = lax.axis_index("dp")
        ring = jnp.array(self.ring, jnp.int32)
        position = jnp.argmax(ring == index // PLANE).astype(jnp.int32)
        level = ring[(position + direction * jnp.arange(self.line, dtype=jnp.int32)) % self.line]
        near = (index % PLANE) ^ jnp.arange(PLANE, dtype=jnp.int32)
        core = (lax.axis_index("fsdp") + jnp.arange(2, dtype=jnp.int32)) % 2
        chip = level[None, None, :] * PLANE + near[None, :, None]
        return (chip * 2 + core[:, None, None]).reshape(-1)

    def gather(self, pieces):
        if not self.paired:
            return [[lax.all_gather(own, ("dp", "fsdp"), axis=0, tiled=False).reshape(1, -1, own.shape[1])] for own in pieces]
        line_done, plane_done, gathered = (), (), []
        for own in pieces:
            own = after(own, *line_done) if line_done else own
            one = self.along(own)
            two = self.along(one)
            three = self.along(two)
            line_done = (two,)
            held = jnp.stack([own, one, two, three])
            held = after(held, *plane_done) if plane_done else held
            first = self.flip(held, 1)
            second = self.flip(held, 2)
            plane_done = (first, second)
            far = (self.flip(first[:2], 2), self.flip(second[2:], 1))
            here = jnp.concatenate([held, first, second, *far])
            gathered.append([here, self.swap(here)])
        return gathered


class Sum:
    def __init__(self, move, arrays):
        self.move = move
        self.arrays = arrays
        if not move.paired:
            self.owned = lax.psum_scatter(wide(arrays[0][0]), ("dp", "fsdp"), scatter_dimension=0, tiled=True)

    def turn(self):
        move = self.move
        shape = (PLANE, move.line) + self.arrays[0].shape[1:]
        self.here = self.arrays[0].reshape(shape)
        self.there = move.swap(self.arrays[1]).reshape(shape)
        return self.there

    def pair(self, chip, steps):
        return wide(self.here[chip, steps]) + wide(self.there[chip, steps])

    def diagonal(self):
        half = self.move.line // 2
        self.far = (
            self.move.flip(low(self.pair(3, slice(None, half))), 2),
            self.move.flip(low(self.pair(3, slice(half, None))), 1),
        )
        return self.far

    def plane(self):
        half = self.move.line // 2
        near, rest = slice(None, half), slice(half, None)
        first = jnp.concatenate([self.pair(1, near) + wide(self.far[0]), self.pair(1, rest)])
        second = jnp.concatenate([self.pair(2, near), self.pair(2, rest) + wide(self.far[1])])
        self.sides = (self.move.flip(low(first), 1), self.move.flip(low(second), 2))
        return self.sides

    def finish(self):
        held = self.pair(0, slice(None)) + wide(self.sides[0]) + wide(self.sides[1])
        three = self.move.along(low(held[3]))
        two = self.move.along(low(held[2] + wide(three)))
        one = self.move.along(low(held[1] + wide(two)))
        self.owned = held[0] + wide(one)
        return self.owned


def local(
    move,
    features,
    grid_live,
    pos_embed,
    w_in,
    w_mid,
    w_out,
    norm_gain,
    norm_bias,
    readout_w,
    readout_b,
    cotangent,
):
    rows, middle_rows, width = w_in.shape[1], w_mid.shape[1], readout_w.shape[1]
    cells = pos_embed.shape[0]
    pooled_cells = cells // 4
    misc_at = C + cells
    half_side = G // 2
    spare = jnp.zeros((rows, HEAD - misc_at - MISC), jnp.bfloat16)
    head = jnp.concatenate(
        [w_in[0], pos_embed.T, norm_gain.reshape(6, rows).T, norm_bias.reshape(6, rows).T, readout_b.reshape(rows, 4), spare],
        axis=1,
    )
    outer = jnp.concatenate([w_out[0], w_in[1], w_out[1]])
    parts_0, parts_1 = (3, 2) if move.paired else (1, 1)
    cut_0, cut_1 = middle_rows // parts_0, middle_rows // parts_1
    pieces = [head]
    pieces += [w_mid[0, i * cut_0 : (i + 1) * cut_0] for i in range(parts_0)]
    pieces += [outer]
    pieces += [w_mid[1, i * cut_1 : (i + 1) * cut_1] for i in range(parts_1)]
    pieces += [readout_w]
    if move.paired:
        gathered = move.gather(pieces)
        heads, middles_0, outers = gathered[0], gathered[1 : 1 + parts_0], gathered[1 + parts_0]
        middles_1, readouts = gathered[2 + parts_0 : -1], gathered[-1]
        outers = [[(outers, i * rows, rows, 0)] for i in range(3)]
    else:
        heads, middle_0, last_0, first_1, last_1, middle_1, readouts = move.gather(
            [head, w_mid[0], w_out[0], w_in[1], w_out[1], w_mid[1], readout_w]
        )
        middles_0, middles_1 = [middle_0], [middle_1]
        outers = [[(whole, 0, C, 0)] for whole in (last_0, first_1, last_1)]

    def middle_blocks(groups, cut):
        count = cut if move.paired else 9 * C
        return Blocks([(arrays, 0, count, i * cut) for i, arrays in enumerate(groups)], middle_rows)

    count = rows if move.paired else C
    head_blocks = Blocks([(heads, 0, count, 0)], rows)
    first_0 = Blocks([(heads, 0, count, 0)], rows, pl.ds(0, C))
    mid_0, mid_1 = middle_blocks(middles_0, cut_0), middle_blocks(middles_1, cut_1)
    last_0, first_1, last_1 = [Blocks(parts, rows) for parts in outers]
    readout_blocks = Blocks([(readouts, 0, count, 0)], rows)

    def out_blocks(block_rows, columns, parts=1):
        if not move.paired:
            return Blocks([([shaped(1, move.devices * block_rows, columns)], 0, move.devices * block_rows, 0)], block_rows)
        cut = block_rows // parts
        return Blocks([([shaped(move.dp, cut, columns)] * 2, 0, cut, i * cut) for i in range(parts)], block_rows)

    places = (move.places(-1), move.places(1))
    misc, stream_in, pooled, pre1_0, pre2_0, pre3_0, act1_0 = forward_block(
        places[0], 0, G, None, features[0], None, head_blocks, mid_0, last_0
    )
    low_out, pre1_1, pre2_1, pre3_1, act1_1 = forward_block(
        places[0], 1, half_side, pooled, None, misc, first_1, mid_1, last_1
    )
    readout_bias = misc[12:].T.reshape(1, width)
    output, grad_top, grad_readout_b, *readout_terms = readout(
        places, grid_live, low_out, readout_bias, cotangent[0], readout_blocks, out_blocks(rows, width)
    )
    sum_readout = Sum(move, readout_terms)
    direct_1, grad_pre2_1, sums_1, *last_terms_1 = back_last(
        places, 1, half_side, grad_top, pooled, pre3_1, pre2_1, misc, last_1, out_blocks(rows, C)
    )
    hold = after if move.paired else lambda value, *earlier: value
    if move.paired:
        grad_pre2_1 = after(grad_pre2_1, sum_readout.turn())
    middle_terms_1 = back_middle(places, half_side, act1_1, grad_pre2_1, out_blocks(middle_rows, C, parts_1))
    step = 2 if move.paired else 1
    sums_middle_1 = [Sum(move, middle_terms_1[i * step : (i + 1) * step]) for i in range(parts_1)]
    if move.paired:
        grad_pre2_1 = after(grad_pre2_1, middle_terms_1, *sum_readout.diagonal())
    grad_pooled, sums_first_1, *first_terms_1 = back_first(
        places, 1, half_side, grad_pre2_1, pre1_1, pooled, direct_1, misc, None, mid_1, first_1, out_blocks(rows, C)
    )
    if move.paired:
        waited = [*sum_readout.plane(), sums_middle_1[0].turn(), sums_middle_1[1].turn(), *sums_middle_1[0].diagonal()]
        grad_pooled = after(grad_pooled, *waited)
    grad_mid = jnp.broadcast_to(
        (grad_pooled * 0.25).reshape(half_side, 1, half_side, 1, C), (half_side, 2, half_side, 2, C)
    ).reshape(cells, C)
    direct_0, grad_pre2_0, sums_0, *last_terms_0 = back_last(
        places, 0, G, grad_mid, stream_in, pre3_0, pre2_0, misc, last_0, out_blocks(rows, C)
    )
    if move.paired:
        outer_terms = [jnp.concatenate(pair, axis=1) for pair in zip(last_terms_0, first_terms_1, last_terms_1)]
        sum_outer = Sum(move, outer_terms)
        waited = [sum_readout.finish(), *sums_middle_1[0].plane(), *sums_middle_1[1].diagonal()]
        grad_pre2_0 = after(grad_pre2_0, *waited)
    middle_terms_0 = back_middle(places, G, act1_0, grad_pre2_0, out_blocks(middle_rows, C, parts_0))
    sums_middle_0 = [Sum(move, middle_terms_0[i * step : (i + 1) * step]) for i in range(parts_0)]
    if move.paired:
        waited = [sums_middle_1[0].finish(), *sums_middle_1[1].plane(), sum_outer.turn(), *sum_outer.diagonal()]
        grad_pre2_0 = after(grad_pre2_0, middle_terms_0, *waited)
    blank = jnp.zeros((1, C), jnp.float32)
    rest = jnp.concatenate(
        [
            blank, sums_0[2:3], sums_0[0:1], sums_first_1[0:1], sums_1[2:3], sums_1[0:1],
            blank, sums_0[3:4], sums_0[1:2], sums_first_1[1:2], sums_1[3:4], sums_1[1:2],
            grad_readout_b.reshape(C, 4).T,
        ]
    )
    grad_in, _, *head_terms = back_first(
        places, 0, G, grad_pre2_0, pre1_0, stream_in, direct_0, misc, rest, mid_0, first_0, out_blocks(rows, HEAD)
    )
    sum_head = Sum(move, head_terms)
    if move.paired:
        sums_middle_1[1].finish()
        sum_outer.plane()
        for total in sums_middle_0:
            total.turn()
        sums_middle_0[0].diagonal()
        sum_outer.finish()
        sums_middle_0[0].plane()
        sums_middle_0[1].diagonal()
        sums_middle_0[0].finish()
        sums_middle_0[1].plane()
        sums_middle_0[2].diagonal()
        sums_middle_0[1].finish()
        sums_middle_0[2].plane()
        sum_head.turn()
        sum_head.diagonal()
        sums_middle_0[2].finish()
        sum_head.plane()
        sum_head.finish()
        outer_owned = sum_outer.owned.reshape(3, rows, C)
    else:
        outer_owned = [Sum(move, terms).owned for terms in (last_terms_0, first_terms_1, last_terms_1)]
    head_owned = sum_head.owned
    scales = head_owned[:, misc_at : misc_at + MISC]
    return (
        output[None],
        grad_in[None],
        head_owned[:, C:misc_at].T,
        jnp.stack([head_owned[:, :C], outer_owned[1]]),
        jnp.stack(
            [
                jnp.concatenate([total.owned for total in sums_middle_0]),
                jnp.concatenate([total.owned for total in sums_middle_1]),
            ]
        ),
        jnp.stack([outer_owned[0], outer_owned[2]]),
        scales[:, 0:6].T.reshape(2, 3, rows),
        scales[:, 6:12].T.reshape(2, 3, rows),
        sum_readout.owned,
        scales[:, 12:].reshape(-1),
    )


def solution(mesh):
    return jax.shard_map(
        functools.partial(local, Movement(mesh)),
        mesh=mesh,
        in_specs=(
            P(("dp", "fsdp"), None, None),
            P(("dp", "fsdp")),
            P(None, ("dp", "fsdp")),
            P(None, ("dp", "fsdp"), None),
            P(None, ("dp", "fsdp"), None),
            P(None, ("dp", "fsdp"), None),
            P(None, None, ("dp", "fsdp")),
            P(None, None, ("dp", "fsdp")),
            P(("dp", "fsdp"), None),
            P(("dp", "fsdp")),
            P(("dp", "fsdp"), None, None),
        ),
        out_specs=(
            P(("dp", "fsdp"), None, None),
            P(("dp", "fsdp"), None, None),
            P(None, ("dp", "fsdp")),
            P(None, ("dp", "fsdp"), None),
            P(None, ("dp", "fsdp"), None),
            P(None, ("dp", "fsdp"), None),
            P(None, None, ("dp", "fsdp")),
            P(None, None, ("dp", "fsdp")),
            P(("dp", "fsdp"), None),
            P(("dp", "fsdp")),
        ),
        check_vma=False,
    )
```

```python
import functools

import jax
import jax.numpy as jnp
import numpy as np
from jax import lax
from jax.experimental import pallas as pl
from jax.experimental.pallas import tpu as pltpu
from jax.sharding import PartitionSpec as P

C = 1024
G = 24
PLANE = 4
TILE = 256
ROWS = 144
PAD = 24
MISC = 16
HEAD = 1664
SIDE = 384
STEPS, LEVELS, OUT_STEPS, OUT_LEVELS, OUT_LINE, CORE, TABLE = 0, 32, 64, 80, 96, 112, 113
COST = 30
COSTS = {"forward_block": 50}
VMEM = 60 * 1024 * 1024


def low(value):
    return value.astype(jnp.bfloat16)


def wide(value):
    return value.astype(jnp.float32)


def dot(left, right):
    return jnp.dot(left, right, preferred_element_type=jnp.float32)


def dot_rows(left, right):
    return lax.dot_general(left, right, (((1,), (1,)), ((), ())), preferred_element_type=jnp.float32)


def dot_sums(left, right):
    return lax.dot_general(left, right, (((0,), (0,)), ((), ())), preferred_element_type=jnp.float32)


def sigmoid(value):
    return 1.0 / (1.0 + jnp.exp(-value))


def centered(value):
    center = value - jnp.mean(value, axis=-1, keepdims=True)
    spread = jnp.mean(center * center, axis=-1, keepdims=True)
    scale = lax.rsqrt(spread + 1e-05)
    return center * scale, scale


def norm_back(grad, normal, scale, gain):
    inner = grad * gain
    first = jnp.mean(inner, axis=-1, keepdims=True)
    second = jnp.mean(inner * normal, axis=-1, keepdims=True)
    return scale * (inner - first - normal * second)


def silu_back(value):
    gate = sigmoid(value)
    return gate * (1.0 + value * (1.0 - gate))


def tiles(extent, size, body):
    def step(i, carry):
        body(pl.ds(pl.multiple_of(i * size, size), size))
        return carry

    lax.fori_loop(0, extent // size, step, 0)


def fold(value):
    return jnp.sum(value.reshape(-1, 8, value.shape[-1]), axis=0)


def columns_of(cells, side, lanes):
    index = lax.broadcasted_iota(jnp.int32, (cells, lanes), 0).astype(jnp.float32)
    return index - side * jnp.floor((index + 0.5) * (1.0 / side))


def beside(value, side, step):
    cells = value.shape[0]
    column = columns_of(cells, side, value.shape[1])
    inside = column < side - 1 if step > 0 else column > 0
    return jnp.where(inside, pltpu.roll(value, (cells - step) % cells, 0), 0.0)


class Blocks:
    def __init__(self, block_rows):
        self.block_rows = block_rows
        self.operands = []
        self.moves = []

    def operand(self, array):
        for number, known in enumerate(self.operands):
            if known is array:
                return number
        self.operands.append(array)
        return len(self.operands) - 1

    def add(self, array, block, row, column, place, to_row, to_column, rows, columns):
        self.moves.append((self.operand(array), block, row, column, place, to_row, to_column, rows, columns))

    @property
    def copies(self):
        return len(self.moves)

    def bind(self, refs, places, matrix, sems, to_blocks=False, base=0):
        made = []
        for number, block, row, column, place, to_row, to_column, rows, columns in self.moves:
            first = to_row
            if place is not None:
                first = pl.multiple_of(places[place] * self.block_rows + to_row, 16)
            inside = matrix.at[pl.ds(first, rows), pl.ds(to_column, columns)]
            outside = refs[number] if block is None else refs[number].at[block]
            outside = outside.at[pl.ds(row, rows), pl.ds(column, columns)]
            pair = (inside, outside) if to_blocks else (outside, inside)
            made.append(pltpu.make_async_copy(*pair, sems.at[base + len(made)]))
        return made


def start(copies):
    for copy in copies:
        copy.start()


def wait(copies):
    for copy in copies:
        copy.wait()


ANY = pl.BlockSpec(memory_space=pl.ANY)
IN = pl.BlockSpec(memory_space=pltpu.VMEM)
SMEM = pl.BlockSpec(memory_space=pltpu.SMEM)


def call(kernel, name, ins, in_specs, outs, out_specs, scratch, flops, moved):
    short = COSTS.get(name, COST)
    return pl.pallas_call(
        kernel,
        name=name,
        out_shape=outs,
        in_specs=in_specs,
        out_specs=out_specs,
        scratch_shapes=scratch,
        compiler_params=pltpu.CompilerParams(vmem_limit_bytes=VMEM),
        cost_estimate=pl.CostEstimate(flops=int(flops) // short, bytes_accessed=int(moved) // short, transcendentals=0),
    )(*ins)


class Traffic:
    def __init__(self, sems):
        self.sems = sems
        self.used = 0
        self.sent = []

    def begin(self, source, target):
        copy = pltpu.make_async_copy(source, target, self.sems.at[self.used])
        self.used += 1
        copy.start()
        return copy

    def send(self, source, target):
        self.sent.append(self.begin(source, target))

    def load(self, blocks, refs, places, matrix):
        copies = blocks.bind(refs, places, matrix, self.sems, base=self.used)
        self.used += len(copies)
        start(copies)
        return copies

    def store(self, blocks, refs, places, matrix):
        copies = blocks.bind(refs, places, matrix, self.sems, to_blocks=True, base=self.used)
        self.used += len(copies)
        start(copies)
        self.sent += copies

    def finish(self):
        wait(self.sent)


def shaped(*shape, dtype=jnp.float32):
    return jax.ShapeDtypeStruct(shape, dtype)


def forward_block(table, number, side, stream, features, misc, w_first, w_middle, w_last):
    cells = side * side
    opening = features is not None
    n_first, n_middle, n_last = len(w_first.operands), len(w_middle.operands), len(w_last.operands)
    given = [features] if opening else [stream, misc]
    given_count = len(given)
    bf16 = jnp.bfloat16
    n_lefts = 3 if opening else 4

    def kernel(table_ref, *refs):
        refs = list(refs)
        heads = [refs.pop(0) for _ in range(given_count)]
        firsts = [refs.pop(0) for _ in range(n_first)]
        middles = [refs.pop(0) for _ in range(n_middle)]
        lasts = [refs.pop(0) for _ in range(n_last)]
        if opening:
            misc_ref, pooled_ref, u_out = refs.pop(0), refs.pop(0), refs.pop(0)
            u_ref = refs.pop(0 - 1)
        else:
            u_ref, misc_ref = heads
        lefts_out, pre1_out, pre2_out, pre3_out = [refs.pop(0) for _ in range(4)]
        wi, wm, wo, taps, lefts, above, below, work, pairs, pre1, pre2, pre3, sems = refs
        traffic = Traffic(sems)
        first_copies = traffic.load(w_first, firsts, table_ref, wi)
        middle_copies = traffic.load(w_middle, middles, table_ref, wm)
        last_copies = traffic.load(w_last, lasts, table_ref, wo)
        wait(first_copies)
        if opening:

            def place(cut):
                turned = jnp.transpose(wide(wi[cut, C:HEAD]))
                u_ref[:, cut] = wide(heads[0][:, cut]) + turned[:cells]
                misc_ref[:, cut] = turned[cells : cells + MISC]

            tiles(C, 128, place)
            traffic.send(u_ref, u_out)

        def lower(rows):
            lefts[0, rows, :] = low(u_ref[rows, :])

        tiles(cells, ROWS, lower)

        def first(cut):
            pre1[:, cut] = dot(lefts[0], wi[:, cut])

        tiles(C, TILE, first)
        traffic.send(pre1, pre1_out)

        def norm_act(source, norm, store):
            gain = misc_ref[3 * number + norm : 3 * number + norm + 1, :]
            bias = misc_ref[6 + 3 * number + norm : 7 + 3 * number + norm, :]

            def rows_of(rows):
                normal, _ = centered(source[rows, :])
                hidden = normal * gain + bias
                store(rows, hidden * sigmoid(hidden))

            tiles(cells, ROWS, rows_of)

        def keep_first(rows, value):
            work[rows, :] = value
            lefts[1, rows, :] = low(value)

        norm_act(pre1, 0, keep_first)

        def spread(i, carry):
            cut = pl.ds(pl.multiple_of(i * 128, 128), 128)
            value = work[:, cut]
            taps[:, pl.ds(pl.multiple_of(i * 128, 128), 128)] = low(beside(value, side, -1))
            taps[:, pl.ds(pl.multiple_of(C + i * 128, 128), 128)] = low(value)
            taps[:, pl.ds(pl.multiple_of(2 * C + i * 128, 128), 128)] = low(beside(value, side, 1))
            return carry

        lax.fori_loop(0, C // 128, spread, 0)
        zeros = jnp.zeros((PAD, TILE), jnp.float32)
        for ref in (above, below):
            ref[:PAD, :] = zeros
            ref[PAD + cells :, :] = zeros
        wait(middle_copies)

        def middle(cut):
            above[PAD : PAD + cells, :] = dot(taps[...], wm[0 : 3 * C, cut])
            below[PAD : PAD + cells, :] = dot(taps[...], wm[6 * C : 9 * C, cut])
            same = dot(taps[...], wm[3 * C : 6 * C, cut])
            pre2[:, cut] = same + above[PAD - side : PAD - side + cells, :] + below[PAD + side : PAD + side + cells, :]

        tiles(C, TILE, middle)
        traffic.send(pre2, pre2_out)

        def keep_second(rows, value):
            lefts[2, rows, :] = low(value)

        norm_act(pre2, 1, keep_second)
        if opening:
            traffic.send(lefts, lefts_out)
        wait(last_copies)

        def last(cut):
            pre3[:, cut] = dot(lefts[2], wo[:, cut])

        tiles(C, TILE, last)
        traffic.send(pre3, pre3_out)
        gain = misc_ref[3 * number + 2 : 3 * number + 3, :]
        bias = misc_ref[8 + 3 * number : 9 + 3 * number, :]

        def close(rows):
            normal, _ = centered(pre3[rows, :])
            total = u_ref[rows, :] + (normal * gain + bias)
            value = total * sigmoid(total)
            if opening:
                work[rows, :] = value
            else:
                lefts[3, rows, :] = low(value)

        tiles(cells, ROWS, close)
        if opening:
            half = side // 2

            def pool(cut):
                value = work[:, cut].reshape(half, 2, side, 128)
                pairs[...] = (value[:, 0] + value[:, 1]).reshape(half * side, 128)
                pooled_ref[:, cut] = 0.25 * (
                    pairs[pl.ds(0, half * half, 2), :] + pairs[pl.ds(1, half * half, 2), :]
                )

            tiles(C, 128, pool)
        else:
            traffic.send(lefts, lefts_out)
        traffic.finish()

    outs, out_specs = [], []
    if opening:
        outs += [shaped(MISC, C), shaped(cells // 4, C), shaped(cells, C)]
        out_specs += [IN, IN, ANY]
    outs += [shaped(n_lefts, cells, C, dtype=bf16)] + [shaped(cells, C)] * 3
    out_specs += [ANY] * 4
    copies = w_first.copies + w_middle.copies + w_last.copies + 5
    scratch = [
        pltpu.VMEM((C, HEAD if opening else C), bf16),
        pltpu.VMEM((9 * C, C), bf16),
        pltpu.VMEM((C, C), bf16),
        pltpu.VMEM((cells, 3 * C), bf16),
        pltpu.VMEM((n_lefts, cells, C), bf16),
        pltpu.VMEM((cells + 2 * PAD, TILE), jnp.float32),
        pltpu.VMEM((cells + 2 * PAD, TILE), jnp.float32),
        pltpu.VMEM((cells, C), jnp.float32),
        pltpu.VMEM((cells // 2, 128), jnp.float32),
        pltpu.VMEM((cells, C), jnp.float32),
        pltpu.VMEM((cells, C), jnp.float32),
        pltpu.VMEM((cells, C), jnp.float32),
        pltpu.SemaphoreType.DMA((copies,)),
    ]
    if opening:
        scratch.append(pltpu.VMEM((cells, C), jnp.float32))
    weights = w_first.operands + w_middle.operands + w_last.operands
    return call(
        kernel,
        "forward_block",
        [table] + given + weights,
        [SMEM] + [IN] * given_count + [ANY] * len(weights),
        outs,
        out_specs,
        scratch,
        2 * cells * 11 * C * C,
        22 * C * C + 20 * cells * C,
    )


def readout(table, live, lefts, bias, cotangent, weights):
    cells, columns = cotangent.shape
    n_weights = len(weights.operands)
    bf16 = jnp.bfloat16
    cut_size = 512
    half = columns // 2

    def kernel(table_ref, live_ref, lefts_ref, bias_ref, cot_ref, *refs):
        refs = list(refs)
        sources = [refs.pop(0) for _ in range(n_weights)]
        output, grad_stream, grad_bias, own, other, matrix, low_ref, sems = refs
        traffic = Traffic(sems)
        given = traffic.begin(lefts_ref.at[3], low_ref)
        copies = traffic.load(weights, sources, table_ref, matrix)
        factor = wide(live_ref[0])
        core = table_ref[CORE]
        grad_stream[...] = jnp.zeros((cells, C), jnp.float32)
        given.wait()
        wait(copies)
        for part in range(2):

            def step(cut, part=part):
                here = pl.ds(pl.multiple_of(part * half + cut.start, cut_size), cut_size)
                logits = dot(low_ref[...], matrix[:, here]) + bias_ref[:, here]
                share = 0.5 * (1.0 + lax.erf(logits * (0.5**0.5)))
                output[:, here] = low(logits * share * factor)
                slope = share + logits * (jnp.exp(-0.5 * logits * logits) * (0.5 / jnp.pi) ** 0.5)
                grad_logits = low(wide(cot_ref[:, here]) * factor * slope)
                grad_bias[:, here] = jnp.sum(wide(grad_logits), axis=0, keepdims=True)

                @pl.when(core == part)
                def _():
                    own[:, cut] = grad_logits

                @pl.when(core != part)
                def _():
                    other[:, cut] = grad_logits

                grad_stream[...] += dot_rows(grad_logits, matrix[:, here])

            tiles(half, cut_size, step)

    outs = [shaped(cells, columns, dtype=bf16), shaped(cells, C), shaped(1, columns)]
    outs += [shaped(cells, half, dtype=bf16)] * 2
    scratch = [
        pltpu.VMEM((C, columns), bf16),
        pltpu.VMEM((cells, C), bf16),
        pltpu.SemaphoreType.DMA((weights.copies + 1,)),
    ]
    return call(
        kernel,
        "readout",
        [table, live, lefts, bias, cotangent] + weights.operands,
        [SMEM] * 2 + [ANY] + [IN] * 2 + [ANY] * n_weights,
        outs,
        [IN] * 5,
        scratch,
        4 * cells * C * columns,
        2 * C * columns + 4 * cells * columns,
    )


def back_last(table, number, side, grad_out, stream, pre3, pre2, misc, w_last):
    cells = side * side
    pooled = grad_out.shape[0] != cells
    n_weights = len(w_last.operands)
    bf16 = jnp.bfloat16
    half = C // 2

    def kernel(table_ref, grad_ref, u_in, pre3_in, pre2_in, misc_ref, *refs):
        refs = list(refs)
        sources = [refs.pop(0) for _ in range(n_weights)]
        direct_out, grads, other, sums, matrix, direct, u_ref, pre3_ref, pre2_ref, work, parts, pairs, sems = refs
        traffic = Traffic(sems)
        opened = [traffic.begin(u_in, u_ref), traffic.begin(pre3_in, pre3_ref)]
        later = traffic.begin(pre2_in, pre2_ref)
        copies = traffic.load(w_last, sources, table_ref, matrix)
        parts[...] = jnp.zeros_like(parts)
        gain = misc_ref[3 * number + 2 : 3 * number + 3, :]
        bias = misc_ref[8 + 3 * number : 9 + 3 * number, :]
        if pooled:

            def spread(cut):
                value = 0.25 * grad_ref[:, cut]
                pairs[pl.ds(0, cells // 4, 2), :] = value
                pairs[pl.ds(1, cells // 4, 2), :] = value
                twice = pairs[...].reshape(side // 2, 1, side, 128)
                work[:, cut] = jnp.broadcast_to(twice, (side // 2, 2, side, 128)).reshape(cells, 128)

            tiles(C, 128, spread)
        grad_from = work if pooled else grad_ref
        wait(opened)

        def close(rows):
            normal, scale = centered(pre3_ref[rows, :])
            total = u_ref[rows, :] + (normal * gain + bias)
            inner = grad_from[rows, :] * silu_back(total)
            direct[rows, :] = inner
            parts[0:8, :] += fold(inner * normal)
            parts[8:16, :] += fold(inner)
            grads[0, rows, :] = low(norm_back(inner, normal, scale, gain))

        tiles(cells, ROWS, close)
        traffic.send(direct, direct_out)
        gain = misc_ref[3 * number + 1 : 3 * number + 2, :]
        bias = misc_ref[7 + 3 * number : 8 + 3 * number, :]
        wait(copies)

        def last(cut):
            work[:, cut] = dot_rows(grads[0], matrix[cut, :])

        tiles(C, TILE, last)
        later.wait()

        def norm(rows):
            normal, scale = centered(pre2_ref[rows, :])
            hidden = normal * gain + bias
            inner = work[rows, :] * silu_back(hidden)
            parts[16:24, :] += fold(inner * normal)
            parts[24:32, :] += fold(inner)
            grads[1, rows, :] = low(norm_back(inner, normal, scale, gain))

        tiles(cells, ROWS, norm)
        sums[...] = jnp.sum(parts[...].reshape(4, 8, C), axis=1)
        there = pl.ds(pl.multiple_of((1 - table_ref[CORE]) * half, half), half)
        for i in range(2):
            other[i] = grads[i, :, there]
        traffic.finish()

    outs = [shaped(cells, C), shaped(2, cells, C, dtype=bf16), shaped(2, cells, half, dtype=bf16), shaped(4, C)]
    f32 = jnp.float32
    scratch = [pltpu.VMEM((C, C), bf16)] + [pltpu.VMEM((cells, C), f32)] * 5
    scratch += [pltpu.VMEM((32, C), f32), pltpu.VMEM((cells // 2, 128), f32), pltpu.SemaphoreType.DMA((w_last.copies + 4,))]
    return call(
        kernel,
        "back_last",
        [table, grad_out, stream, pre3, pre2, misc] + w_last.operands,
        [SMEM, IN, ANY, ANY, ANY, IN] + [ANY] * n_weights,
        outs,
        [ANY, IN, IN, IN],
        scratch,
        2 * cells * C * C,
        2 * C * C + 24 * cells * C,
    )


def middle_terms(table, side, lefts, lefts_other, grads, grads_other, out_blocks):
    cells = side * side
    n_outs = len(out_blocks.operands)
    bf16 = jnp.bfloat16
    pair = lefts_other is not None
    both = 2 * cells if pair else cells
    half = C // 2 if pair else C
    given = [lefts, grads] + ([lefts_other, grads_other] if pair else [])

    def kernel(table_ref, *refs):
        refs = list(refs)
        sources = [refs.pop(0) for _ in given]
        targets = [refs.pop(0) for _ in range(n_outs)]
        act, right, grad, taps, shifted, padded, sems = refs
        traffic = Traffic(sems)
        copies = [traffic.begin(sources[0].at[1], act.at[pl.ds(0, cells), :])]
        if pair:
            mine = pl.ds(pl.multiple_of(table_ref[CORE] * half, half), half)
            copies += [
                traffic.begin(sources[1].at[1, :, mine], right.at[pl.ds(0, cells), :]),
                traffic.begin(sources[2].at[1], act.at[pl.ds(cells, cells), :]),
                traffic.begin(sources[3].at[1], right.at[pl.ds(cells, cells), :]),
            ]
        else:
            copies += [traffic.begin(sources[1].at[1], right.at[pl.ds(0, cells), :])]
        padded[:PAD, :] = jnp.zeros((PAD, 128), jnp.float32)
        padded[PAD + cells :, :] = jnp.zeros((PAD, 128), jnp.float32)
        wait(copies)
        for first in range(0, both, cells):
            rows = slice(first, first + cells)

            def spread(i, carry, rows=rows):
                cut = pl.ds(pl.multiple_of(i * 128, 128), 128)
                value = wide(act[rows, cut])
                taps[rows, cut] = low(beside(value, side, -1))
                taps[rows, pl.ds(pl.multiple_of(C + i * 128, 128), 128)] = act[rows, cut]
                taps[rows, pl.ds(pl.multiple_of(2 * C + i * 128, 128), 128)] = low(beside(value, side, 1))
                return carry

            def shift(i, carry, rows=rows):
                cut = pl.ds(pl.multiple_of(i * 128, 128), 128)
                padded[PAD : PAD + cells, :] = wide(right[rows, cut])
                shifted[0, rows, cut] = low(padded[PAD + side : PAD + side + cells, :])
                shifted[1, rows, cut] = right[rows, cut]
                shifted[2, rows, cut] = low(padded[PAD - side : PAD - side + cells, :])
                return carry

            lax.fori_loop(0, C // 128, spread, 0)
            lax.fori_loop(0, half // 128, shift, 0)
        size = 512
        for row_tap in range(3):

            def part(i, carry, row_tap=row_tap):
                cut = pl.ds(pl.multiple_of(i * size, size), size)
                target = pl.ds(pl.multiple_of(row_tap * 3 * C + i * size, size), size)
                grad[target, :] = low(dot_sums(taps[:, cut], shifted[row_tap]))
                return carry

            lax.fori_loop(0, 3 * C // size, part, 0)
        traffic.store(out_blocks, targets, table_ref, grad)
        traffic.finish()

    outs = [shaped(*array.shape, dtype=bf16) for array in out_blocks.operands]
    scratch = [
        pltpu.VMEM((both, C), bf16),
        pltpu.VMEM((both, half), bf16),
        pltpu.VMEM((9 * C, half), bf16),
        pltpu.VMEM((both, 3 * C), bf16),
        pltpu.VMEM((3, both, half), bf16),
        pltpu.VMEM((cells + 2 * PAD, 128), jnp.float32),
        pltpu.SemaphoreType.DMA((out_blocks.copies + 4,)),
    ]
    return call(
        kernel,
        "middle_terms",
        [table] + given,
        [SMEM] + [ANY] * len(given),
        outs,
        [ANY] * n_outs,
        scratch,
        2 * cells * 9 * C * C,
        18 * C * half + 8 * cells * C,
    )


def plain_terms(table, products, sides, out_blocks):
    bf16 = jnp.bfloat16
    pair = products[0][2] is not None
    given = []
    for left, _, left_other, right, _, right_other, _ in products:
        given += [left, right] + ([left_other, right_other] if pair else [])
    n_given = len(given)
    n_outs = len(out_blocks.operands)
    columns = out_blocks.operands[0].shape[-1]
    width = columns
    rows_of = [product[0].shape[-2] for product in products]

    def kernel(table_ref, *refs):
        refs = list(refs)
        sources = [refs.pop(0) for _ in range(n_given)]
        beside_refs = [refs.pop(0) for _ in range(len(sides) * (2 if pair else 1))]
        targets = [refs.pop(0) for _ in range(n_outs)]
        grad, sems = refs.pop(0), refs.pop(0)
        traffic = Traffic(sems)
        waits = []
        for (_, left_at, _, _, right_at, _, other_at), cells in zip(products, rows_of):
            left, right = refs.pop(0), refs.pop(0)
            left_in, right_in = sources.pop(0), sources.pop(0)
            copies = [traffic.begin(left_in.at[left_at], left.at[pl.ds(0, cells), :])]
            if right_at is not None:
                right_in = right_in.at[right_at]
                if pair:
                    right_in = right_in.at[:, pl.ds(pl.multiple_of(table_ref[CORE] * width, width), width)]
            copies.append(traffic.begin(right_in, right.at[pl.ds(0, cells), :]))
            if pair:
                left_in, right_in = sources.pop(0), sources.pop(0)
                copies.append(traffic.begin(left_in.at[left_at], left.at[pl.ds(cells, cells), :]))
                if other_at is not None:
                    right_in = right_in.at[other_at]
                copies.append(traffic.begin(right_in, right.at[pl.ds(cells, cells), :]))
            waits.append((copies, left, right))
        at, below = 0, len(products) * C
        for side in sides:
            extent = side[0].shape[-1]
            total = beside_refs.pop(0)[...]
            if pair:
                total = low(wide(total) + wide(beside_refs.pop(0)[...]))
            grad[below:, at : at + extent] = total
            at += extent
        if sides:
            grad[below:, at:] = jnp.zeros((C, columns - at), bf16)
        for number, (copies, left, right) in enumerate(waits):
            wait(copies)

            def part(cut, number=number, left=left, right=right):
                target = pl.ds(pl.multiple_of(number * C + cut.start, TILE), TILE)
                grad[target, :] = low(dot_sums(left[:, cut], right[...]))

            tiles(C, TILE, part)
        traffic.store(out_blocks, targets, table_ref, grad)
        traffic.finish()

    factor = 2 if pair else 1
    outs = [shaped(*array.shape, dtype=bf16) for array in out_blocks.operands]
    scratch = [
        pltpu.VMEM(((len(products) + (1 if sides else 0)) * C, columns), bf16),
        pltpu.SemaphoreType.DMA((out_blocks.copies + 4 * len(products),)),
    ]
    for cells in rows_of:
        scratch += [pltpu.VMEM((factor * cells, C), bf16), pltpu.VMEM((factor * cells, width), bf16)]
    besides = [array for side in sides for array in side if array is not None]
    return call(
        kernel,
        "plain_terms",
        [table] + given + besides,
        [SMEM] + [ANY] * n_given + [IN] * len(besides),
        outs,
        [ANY] * n_outs,
        scratch,
        sum(2 * factor * cells * C * width for cells in rows_of),
        2 * len(products) * C * columns + sum(4 * factor * cells * C for cells in rows_of),
    )


def back_first(table, number, side, grads, pre1, direct, misc, rest, w_middle, w_first):
    cells = side * side
    closing = rest is not None
    n_middle, n_first = len(w_middle.operands), len(w_first.operands)
    bf16 = jnp.bfloat16
    extra = [rest] if closing else []
    half = C // 2
    side_half = SIDE

    def kernel(table_ref, grads_in, pre1_in, direct_in, misc_ref, *refs):
        refs = list(refs)
        rest_ref = refs.pop(0) if closing else None
        middles = [refs.pop(0) for _ in range(n_middle)]
        firsts = [refs.pop(0) for _ in range(n_first)]
        grad_u, sums, grad_pre1, other = [refs.pop(0) for _ in range(4)]
        turned = [refs.pop(0), refs.pop(0)] if closing else None
        wm, wi, grad_ref, pre1_ref, direct_ref, taps, above, below, work, parts, sems = refs
        traffic = Traffic(sems)
        given = traffic.begin(grads_in.at[1], grad_ref)
        middle_copies = traffic.load(w_middle, middles, table_ref, wm)
        pre1_copy = traffic.begin(pre1_in, pre1_ref)
        first_copies = traffic.load(w_first, firsts, table_ref, wi)
        direct_copy = traffic.begin(direct_in, direct_ref)
        parts[...] = jnp.zeros_like(parts)
        zeros = jnp.zeros((PAD, TILE), jnp.float32)
        for ref in (above, below):
            ref[:PAD, :] = zeros
            ref[PAD + cells :, :] = zeros
        given.wait()

        def spread(i, carry):
            cut = pl.ds(pl.multiple_of(i * 128, 128), 128)
            value = wide(grad_ref[:, cut])
            taps[:, cut] = low(beside(value, side, 1))
            taps[:, pl.ds(pl.multiple_of(C + i * 128, 128), 128)] = grad_ref[:, cut]
            taps[:, pl.ds(pl.multiple_of(2 * C + i * 128, 128), 128)] = low(beside(value, side, -1))
            return carry

        lax.fori_loop(0, C // 128, spread, 0)
        wait(middle_copies)

        def middle(i, carry):
            def row(tap):
                total = None
                for column in range(3):
                    source = pl.ds(pl.multiple_of((3 * tap + column) * C + i * TILE, TILE), TILE)
                    term = dot_rows(taps[:, column * C : (column + 1) * C], wm[source, :])
                    total = term if total is None else total + term
                return total

            above[PAD : PAD + cells, :] = row(0)
            below[PAD : PAD + cells, :] = row(2)
            cut = pl.ds(pl.multiple_of(i * TILE, TILE), TILE)
            work[:, cut] = (
                row(1) + above[PAD + side : PAD + side + cells, :] + below[PAD - side : PAD - side + cells, :]
            )
            return carry

        lax.fori_loop(0, C // TILE, middle, 0)
        gain = misc_ref[3 * number : 3 * number + 1, :]
        bias = misc_ref[6 + 3 * number : 7 + 3 * number, :]
        pre1_copy.wait()

        def norm(rows):
            normal, scale = centered(pre1_ref[rows, :])
            hidden = normal * gain + bias
            inner = work[rows, :] * silu_back(hidden)
            parts[0:8, :] += fold(inner * normal)
            parts[8:16, :] += fold(inner)
            grad_pre1[0, rows, :] = low(norm_back(inner, normal, scale, gain))

        tiles(cells, ROWS, norm)
        sums[...] = jnp.sum(parts[...].reshape(2, 8, C), axis=1)
        core = table_ref[CORE]
        other[...] = grad_pre1[0, :, pl.ds(pl.multiple_of((1 - core) * half, half), half)]
        wait(first_copies)
        direct_copy.wait()

        def first(cut):
            grad_u[:, cut] = direct_ref[:, cut] + dot_rows(grad_pre1[0], wi[cut, :])

        tiles(C, TILE, first)
        if closing:

            def turn(cut):
                stacked = jnp.concatenate(
                    [
                        grad_u[:, cut],
                        sums[0:1, cut],
                        rest_ref[1:6, cut],
                        sums[1:2, cut],
                        rest_ref[7:MISC, cut],
                        jnp.zeros((2 * side_half - cells - MISC, 128), jnp.float32),
                    ]
                )
                parts_of = low(jnp.transpose(stacked))
                for part in range(2):
                    piece = parts_of[:, part * side_half : (part + 1) * side_half]

                    @pl.when(core == part)
                    def _(piece=piece):
                        turned[0][cut, :] = piece

                    @pl.when(core != part)
                    def _(piece=piece):
                        turned[1][cut, :] = piece

            tiles(C, 128, turn)

    outs = [shaped(cells, C), shaped(2, C), shaped(1, cells, C, dtype=bf16), shaped(cells, half, dtype=bf16)]
    if closing:
        outs += [shaped(C, side_half, dtype=bf16)] * 2
    f32 = jnp.float32
    scratch = [
        pltpu.VMEM((9 * C, C), bf16),
        pltpu.VMEM((C, C), bf16),
        pltpu.VMEM((cells, C), bf16),
        pltpu.VMEM((cells, C), f32),
        pltpu.VMEM((cells, C), f32),
        pltpu.VMEM((cells, 3 * C), bf16),
        pltpu.VMEM((cells + 2 * PAD, TILE), f32),
        pltpu.VMEM((cells + 2 * PAD, TILE), f32),
        pltpu.VMEM((cells, C), f32),
        pltpu.VMEM((16, C), f32),
        pltpu.SemaphoreType.DMA((w_middle.copies + w_first.copies + 3,)),
    ]
    weights = w_middle.operands + w_first.operands
    return call(
        kernel,
        "back_first",
        [table, grads, pre1, direct, misc] + extra + weights,
        [SMEM] + [ANY] * 3 + [IN] * (1 + len(extra)) + [ANY] * len(weights),
        outs,
        [IN] * len(outs),
        scratch,
        2 * cells * 10 * C * C,
        20 * C * C + 24 * cells * C,
    )


def after(value, *earlier):
    return lax.optimization_barrier((value, earlier))[0]


class Movement:
    def __init__(self, mesh):
        self.dp = mesh.shape["dp"]
        self.cores = mesh.shape["fsdp"]
        self.line = self.dp // PLANE
        self.devices = self.dp * self.cores
        self.ring = [0] + list(range(1, self.line, 2)) + list(range(2, self.line, 2))[::-1]
        self.paired = self.cores == 2 and self.line == 4

    def flip(self, value, bits):
        return lax.ppermute(value, "dp", [(i, i ^ bits) for i in range(self.dp)])

    def along(self, value):
        pairs = []
        for position, level in enumerate(self.ring):
            following = self.ring[(position + 1) % self.line]
            pairs += [(level * PLANE + near, following * PLANE + near) for near in range(PLANE)]
        return lax.ppermute(value, "dp", pairs)

    def swap(self, value):
        return lax.ppermute(value, "fsdp", [(0, 1), (1, 0)])

    def lines(self):
        return [[level * PLANE + near for level in range(self.line)] for near in range(PLANE)]

    def table(self):
        if not self.paired:
            return jnp.zeros((TABLE,), jnp.int32)
        steps, chips = range(self.line), range(PLANE)
        halves = [(1, 0), (1, 1), (3, 0), (3, 1), (2, 2), (2, 3), (3, 2), (3, 3), (1, 2), (1, 3), (2, 0), (2, 1)]
        halves += [(0, step) for step in steps]
        rows = []
        for device in range(self.devices):
            chip, core = divmod(device, 2)
            level, near = divmod(chip, PLANE)
            position = self.ring.index(level)

            def chip_at(far, level, near=near):
                return level * PLANE + (near ^ far)

            def step_at(step, position=position):
                return self.ring[(position + step) % self.line]

            row = [chip_at(far, step_at(-step)) * 2 + (core + k) % 2 for k in range(2) for far in chips for step in steps]
            row += [chip_at(far, step) * 2 + (core + k) % 2 for k in range(2) for far in chips for step in steps]
            row += [chip_at(far, step_at(step)) for far, step in halves]
            row += [chip_at(far, step) for far, step in halves]
            row += [chip_at(far, step_at(step)) for step in reversed(steps) for far in chips]
            rows.append(row + [core])
        index = lax.axis_index("dp") * self.cores + lax.axis_index("fsdp")
        return lax.dynamic_index_in_dim(jnp.asarray(np.array(rows, np.int32)), index, 0, keepdims=False)


class Piece:
    def __init__(self, move, own, name):
        self.move = move
        self.own = own
        self.name = name
        self.rows = own.shape[0]
        self.at = STEPS
        self.found = []

    def keep(self, array, far, steps, first=0, other=None):
        for i, step in enumerate(steps):
            for core, held in enumerate((array, other)):
                self.found.append((held, first + i * self.rows, self.at + 16 * core + 4 * far + step))

    def line(self, second, third):
        with jax.named_scope(self.name + "_line"):
            one = self.move.along(self.own)
            two = self.move.along(after(one, *second) if second else one)
            three = self.move.along(after(two, *third))
        self.passed = (one, two, three)
        self.held = jnp.concatenate([self.own, one, two, three])

    def levels(self, *earlier):
        with jax.named_scope(self.name + "_levels"):
            own = after(self.own, *earlier) if earlier else self.own
            self.held = lax.all_gather(own, "dp", axis_index_groups=self.move.lines(), axis=0, tiled=True)
        self.at = LEVELS

    def settle_line(self, *earlier):
        with jax.named_scope("swap"):
            other = self.move.swap(after(self.held, *earlier) if earlier else self.held)
        self.keep(self.held, 0, range(4), other=other)

    def plane_first(self):
        half = self.rows // 2
        with jax.named_scope(self.name + "_plane"):
            first, second = self.sides = self.move.flip(self.own, 1), self.move.flip(self.own, 2)
            self.fars = (self.move.flip(first[:half], 2), self.move.flip(second[half:], 1))
            self.passed = (jnp.concatenate([self.own, first, second, *self.fars]),)

    def pass_on(self, *earlier):
        with jax.named_scope(self.name + "_line"):
            self.passed += (self.move.along(after(self.passed[-1], *earlier)),)

    def end_line(self, *earlier):
        for step, array in enumerate(after(self.passed, *earlier)):
            other = self.move.swap(array)
            for far in range(PLANE):
                self.keep(array, far, [step], first=far * self.rows, other=other)


def cross(move, pieces, fars, *earlier):
    over_first = [piece.held for piece in pieces] + [piece.second[2 * piece.rows : 4 * piece.rows] for piece in fars]
    over_second = [piece.held for piece in pieces] + [piece.first[: 2 * piece.rows] for piece in fars]
    over_first, over_second = [jnp.concatenate(parts) if len(parts) > 1 else parts[0] for parts in (over_first, over_second)]
    if earlier:
        over_first, over_second = after((over_first, over_second), *earlier)
    with jax.named_scope("_".join(piece.name for piece in pieces + fars) + "_plane"):
        first, second = move.flip(over_first, 1), move.flip(over_second, 2)
    row = 0
    for piece in pieces:
        piece.sides = (first, second, row)
        piece.first = first[row : row + 4 * piece.rows]
        piece.second = second[row : row + 4 * piece.rows]
        row += 4 * piece.rows
    for piece in fars:
        piece.far_sides = (first, second, row)
        piece.far_first = first
        row += 2 * piece.rows
    return first, second


def settle(move, pieces, fars, *earlier):
    first, second = (pieces[0].sides if pieces else fars[0].far_sides)[:2]
    if earlier:
        first, second = after((first, second), *earlier)
    with jax.named_scope("swap"):
        first_other, second_other = move.swap(first), move.swap(second)
    for piece in pieces:
        row = piece.sides[2]
        piece.first = first[row : row + 4 * piece.rows]
        piece.second = second[row : row + 4 * piece.rows]
        piece.keep(first, 1, range(4), first=row, other=first_other)
        piece.keep(second, 2, range(4), first=row, other=second_other)
    for piece in fars:
        row = piece.far_sides[2]
        piece.keep(first, 3, (2, 3), first=row, other=first_other)
        piece.keep(second, 3, (0, 1), first=row, other=second_other)


class Sum:
    def __init__(self, move, arrays, name, levels=False):
        self.move = move
        self.arrays = arrays
        self.name = name
        self.levels = levels

    def across(self, *earlier):
        first, second = after(tuple(self.arrays[:2]), *earlier) if earlier else self.arrays[:2]
        with jax.named_scope(self.name + "_across"):
            self.first = self.move.flip(first, 1)
            self.second = self.move.flip(second, 2)
        return self.first, self.second

    def prepare(self, *earlier):
        self.first, self.second = after((self.first, self.second), *earlier)
        with jax.named_scope(self.name + "_onward"):
            self.rests = (
                low(wide(self.arrays[2]) + wide(self.second[2:])),
                low(wide(self.arrays[3]) + wide(self.first[2:])),
            )
        return self.rests

    def onward(self):
        with jax.named_scope(self.name + "_onward"):
            self.rests = (self.move.flip(self.rests[0], 1), self.move.flip(self.rests[1], 2))
        return self.rests

    def gather(self, *earlier):
        rests = after(self.rests, *earlier) if earlier else self.rests
        with jax.named_scope(self.name + "_held"):
            held = self.arrays[4]
            self.near = wide(held[:2]) + wide(self.first[:2]) + wide(rests[1])
            self.far = wide(held[2:]) + wide(self.second[:2]) + wide(rests[0])
            if self.levels:
                held = jnp.concatenate([low(self.near), low(self.far)])
                self.held = held.reshape(-1, held.shape[-1])
                return self.held

    def finish(self, *earlier):
        with jax.named_scope(self.name + "_line"):
            if self.levels:
                lines = self.move.lines()
                owned = lax.psum_scatter(self.held, "dp", axis_index_groups=lines, scatter_dimension=0, tiled=True)
                self.owned = wide(owned)
            else:
                three = self.move.along(low(self.far[1]))
                if earlier:
                    three = after(three, *earlier)
                two = self.move.along(low(self.far[0] + wide(three)))
                one = self.move.along(low(self.near[1] + wide(two)))
                self.owned = self.near[0] + wide(one)


class LineSum:
    def __init__(self, move, arrays, name):
        self.move = move
        self.arrays = arrays
        self.name = name
        self.next = arrays[0]

    def line(self, step):
        with jax.named_scope(f"{self.name}_line{step}"):
            self.sent = self.move.along(self.next)

    def prepare(self, step, *earlier):
        with jax.named_scope(f"{self.name}_line{step}"):
            sent = after(self.sent, *earlier) if earlier else self.sent
            self.next = low(wide(self.arrays[step]) + wide(sent))
        return self.next

    def across(self):
        with jax.named_scope(self.name + "_across"):
            held = wide(self.arrays[3]) + wide(self.sent)
            half = held.shape[1] // 2
            self.near, self.rest = held[:, :half], held[:, half:]
            self.operands = (low(self.near[1::2]), low(self.rest[2:]))
            self.first = self.move.flip(self.operands[0], 1)
            self.second = self.move.flip(self.operands[1], 2)

    def finish(self):
        with jax.named_scope(self.name + "_onward"):
            first_rest = self.move.flip(low(self.rest[1] + wide(self.second[1])), 1)
            second_rest = self.move.flip(low(self.near[2] + wide(self.first[1])), 2)
            near = self.near[0] + wide(self.first[0]) + wide(second_rest)
            rest = self.rest[0] + wide(self.second[0]) + wide(first_rest)
            self.owned = jnp.concatenate([near, rest])


def unite(move, owned, matrices):
    blocks = owned.reshape(matrices, 2, -1, owned.shape[-1])
    core = lax.axis_index("fsdp")
    mine = lax.dynamic_index_in_dim(blocks, core, 1, keepdims=False)
    other = move.swap(lax.dynamic_index_in_dim(blocks, 1 - core, 1, keepdims=False))
    return jnp.where(core == 0, jnp.stack([mine, other], 2), jnp.stack([other, mine], 2))


def local(
    move,
    features,
    grid_live,
    pos_embed,
    w_in,
    w_mid,
    w_out,
    norm_gain,
    norm_bias,
    readout_w,
    readout_b,
    cotangent,
):
    rows, middle_rows, width = w_in.shape[1], w_mid.shape[1], readout_w.shape[1]
    cells = pos_embed.shape[0]
    half_side = G // 2
    paired = move.paired
    scales = [norm_gain.reshape(6, rows).T, norm_bias.reshape(6, rows).T, readout_b.reshape(rows, 4)]
    beside = jnp.concatenate([pos_embed.T, *scales, jnp.zeros((rows, C - cells - MISC), jnp.bfloat16)], axis=1)
    if paired:
        cut = middle_rows // 2
        stacks = [
            [w_in[0], beside, w_out[0]],
            [w_mid[0, :cut]],
            [w_mid[0, cut:], w_in[1], w_out[1]],
            [w_mid[1]],
            [readout_w[:, i * C : (i + 1) * C] for i in range(width // C)],
        ]
        one, two, three, four, top = [
            Piece(move, jnp.concatenate(stack) if len(stack) > 1 else stack[0], name)
            for stack, name in zip(stacks, ("one", "two", "three", "four", "top"))
        ]
        top.plane_first()
        one.line((), top.sides)
        two.line(one.passed[1:2], one.passed[2:])
        three.line(two.passed[1:2], two.passed[2:])
        four.levels(three.passed[1])
        cross(move, [one], [], *top.fars)
        cross(move, [two], [one], one.first)
        one.settle_line(one.first)
        settle(move, [one], [], one.first)
        cross(move, [three], [two], two.first)
        two.settle_line(two.first)
        settle(move, [two], [one], two.first)
        top.pass_on(two.first)
        cross(move, [], [three], three.first)
        three.settle_line(three.first)
        settle(move, [three], [two], three.first)
        cross(move, [four], [], three.far_first)
        top.pass_on(three.far_first)
        settle(move, [], [three], three.far_first)
        lies = {
            "first_0": [(one, 0, rows, 0, 0, C)],
            "head_0": [(one, 0, rows, 0, 0, C), (one, rows, rows, 0, C, HEAD - C)],
            "middle_0": [(two, 0, cut, 0, 0, C), (three, 0, cut, cut, 0, C)],
            "last_0": [(one, 2 * rows, rows, 0, 0, C)],
            "first_1": [(three, cut, rows, 0, 0, C)],
            "last_1": [(three, cut + rows, rows, 0, 0, C)],
            "middle_1": [(four, 0, middle_rows, 0, 0, C)],
            "readout": [(top, i * rows, rows, 0, i * C, C) for i in range(width // C)],
        }
    else:

        def whole(own):
            return lax.all_gather(own, ("dp", "fsdp"), axis=0, tiled=True)

        first_all = whole(w_in[0])
        lies = {
            "first_0": [(first_all, 0)],
            "head_0": [(first_all, 0), (whole(beside[:, : HEAD - C]), C)],
            "middle_0": [(whole(w_mid[0]), 0)],
            "last_0": [(whole(w_out[0]), 0)],
            "first_1": [(whole(w_in[1]), 0)],
            "last_1": [(whole(w_out[1]), 0)],
            "middle_1": [(whole(w_mid[1]), 0)],
            "readout": [(whole(readout_w), 0)],
        }

    def matrix(name):
        blocks = Blocks(middle_rows if name.startswith("middle") else rows)
        if not paired:
            for array, column in lies[name]:
                blocks.add(array, None, 0, 0, None, 0, column, *array.shape)
            return blocks
        for piece, row, extent, to_row, to_column, columns in lies[name]:
            for array, first, place in piece.found:
                blocks.add(array, None, first + row, 0, place, to_row, to_column, extent, columns)
        return blocks

    def sums_of(block_rows, columns, matrices=1, parts=1, levels=False, last_line=False):
        if not paired:
            extent = matrices * move.devices * block_rows
            blocks = Blocks(block_rows)
            blocks.add(shaped(1, extent, columns), 0, 0, 0, None, 0, 0, extent, columns)
            return blocks
        chip_rows = 2 * block_rows
        cut = chip_rows // parts
        blocks = Blocks(chip_rows)
        for part in range(parts):
            line_first = last_line and part == parts - 1
            place = OUT_LINE if line_first else OUT_LEVELS if levels else OUT_STEPS
            for count in (4, 4, 4, 4) if line_first else (4, 4, 2, 2, 4):
                array = shaped(count, matrices * cut, columns)
                for block in range(count):
                    for i in range(matrices):
                        blocks.add(array, block, i * cut, 0, place, i * C + part * cut, 0, cut, columns)
                    place += 1
        return blocks

    def swap(value):
        return move.swap(value) if paired else None

    def tie(value, *earlier):
        return after(value, *earlier) if paired else value

    def scattered(terms, matrices=1):
        total = wide(terms[0][0]).reshape(matrices, -1, terms[0].shape[-1])
        return lax.psum_scatter(total, ("dp", "fsdp"), scatter_dimension=1, tiled=True)

    half = 2 if paired else 1
    table = move.table()
    mid_0, last_0 = matrix("middle_0"), matrix("last_0")
    misc, pooled, stream_in, lefts_0, pre1_0, pre2_0, pre3_0 = forward_block(
        table, 0, G, None, features[0], None, matrix("head_0"), mid_0, last_0
    )
    lefts_other_0 = swap(lefts_0)
    if paired:
        settle(move, [four], [], pooled)
        cross(move, [], [four])
        top.pass_on(pooled)
        four.settle_line(pooled)
        settle(move, [], [four])
    first_1, mid_1, last_1 = matrix("first_1"), matrix("middle_1"), matrix("last_1")
    lefts_1, pre1_1, pre2_1, pre3_1 = forward_block(table, 1, half_side, pooled, None, misc, first_1, mid_1, last_1)
    lefts_other_1 = swap(lefts_1)
    if paired:
        top.end_line(lefts_1)
    readout_bias = misc[12:].T.reshape(1, width)
    output, grad_top, grad_readout_b, grad_logits, grad_logits_other = readout(
        table, grid_live, lefts_1, readout_bias, cotangent[0], matrix("readout")
    )
    if paired:
        grad_logits_other = swap(grad_logits_other)
    else:
        grad_logits, grad_logits_other = jnp.concatenate([grad_logits, grad_logits_other], axis=1), None
    direct_1, grads_1, grads_other_1, sums_1 = back_last(
        table, 1, half_side, grad_top, pooled, pre3_1, pre2_1, misc, last_1
    )
    grads_other_1 = swap(grads_other_1)
    readout_terms = plain_terms(
        table,
        [(lefts_1, 3, lefts_other_1, tie(grad_logits, sums_1), None, grad_logits_other, None)],
        [],
        sums_of(rows, width // half, levels=True),
    )
    middle_terms_1 = middle_terms(
        table,
        half_side,
        tie(lefts_1, *readout_terms),
        lefts_other_1,
        grads_1,
        grads_other_1,
        sums_of(middle_rows, C // half, parts=2 if paired else 1, levels=True),
    )
    if paired:
        sum_readout = Sum(move, readout_terms, "readout", levels=True)
        sums_middle_1 = [Sum(move, middle_terms_1[5 * i : 5 * i + 5], f"middle_1_{i}", levels=True) for i in range(2)]
        sum_readout.across()
        sums_middle_1[0].across()
        grads_1 = tie(grads_1, *middle_terms_1)
    grad_pooled, sums_first_1, grad_first_1, grad_first_other_1 = back_first(
        table, 1, half_side, grads_1, pre1_1, direct_1, misc, None, mid_1, first_1
    )
    grad_first_other_1 = swap(grad_first_other_1)
    if paired:
        grad_pooled = tie(grad_pooled, *sum_readout.prepare(grad_pooled))
        sum_readout.onward()
    direct_0, grads_0, grads_other_0, sums_0 = back_last(
        table, 0, G, grad_pooled, stream_in, pre3_0, pre2_0, misc, last_0
    )
    grads_other_0 = swap(grads_other_0)
    if paired:
        held = sum_readout.gather(sums_0)
        lefts_other_0 = tie(lefts_other_0, held, *sums_middle_1[0].prepare(sums_0))
        sum_readout.finish()
        sums_middle_1[0].onward()
        sums_middle_1[1].across(sums_0)
    middle_terms_0 = middle_terms(
        table,
        G,
        lefts_0,
        lefts_other_0,
        grads_0,
        grads_other_0,
        sums_of(middle_rows, C // half, parts=2 if paired else 1, last_line=True),
    )
    if paired:
        sum_middle_0 = Sum(move, middle_terms_0[:5], "middle_0_0")
        line_middle_0 = LineSum(move, middle_terms_0[5:], "middle_0_1")
        waited = [sums_middle_1[0].gather(*middle_terms_0), *sums_middle_1[1].prepare(*middle_terms_0)]
        grads_0 = tie(grads_0, *middle_terms_0, *waited)
        sums_middle_1[0].finish()
        sums_middle_1[1].onward()
        sum_middle_0.across()
        line_middle_0.line(0)
    blank = jnp.zeros((1, C), jnp.float32)
    rest = jnp.concatenate(
        [
            blank, sums_0[2:3], sums_0[0:1], sums_first_1[0:1], sums_1[2:3], sums_1[0:1],
            blank, sums_0[3:4], sums_0[1:2], sums_first_1[1:2], sums_1[3:4], sums_1[1:2],
            grad_readout_b.reshape(C, 4).T,
        ]
    )
    grad_in, _, grad_first_0, grad_first_other_0, side, side_other = back_first(
        table, 0, G, grads_0, pre1_0, direct_0, misc, rest, mid_0, matrix("first_0")
    )
    grad_first_other_0 = swap(grad_first_other_0)
    if paired:
        sides = [(side, swap(side_other))]
        waited = [line_middle_0.prepare(1, grad_in), *sum_middle_0.prepare(grad_in), sums_middle_1[1].gather(grad_in)]
        lefts_other_0 = tie(lefts_other_0, *waited)
        line_middle_0.line(1)
        sum_middle_0.onward()
        sums_middle_1[1].finish()
    else:
        sides = [(side, None), (side_other, None)]
    last_terms = plain_terms(
        table,
        [
            (lefts_0, 2, lefts_other_0, grads_0, 0, grads_other_0, 0),
            (lefts_1, 0, lefts_other_1, grad_first_1, 0, grad_first_other_1, None),
            (lefts_1, 2, lefts_other_1, grads_1, 0, grads_other_1, 0),
            (lefts_0, 0, lefts_other_0, grad_first_0, 0, grad_first_other_0, None),
        ],
        sides,
        sums_of(rows, C // half, matrices=5),
    )
    if paired:
        sum_last = Sum(move, last_terms, "last")
        sum_last.across()
        waited = sum_middle_0.gather(*last_terms)
        next_line = line_middle_0.prepare(2, *last_terms)
        line_middle_0.line(2)
        sum_middle_0.finish(next_line)
        sum_last.prepare(next_line)
        sum_last.onward()
        line_middle_0.across()
        sum_last.gather(*line_middle_0.operands)
        sum_last.finish()
        line_middle_0.finish()
        readout_owned = unite(move, sum_readout.owned, 1).reshape(rows, width)
        owned_1 = jnp.concatenate([total.owned for total in sums_middle_1])
        owned_0 = jnp.concatenate([sum_middle_0.owned, line_middle_0.owned])
        middle_owned = [unite(move, owned, 1).reshape(middle_rows, C) for owned in (owned_0, owned_1)]
        last_owned = unite(move, sum_last.owned, 5)
        side_owned = jnp.concatenate([last_owned[4, :, i, :SIDE] for i in range(2)], axis=1)
        last_owned = last_owned.reshape(5, rows, C)
    else:
        readout_owned = scattered(readout_terms)[0]
        middle_owned = [scattered(terms)[0] for terms in (middle_terms_0, middle_terms_1)]
        last_owned = scattered(last_terms, 5)
        side_owned = last_owned[4]
    scales = side_owned[:, cells : cells + MISC]
    return (
        output[None],
        grad_in[None],
        side_owned[:, :cells].T,
        jnp.stack([last_owned[3], last_owned[1]]),
        jnp.stack(middle_owned),
        jnp.stack([last_owned[0], last_owned[2]]),
        scales[:, 0:6].T.reshape(2, 3, rows),
        scales[:, 6:12].T.reshape(2, 3, rows),
        readout_owned,
        scales[:, 12:].reshape(-1),
    )


def solution(mesh):
    return jax.shard_map(
        functools.partial(local, Movement(mesh)),
        mesh=mesh,
        in_specs=(
            P(("dp", "fsdp"), None, None),
            P(("dp", "fsdp")),
            P(None, ("dp", "fsdp")),
            P(None, ("dp", "fsdp"), None),
            P(None, ("dp", "fsdp"), None),
            P(None, ("dp", "fsdp"), None),
            P(None, None, ("dp", "fsdp")),
            P(None, None, ("dp", "fsdp")),
            P(("dp", "fsdp"), None),
            P(("dp", "fsdp")),
            P(("dp", "fsdp"), None, None),
        ),
        out_specs=(
            P(("dp", "fsdp"), None, None),
            P(("dp", "fsdp"), None, None),
            P(None, ("dp", "fsdp")),
            P(None, ("dp", "fsdp"), None),
            P(None, ("dp", "fsdp"), None),
            P(None, ("dp", "fsdp"), None),
            P(None, None, ("dp", "fsdp")),
            P(None, None, ("dp", "fsdp")),
            P(("dp", "fsdp"), None),
            P(("dp", "fsdp")),
        ),
        check_vma=False,
    )
```

```python
import functools

import jax
import jax.numpy as jnp
import numpy as np
from jax import lax
from jax.experimental import pallas as pl
from jax.experimental.pallas import tpu as pltpu
from jax.sharding import PartitionSpec as P

C = 1024
G = 24
PLANE = 4
TILE = 256
ROWS = 144
PAD = 24
MISC = 16
HEAD = 1664
SIDE = 384
STEPS, LEVELS, OUT_STEPS, OUT_LEVELS, OUT_LINE, CORE, WINDOWS, TABLE = 0, 32, 64, 80, 96, 112, 113, 165
STEPPED, LEVELED, LINED = range(3)
COST = 4
COSTS = {"forward_block": 50}
VMEM = 60 * 1024 * 1024


def low(value):
    return value.astype(jnp.bfloat16)


def wide(value):
    return value.astype(jnp.float32)


def dot(left, right):
    return jnp.dot(left, right, preferred_element_type=jnp.float32)


def dot_rows(left, right):
    return lax.dot_general(left, right, (((1,), (1,)), ((), ())), preferred_element_type=jnp.float32)


def dot_sums(left, right):
    return lax.dot_general(left, right, (((0,), (0,)), ((), ())), preferred_element_type=jnp.float32)


def sigmoid(value):
    return 1.0 / (1.0 + jnp.exp(-value))


def centered(value):
    center = value - jnp.mean(value, axis=-1, keepdims=True)
    spread = jnp.mean(center * center, axis=-1, keepdims=True)
    scale = lax.rsqrt(spread + 1e-05)
    return center * scale, scale


def norm_back(grad, normal, scale, gain):
    inner = grad * gain
    first = jnp.mean(inner, axis=-1, keepdims=True)
    second = jnp.mean(inner * normal, axis=-1, keepdims=True)
    return scale * (inner - first - normal * second)


def silu_back(value):
    gate = sigmoid(value)
    return gate * (1.0 + value * (1.0 - gate))


def tiles(extent, size, body):
    def step(i, carry):
        body(pl.ds(pl.multiple_of(i * size, size), size))
        return carry

    lax.fori_loop(0, extent // size, step, 0)


def fold(value):
    return jnp.sum(value.reshape(-1, 8, value.shape[-1]), axis=0)


def columns_of(cells, side, lanes):
    index = lax.broadcasted_iota(jnp.int32, (cells, lanes), 0).astype(jnp.float32)
    return index - side * jnp.floor((index + 0.5) * (1.0 / side))


def beside(value, side, step):
    cells = value.shape[0]
    column = columns_of(cells, side, value.shape[1])
    inside = column < side - 1 if step > 0 else column > 0
    return jnp.where(inside, pltpu.roll(value, (cells - step) % cells, 0), 0.0)


class Blocks:
    def __init__(self):
        self.operands = []
        self.moves = []

    def operand(self, array):
        for number, known in enumerate(self.operands):
            if known is array:
                return number
        self.operands.append(array)
        return len(self.operands) - 1

    def add(self, array, block, row, column, place, stride, to_row, to_column, rows, columns):
        self.moves.append((self.operand(array), block, row, column, place, stride, to_row, to_column, rows, columns))

    @property
    def copies(self):
        return len(self.moves)

    def bind(self, refs, places, matrix, sems, to_blocks=False, base=0):
        made = []
        for number, block, row, column, place, stride, to_row, to_column, rows, columns in self.moves:
            first = to_row
            if place is not None:
                first = pl.multiple_of(places[place] * stride + to_row, 16)
            inside = matrix.at[pl.ds(first, rows), pl.ds(to_column, columns)]
            outside = refs[number] if block is None else refs[number].at[block]
            outside = outside.at[pl.ds(row, rows), pl.ds(column, columns)]
            pair = (inside, outside) if to_blocks else (outside, inside)
            made.append(pltpu.make_async_copy(*pair, sems.at[base + len(made)]))
        return made


def start(copies):
    for copy in copies:
        copy.start()


def wait(copies):
    for copy in copies:
        copy.wait()


ANY = pl.BlockSpec(memory_space=pltpu.HBM)
IN = pl.BlockSpec(memory_space=pltpu.VMEM)
SMEM = pl.BlockSpec(memory_space=pltpu.SMEM)


def call(kernel, name, ins, in_specs, outs, out_specs, scratch, flops, moved):
    short = COSTS.get(name, COST)
    return pl.pallas_call(
        kernel,
        name=name,
        out_shape=outs,
        in_specs=in_specs,
        out_specs=out_specs,
        scratch_shapes=scratch,
        compiler_params=pltpu.CompilerParams(vmem_limit_bytes=VMEM),
        cost_estimate=pl.CostEstimate(flops=int(flops) // short, bytes_accessed=int(moved) // short, transcendentals=0),
    )(*ins)


class Traffic:
    def __init__(self, sems):
        self.sems = sems
        self.used = 0
        self.sent = []

    def begin(self, source, target):
        copy = pltpu.make_async_copy(source, target, self.sems.at[self.used])
        self.used += 1
        copy.start()
        return copy

    def send(self, source, target):
        self.sent.append(self.begin(source, target))

    def load(self, blocks, refs, places, matrix):
        copies = blocks.bind(refs, places, matrix, self.sems, base=self.used)
        self.used += len(copies)
        start(copies)
        return copies

    def store(self, blocks, refs, places, matrix):
        copies = blocks.bind(refs, places, matrix, self.sems, to_blocks=True, base=self.used)
        self.used += len(copies)
        start(copies)
        self.sent += copies

    def finish(self):
        wait(self.sent)


def shaped(*shape, dtype=jnp.float32):
    return jax.ShapeDtypeStruct(shape, dtype)


def forward_block(table, number, side, stream, features, misc, w_first, w_middle, w_last):
    cells = side * side
    opening = features is not None
    n_first, n_middle, n_last = len(w_first.operands), len(w_middle.operands), len(w_last.operands)
    given = [features] if opening else [stream, misc]
    given_count = len(given)
    bf16 = jnp.bfloat16
    n_lefts = 3 if opening else 4

    def kernel(table_ref, *refs):
        refs = list(refs)
        heads = [refs.pop(0) for _ in range(given_count)]
        firsts = [refs.pop(0) for _ in range(n_first)]
        middles = [refs.pop(0) for _ in range(n_middle)]
        lasts = [refs.pop(0) for _ in range(n_last)]
        if opening:
            misc_ref, pooled_ref, u_out = refs.pop(0), refs.pop(0), refs.pop(0)
            u_ref = refs.pop(0 - 1)
        else:
            u_ref, misc_ref = heads
        lefts_out, pre1_out, pre2_out, pre3_out, wi_out, wo_out = [refs.pop(0) for _ in range(6)]
        wi, wm, wo, taps, lefts, above, below, work, pairs, pre1, pre2, pre3, sems = refs
        traffic = Traffic(sems)
        first_copies = traffic.load(w_first, firsts, table_ref, wi)
        middle_copies = traffic.load(w_middle, middles, table_ref, wm)
        last_copies = traffic.load(w_last, lasts, table_ref, wo)
        wait(first_copies)
        traffic.send(wi.at[:, pl.ds(0, C)], wi_out)
        if opening:

            def place(cut):
                turned = jnp.transpose(wide(wi[cut, C:HEAD]))
                u_ref[:, cut] = wide(heads[0][:, cut]) + turned[:cells]
                misc_ref[:, cut] = turned[cells : cells + MISC]

            tiles(C, 128, place)
            traffic.send(u_ref, u_out)

        def lower(rows):
            lefts[0, rows, :] = low(u_ref[rows, :])

        tiles(cells, ROWS, lower)

        def first(cut):
            pre1[:, cut] = dot(lefts[0], wi[:, cut])

        tiles(C, TILE, first)
        traffic.send(pre1, pre1_out)

        def norm_act(source, norm, store):
            gain = misc_ref[3 * number + norm : 3 * number + norm + 1, :]
            bias = misc_ref[6 + 3 * number + norm : 7 + 3 * number + norm, :]

            def rows_of(rows):
                normal, _ = centered(source[rows, :])
                hidden = normal * gain + bias
                store(rows, hidden * sigmoid(hidden))

            tiles(cells, ROWS, rows_of)

        def keep_first(rows, value):
            work[rows, :] = value
            lefts[1, rows, :] = low(value)

        norm_act(pre1, 0, keep_first)

        def spread(i, carry):
            cut = pl.ds(pl.multiple_of(i * 128, 128), 128)
            value = work[:, cut]
            taps[:, pl.ds(pl.multiple_of(i * 128, 128), 128)] = low(beside(value, side, -1))
            taps[:, pl.ds(pl.multiple_of(C + i * 128, 128), 128)] = low(value)
            taps[:, pl.ds(pl.multiple_of(2 * C + i * 128, 128), 128)] = low(beside(value, side, 1))
            return carry

        lax.fori_loop(0, C // 128, spread, 0)
        zeros = jnp.zeros((PAD, TILE), jnp.float32)
        for ref in (above, below):
            ref[:PAD, :] = zeros
            ref[PAD + cells :, :] = zeros
        wait(middle_copies)

        def middle(cut):
            above[PAD : PAD + cells, :] = dot(taps[...], wm[0 : 3 * C, cut])
            below[PAD : PAD + cells, :] = dot(taps[...], wm[6 * C : 9 * C, cut])
            same = dot(taps[...], wm[3 * C : 6 * C, cut])
            pre2[:, cut] = same + above[PAD - side : PAD - side + cells, :] + below[PAD + side : PAD + side + cells, :]

        tiles(C, TILE, middle)
        traffic.send(pre2, pre2_out)

        def keep_second(rows, value):
            lefts[2, rows, :] = low(value)

        norm_act(pre2, 1, keep_second)
        if opening:
            traffic.send(lefts, lefts_out)
        wait(last_copies)
        traffic.send(wo, wo_out)

        def last(cut):
            pre3[:, cut] = dot(lefts[2], wo[:, cut])

        tiles(C, TILE, last)
        traffic.send(pre3, pre3_out)
        gain = misc_ref[3 * number + 2 : 3 * number + 3, :]
        bias = misc_ref[8 + 3 * number : 9 + 3 * number, :]

        def close(rows):
            normal, _ = centered(pre3[rows, :])
            total = u_ref[rows, :] + (normal * gain + bias)
            value = total * sigmoid(total)
            if opening:
                work[rows, :] = value
            else:
                lefts[3, rows, :] = low(value)

        tiles(cells, ROWS, close)
        if opening:
            half = side // 2

            def pool(cut):
                value = work[:, cut].reshape(half, 2, side, 128)
                pairs[...] = (value[:, 0] + value[:, 1]).reshape(half * side, 128)
                pooled_ref[:, cut] = 0.25 * (
                    pairs[pl.ds(0, half * half, 2), :] + pairs[pl.ds(1, half * half, 2), :]
                )

            tiles(C, 128, pool)
        else:
            traffic.send(lefts, lefts_out)
        traffic.finish()

    outs, out_specs = [], []
    if opening:
        outs += [shaped(MISC, C), shaped(cells // 4, C), shaped(cells, C)]
        out_specs += [IN, IN, ANY]
    outs += [shaped(n_lefts, cells, C, dtype=bf16)] + [shaped(cells, C)] * 3 + [shaped(C, C, dtype=bf16)] * 2
    out_specs += [ANY] * 6
    copies = w_first.copies + w_middle.copies + w_last.copies + 7
    scratch = [
        pltpu.VMEM((C, HEAD if opening else C), bf16),
        pltpu.VMEM((9 * C, C), bf16),
        pltpu.VMEM((C, C), bf16),
        pltpu.VMEM((cells, 3 * C), bf16),
        pltpu.VMEM((n_lefts, cells, C), bf16),
        pltpu.VMEM((cells + 2 * PAD, TILE), jnp.float32),
        pltpu.VMEM((cells + 2 * PAD, TILE), jnp.float32),
        pltpu.VMEM((cells, C), jnp.float32),
        pltpu.VMEM((cells // 2, 128), jnp.float32),
        pltpu.VMEM((cells, C), jnp.float32),
        pltpu.VMEM((cells, C), jnp.float32),
        pltpu.VMEM((cells, C), jnp.float32),
        pltpu.SemaphoreType.DMA((copies,)),
    ]
    if opening:
        scratch.append(pltpu.VMEM((cells, C), jnp.float32))
    weights = w_first.operands + w_middle.operands + w_last.operands
    return call(
        kernel,
        "forward_block",
        [table] + given + weights,
        [SMEM] + [IN] * given_count + [ANY] * len(weights),
        outs,
        out_specs,
        scratch,
        2 * cells * 11 * C * C,
        22 * C * C + 20 * cells * C,
    )


def readout(table, live, lefts, bias, cotangent, weights):
    cells, columns = cotangent.shape
    n_weights = len(weights.operands)
    bf16 = jnp.bfloat16
    cut_size = 512
    half = columns // 2

    def kernel(table_ref, live_ref, lefts_ref, bias_ref, cot_ref, *refs):
        refs = list(refs)
        sources = [refs.pop(0) for _ in range(n_weights)]
        output, grad_stream, grad_bias, own, other, matrix, low_ref, sems = refs
        traffic = Traffic(sems)
        given = traffic.begin(lefts_ref.at[3], low_ref)
        copies = traffic.load(weights, sources, table_ref, matrix)
        factor = wide(live_ref[0])
        core = table_ref[CORE]
        grad_stream[...] = jnp.zeros((cells, C), jnp.float32)
        given.wait()
        wait(copies)
        for part in range(2):

            def step(cut, part=part):
                here = pl.ds(pl.multiple_of(part * half + cut.start, cut_size), cut_size)
                logits = dot(low_ref[...], matrix[:, here]) + bias_ref[:, here]
                share = 0.5 * (1.0 + lax.erf(logits * (0.5**0.5)))
                output[:, here] = low(logits * share * factor)
                slope = share + logits * (jnp.exp(-0.5 * logits * logits) * (0.5 / jnp.pi) ** 0.5)
                grad_logits = low(wide(cot_ref[:, here]) * factor * slope)
                grad_bias[:, here] = jnp.sum(wide(grad_logits), axis=0, keepdims=True)

                @pl.when(core == part)
                def _():
                    own[:, cut] = grad_logits

                @pl.when(core != part)
                def _():
                    other[:, cut] = grad_logits

                grad_stream[...] += dot_rows(grad_logits, matrix[:, here])

            tiles(half, cut_size, step)

    outs = [shaped(cells, columns, dtype=bf16), shaped(cells, C), shaped(1, columns)]
    outs += [shaped(cells, half, dtype=bf16)] * 2
    scratch = [
        pltpu.VMEM((C, columns), bf16),
        pltpu.VMEM((cells, C), bf16),
        pltpu.SemaphoreType.DMA((weights.copies + 1,)),
    ]
    return call(
        kernel,
        "readout",
        [table, live, lefts, bias, cotangent] + weights.operands,
        [SMEM] * 2 + [ANY] + [IN] * 2 + [ANY] * n_weights,
        outs,
        [IN] * 5,
        scratch,
        4 * cells * C * columns,
        2 * C * columns + 4 * cells * columns,
    )


def back_last(table, number, side, grad_out, stream, pre3, pre2, misc, w_last):
    cells = side * side
    pooled = grad_out.shape[0] != cells
    n_weights = len(w_last.operands)
    bf16 = jnp.bfloat16
    half = C // 2

    def kernel(table_ref, grad_ref, u_in, pre3_in, pre2_in, misc_ref, *refs):
        refs = list(refs)
        sources = [refs.pop(0) for _ in range(n_weights)]
        direct_out, grads, other, sums, matrix, direct, u_ref, pre3_ref, pre2_ref, work, parts, pairs, sems = refs
        traffic = Traffic(sems)
        opened = [traffic.begin(u_in, u_ref), traffic.begin(pre3_in, pre3_ref)]
        later = traffic.begin(pre2_in, pre2_ref)
        copies = traffic.load(w_last, sources, table_ref, matrix)
        parts[...] = jnp.zeros_like(parts)
        gain = misc_ref[3 * number + 2 : 3 * number + 3, :]
        bias = misc_ref[8 + 3 * number : 9 + 3 * number, :]
        if pooled:

            def spread(cut):
                value = 0.25 * grad_ref[:, cut]
                pairs[pl.ds(0, cells // 4, 2), :] = value
                pairs[pl.ds(1, cells // 4, 2), :] = value
                twice = pairs[...].reshape(side // 2, 1, side, 128)
                work[:, cut] = jnp.broadcast_to(twice, (side // 2, 2, side, 128)).reshape(cells, 128)

            tiles(C, 128, spread)
        grad_from = work if pooled else grad_ref
        wait(opened)

        def close(rows):
            normal, scale = centered(pre3_ref[rows, :])
            total = u_ref[rows, :] + (normal * gain + bias)
            inner = grad_from[rows, :] * silu_back(total)
            direct[rows, :] = inner
            parts[0:8, :] += fold(inner * normal)
            parts[8:16, :] += fold(inner)
            grads[0, rows, :] = low(norm_back(inner, normal, scale, gain))

        tiles(cells, ROWS, close)
        traffic.send(direct, direct_out)
        gain = misc_ref[3 * number + 1 : 3 * number + 2, :]
        bias = misc_ref[7 + 3 * number : 8 + 3 * number, :]
        wait(copies)

        def last(cut):
            work[:, cut] = dot_rows(grads[0], matrix[cut, :])

        tiles(C, TILE, last)
        later.wait()

        def norm(rows):
            normal, scale = centered(pre2_ref[rows, :])
            hidden = normal * gain + bias
            inner = work[rows, :] * silu_back(hidden)
            parts[16:24, :] += fold(inner * normal)
            parts[24:32, :] += fold(inner)
            grads[1, rows, :] = low(norm_back(inner, normal, scale, gain))

        tiles(cells, ROWS, norm)
        sums[...] = jnp.sum(parts[...].reshape(4, 8, C), axis=1)
        there = pl.ds(pl.multiple_of((1 - table_ref[CORE]) * half, half), half)
        for i in range(2):
            other[i] = grads[i, :, there]
        traffic.finish()

    outs = [shaped(cells, C), shaped(2, cells, C, dtype=bf16), shaped(2, cells, half, dtype=bf16), shaped(4, C)]
    f32 = jnp.float32
    scratch = [pltpu.VMEM((C, C), bf16)] + [pltpu.VMEM((cells, C), f32)] * 5
    scratch += [pltpu.VMEM((32, C), f32), pltpu.VMEM((cells // 2, 128), f32), pltpu.SemaphoreType.DMA((w_last.copies + 4,))]
    return call(
        kernel,
        "back_last",
        [table, grad_out, stream, pre3, pre2, misc] + w_last.operands,
        [SMEM, IN, ANY, ANY, ANY, IN] + [ANY] * n_weights,
        outs,
        [ANY, IN, IN, IN],
        scratch,
        2 * cells * C * C,
        2 * C * C + 24 * cells * C,
    )


def weight_terms(table, middle, products, sides, out_blocks):
    bf16 = jnp.bfloat16
    if middle is not None:
        products = [(middle[1], 1, middle[2], middle[3], 1, middle[4], 1)] + products
    pair = products[0][2] is not None
    given = []
    for left, _, left_other, right, _, right_other, _ in products:
        given += [left, right] + ([left_other, right_other] if pair else [])
    n_given = len(given)
    n_outs = len(out_blocks.operands)
    width = out_blocks.operands[0].shape[-1]
    cells_of = [product[0].shape[-2] for product in products]
    factor = 2 if pair else 1
    heights = [C] * len(products)
    if middle is not None:
        heights[0] = 9 * C
    starts = [sum(heights[:i]) for i in range(len(heights) + 1)]
    grid_side = middle[0] if middle is not None else 0
    grid_cells = grid_side * grid_side
    size = 512

    def kernel(table_ref, *refs):
        refs = list(refs)
        sources = [refs.pop(0) for _ in range(n_given)]
        beside_refs = [refs.pop(0) for _ in range(len(sides) * factor)]
        targets = [refs.pop(0) for _ in range(n_outs)]
        grad, sems = refs.pop(0), refs.pop(0)
        traffic = Traffic(sems)
        waits = []
        for (_, left_at, _, _, right_at, _, other_at), cells in zip(products, cells_of):
            left, right = refs.pop(0), refs.pop(0)
            left_in, right_in = sources.pop(0), sources.pop(0)
            copies = [traffic.begin(left_in.at[left_at], left.at[pl.ds(0, cells), :])]
            if right_at is not None:
                right_in = right_in.at[right_at]
                if pair:
                    right_in = right_in.at[:, pl.ds(pl.multiple_of(table_ref[CORE] * width, width), width)]
            copies.append(traffic.begin(right_in, right.at[pl.ds(0, cells), :]))
            if pair:
                left_in, right_in = sources.pop(0), sources.pop(0)
                copies.append(traffic.begin(left_in.at[left_at], left.at[pl.ds(cells, cells), :]))
                if other_at is not None:
                    right_in = right_in.at[other_at]
                copies.append(traffic.begin(right_in, right.at[pl.ds(cells, cells), :]))
            waits.append((copies, left, right))
        at = 0
        for side in sides:
            extent = side[0].shape[-1]
            total = beside_refs.pop(0)[...]
            if pair:
                total = low(wide(total) + wide(beside_refs.pop(0)[...]))
            grad[starts[-1] :, at : at + extent] = total
            at += extent
        if sides:
            grad[starts[-1] :, at:] = jnp.zeros((C, width - at), bf16)
        if middle is not None:
            taps, shifted, padded = refs
            copies, act, right = waits[0]
            padded[:PAD, :] = jnp.zeros((PAD, 128), jnp.float32)
            padded[PAD + grid_cells :, :] = jnp.zeros((PAD, 128), jnp.float32)
            wait(copies)
            for first in range(0, factor * grid_cells, grid_cells):
                rows = slice(first, first + grid_cells)

                def spread(i, carry, rows=rows):
                    cut = pl.ds(pl.multiple_of(i * 128, 128), 128)
                    value = wide(act[rows, cut])
                    taps[rows, cut] = low(beside(value, grid_side, -1))
                    taps[rows, pl.ds(pl.multiple_of(C + i * 128, 128), 128)] = act[rows, cut]
                    taps[rows, pl.ds(pl.multiple_of(2 * C + i * 128, 128), 128)] = low(beside(value, grid_side, 1))
                    return carry

                def shift(i, carry, rows=rows):
                    cut = pl.ds(pl.multiple_of(i * 128, 128), 128)
                    padded[PAD : PAD + grid_cells, :] = wide(right[rows, cut])
                    shifted[0, rows, cut] = low(padded[PAD + grid_side : PAD + grid_side + grid_cells, :])
                    shifted[1, rows, cut] = right[rows, cut]
                    shifted[2, rows, cut] = low(padded[PAD - grid_side : PAD - grid_side + grid_cells, :])
                    return carry

                lax.fori_loop(0, C // 128, spread, 0)
                lax.fori_loop(0, width // 128, shift, 0)
            for row_tap in range(3):

                def part(i, carry, row_tap=row_tap):
                    cut = pl.ds(pl.multiple_of(i * size, size), size)
                    target = pl.ds(pl.multiple_of(row_tap * 3 * C + i * size, size), size)
                    grad[target, :] = low(dot_sums(taps[:, cut], shifted[row_tap]))
                    return carry

                lax.fori_loop(0, 3 * C // size, part, 0)
        for number, (copies, left, right) in enumerate(waits):
            if middle is not None and number == 0:
                continue
            wait(copies)

            def part(cut, number=number, left=left, right=right):
                target = pl.ds(pl.multiple_of(starts[number] + cut.start, TILE), TILE)
                grad[target, :] = low(dot_sums(left[:, cut], right[...]))

            tiles(C, TILE, part)
        traffic.store(out_blocks, targets, table_ref, grad)
        traffic.finish()

    outs = [shaped(*array.shape, dtype=bf16) for array in out_blocks.operands]
    scratch = [
        pltpu.VMEM((starts[-1] + (C if sides else 0), width), bf16),
        pltpu.SemaphoreType.DMA((out_blocks.copies + 4 * len(products),)),
    ]
    for cells in cells_of:
        scratch += [pltpu.VMEM((factor * cells, C), bf16), pltpu.VMEM((factor * cells, width), bf16)]
    if middle is not None:
        scratch += [
            pltpu.VMEM((factor * grid_cells, 3 * C), bf16),
            pltpu.VMEM((3, factor * grid_cells, width), bf16),
            pltpu.VMEM((grid_cells + 2 * PAD, 128), jnp.float32),
        ]
    besides = [array for side in sides for array in side if array is not None]
    return call(
        kernel,
        "weight_terms",
        [table] + given + besides,
        [SMEM] + [ANY] * n_given + [IN] * len(besides),
        outs,
        [ANY] * n_outs,
        scratch,
        sum(2 * factor * cells * height * width for cells, height in zip(cells_of, heights)),
        2 * starts[-1] * width + sum(4 * factor * cells * C for cells in cells_of),
    )


def plane_terms(table, side, acts, grads, block_rows):
    cells = side * side
    total = sum(array.shape[0] for array in acts)
    bf16 = jnp.bfloat16
    blocks = 4
    span = 3 * 128

    def kernel(table_ref, *refs):
        refs = list(refs)
        act_refs = [refs.pop(0) for _ in acts]
        grad_refs = [refs.pop(0) for _ in grads]
        target, act, right, taps, terms, sems = refs
        traffic = Traffic(sems)
        copies, row = [], 0
        for source, other in zip(act_refs, grad_refs):
            rows = pl.ds(row, source.shape[0])
            copies += [traffic.begin(source, act.at[rows, :]), traffic.begin(other, right.at[rows, :])]
            row += source.shape[0]
        index = lax.broadcasted_iota(jnp.int32, (total, 128), 0).astype(jnp.float32)
        inside = index - cells * jnp.floor((index + 0.5) * (1.0 / cells))
        line = jnp.floor((inside + 0.5) * (1.0 / side))
        column = inside - side * line
        wait(copies)
        for block in range(blocks):
            for tile in range(3):
                at = WINDOWS + blocks + 4 * (3 * block + tile)
                cut = pl.ds(pl.multiple_of(table_ref[at], 128), 128)
                value = pltpu.roll(wide(act[:, cut]), table_ref[at + 1], 0)
                tap_line = line + (table_ref[at + 2] - 1).astype(jnp.float32)
                tap_column = column + (table_ref[at + 3] - 1).astype(jnp.float32)
                there = (tap_line >= 0) & (tap_line < side) & (tap_column >= 0) & (tap_column < side)
                first = block * span + tile * 128
                taps[:, first : first + 128] = low(jnp.where(there, value, 0.0))
            terms[block] = low(dot_sums(taps[:, block * span : (block + 1) * span], right[...]))
            start_row = pl.multiple_of(table_ref[WINDOWS + block], 32)
            traffic.send(terms.at[block, pl.ds(start_row, block_rows), :], target.at[block])
        traffic.finish()

    return call(
        kernel,
        "plane_terms",
        [table] + acts + grads,
        [SMEM] + [ANY] * (2 * len(acts)),
        shaped(blocks, block_rows, C, dtype=bf16),
        ANY,
        [
            pltpu.VMEM((total, C), bf16),
            pltpu.VMEM((total, C), bf16),
            pltpu.VMEM((total, blocks * span), bf16),
            pltpu.VMEM((blocks, span, C), bf16),
            pltpu.SemaphoreType.DMA((2 * len(acts) + blocks,)),
        ],
        2 * total * blocks * span * C,
        4 * total * C + 2 * blocks * block_rows * C,
    )


def back_first(table, number, side, grads, pre1, direct, misc, rests, w_middle, w_first):
    cells = side * side
    closing = rests is not None
    n_middle, n_first = len(w_middle.operands), len(w_first.operands)
    bf16 = jnp.bfloat16
    extra = rests if closing else []
    half = C // 2
    side_half = SIDE

    def kernel(table_ref, grads_in, pre1_in, direct_in, misc_ref, *refs):
        refs = list(refs)
        rest_refs = [refs.pop(0) for _ in extra]
        middles = [refs.pop(0) for _ in range(n_middle)]
        firsts = [refs.pop(0) for _ in range(n_first)]
        grad_u, sums, grad_pre1, other = [refs.pop(0) for _ in range(4)]
        turned = [refs.pop(0), refs.pop(0)] if closing else None
        wm, wi, grad_ref, pre1_ref, direct_ref, taps, above, below, work, parts, sems = refs
        traffic = Traffic(sems)
        given = traffic.begin(grads_in.at[1], grad_ref)
        middle_copies = traffic.load(w_middle, middles, table_ref, wm)
        pre1_copy = traffic.begin(pre1_in, pre1_ref)
        first_copies = traffic.load(w_first, firsts, table_ref, wi)
        direct_copy = traffic.begin(direct_in, direct_ref)
        parts[...] = jnp.zeros_like(parts)
        zeros = jnp.zeros((PAD, TILE), jnp.float32)
        for ref in (above, below):
            ref[:PAD, :] = zeros
            ref[PAD + cells :, :] = zeros
        given.wait()

        def spread(i, carry):
            cut = pl.ds(pl.multiple_of(i * 128, 128), 128)
            value = wide(grad_ref[:, cut])
            taps[:, cut] = low(beside(value, side, 1))
            taps[:, pl.ds(pl.multiple_of(C + i * 128, 128), 128)] = grad_ref[:, cut]
            taps[:, pl.ds(pl.multiple_of(2 * C + i * 128, 128), 128)] = low(beside(value, side, -1))
            return carry

        lax.fori_loop(0, C // 128, spread, 0)
        wait(middle_copies)

        def middle(i, carry):
            def row(tap):
                total = None
                for column in range(3):
                    source = pl.ds(pl.multiple_of((3 * tap + column) * C + i * TILE, TILE), TILE)
                    term = dot_rows(taps[:, column * C : (column + 1) * C], wm[source, :])
                    total = term if total is None else total + term
                return total

            above[PAD : PAD + cells, :] = row(0)
            below[PAD : PAD + cells, :] = row(2)
            cut = pl.ds(pl.multiple_of(i * TILE, TILE), TILE)
            work[:, cut] = (
                row(1) + above[PAD + side : PAD + side + cells, :] + below[PAD - side : PAD - side + cells, :]
            )
            return carry

        lax.fori_loop(0, C // TILE, middle, 0)
        gain = misc_ref[3 * number : 3 * number + 1, :]
        bias = misc_ref[6 + 3 * number : 7 + 3 * number, :]
        pre1_copy.wait()

        def norm(rows):
            normal, scale = centered(pre1_ref[rows, :])
            hidden = normal * gain + bias
            inner = work[rows, :] * silu_back(hidden)
            parts[0:8, :] += fold(inner * normal)
            parts[8:16, :] += fold(inner)
            grad_pre1[0, rows, :] = low(norm_back(inner, normal, scale, gain))

        tiles(cells, ROWS, norm)
        sums[...] = jnp.sum(parts[...].reshape(2, 8, C), axis=1)
        core = table_ref[CORE]
        other[...] = grad_pre1[0, :, pl.ds(pl.multiple_of((1 - core) * half, half), half)]
        wait(first_copies)
        direct_copy.wait()

        def first(cut):
            grad_u[:, cut] = direct_ref[:, cut] + dot_rows(grad_pre1[0], wi[cut, :])

        tiles(C, TILE, first)
        if closing:

            last_0, first_1, last_1, bias_grad = rest_refs

            def turn(cut):
                stacked = jnp.concatenate(
                    [grad_u[:, cut]]
                    + [ref[row : row + 1, cut] for ref, row in ((sums, 0), (last_0, 2), (last_0, 0))]
                    + [ref[row : row + 1, cut] for ref, row in ((first_1, 0), (last_1, 2), (last_1, 0))]
                    + [ref[row : row + 1, cut] for ref, row in ((sums, 1), (last_0, 3), (last_0, 1))]
                    + [ref[row : row + 1, cut] for ref, row in ((first_1, 1), (last_1, 3), (last_1, 1))]
                    + [bias_grad[:, cut], jnp.zeros((2 * side_half - cells - MISC, 128), jnp.float32)]
                )
                parts_of = low(jnp.transpose(stacked))
                for part in range(2):
                    piece = parts_of[:, part * side_half : (part + 1) * side_half]

                    @pl.when(core == part)
                    def _(piece=piece):
                        turned[0][cut, :] = piece

                    @pl.when(core != part)
                    def _(piece=piece):
                        turned[1][cut, :] = piece

            tiles(C, 128, turn)

    outs = [shaped(cells, C), shaped(2, C), shaped(1, cells, C, dtype=bf16), shaped(cells, half, dtype=bf16)]
    if closing:
        outs += [shaped(C, side_half, dtype=bf16)] * 2
    f32 = jnp.float32
    scratch = [
        pltpu.VMEM((9 * C, C), bf16),
        pltpu.VMEM((C, C), bf16),
        pltpu.VMEM((cells, C), bf16),
        pltpu.VMEM((cells, C), f32),
        pltpu.VMEM((cells, C), f32),
        pltpu.VMEM((cells, 3 * C), bf16),
        pltpu.VMEM((cells + 2 * PAD, TILE), f32),
        pltpu.VMEM((cells + 2 * PAD, TILE), f32),
        pltpu.VMEM((cells, C), f32),
        pltpu.VMEM((16, C), f32),
        pltpu.SemaphoreType.DMA((w_middle.copies + w_first.copies + 3,)),
    ]
    weights = w_middle.operands + w_first.operands
    return call(
        kernel,
        "back_first",
        [table, grads, pre1, direct, misc] + extra + weights,
        [SMEM] + [ANY] * 3 + [IN] * (1 + len(extra)) + [ANY] * len(weights),
        outs,
        [IN] * len(outs),
        scratch,
        2 * cells * 10 * C * C,
        20 * C * C + 24 * cells * C,
    )


def place_halves(core, pair, rest=None):
    _, rows, half = pair[0].shape
    extra = [] if rest is None else [rest]

    def kernel(core_ref, mine, other, *refs):
        target = refs[-1]
        for part in range(2):

            @pl.when(core_ref[0] == part)
            def _(part=part):
                target[0, :, part * half : (part + 1) * half] = mine[0]
                target[0, :, (1 - part) * half : (2 - part) * half] = other[0]

        if extra:
            target[1] = wide(refs[0][0])

    return call(
        kernel,
        "place_halves",
        [core, *pair] + extra,
        [SMEM] + [IN] * (2 + len(extra)),
        shaped(1 + len(extra), rows, 2 * half),
        IN,
        [],
        0,
        16 * rows * half,
    )


def place_last(core, mine, other, cells):
    _, rows, half = mine.shape

    def kernel(core_ref, mine_ref, other_ref, first, last, pos, gains, biases, bias, side):
        for part in range(2):

            @pl.when(core_ref[0] == part)
            def _(part=part):
                for target, block, number in ((last, 0, 0), (first, 1, 1), (last, 1, 2), (first, 0, 3)):
                    target[block, :, part * half : (part + 1) * half] = mine_ref[number]
                    target[block, :, (1 - part) * half : (2 - part) * half] = other_ref[number]
                side[:, part * SIDE : (part + 1) * SIDE] = mine_ref[4, :, :SIDE]
                side[:, (1 - part) * SIDE : (2 - part) * SIDE] = other_ref[4, :, :SIDE]

        turned = jnp.transpose(side[...])
        pos[...] = turned[:cells]
        for number in range(6):
            gains[number // 3, number % 3 : number % 3 + 1, :] = turned[cells + number : cells + number + 1]
            biases[number // 3, number % 3 : number % 3 + 1, :] = turned[cells + 6 + number : cells + 7 + number]
        bias[...] = turned[cells + 12 : cells + MISC]

    return call(
        kernel,
        "place_last",
        [core, mine, other],
        [SMEM, IN, IN],
        [shaped(2, rows, 2 * half)] * 2 + [shaped(cells, rows)] + [shaped(2, 3, rows)] * 2 + [shaped(4, rows)],
        [IN] * 6,
        [pltpu.VMEM((rows, 2 * SIDE), jnp.float32)],
        0,
        32 * rows * half * 5,
    )


def after(value, *earlier):
    return lax.optimization_barrier((value, earlier))[0]


class Movement:
    def __init__(self, mesh):
        self.dp = mesh.shape["dp"]
        self.cores = mesh.shape["fsdp"]
        self.line = self.dp // PLANE
        self.devices = self.dp * self.cores
        self.ring = [0] + list(range(1, self.line, 2)) + list(range(2, self.line, 2))[::-1]
        self.paired = self.cores == 2 and self.line == 4

    def flip(self, value, bits):
        return lax.ppermute(value, "dp", [(i, i ^ bits) for i in range(self.dp)])

    def along(self, value):
        pairs = []
        for position, level in enumerate(self.ring):
            following = self.ring[(position + 1) % self.line]
            pairs += [(level * PLANE + near, following * PLANE + near) for near in range(PLANE)]
        return lax.ppermute(value, "dp", pairs)

    def swap(self, value):
        return lax.ppermute(value, "fsdp", [(0, 1), (1, 0)])

    def lines(self):
        return [[level * PLANE + near for level in range(self.line)] for near in range(PLANE)]

    def table(self):
        if not self.paired:
            return jnp.zeros((TABLE,), jnp.int32)
        steps, chips = range(self.line), range(PLANE)
        halves = [(1, 0), (1, 1), (3, 0), (3, 1), (2, 2), (2, 3), (3, 2), (3, 3), (1, 2), (1, 3), (2, 0), (2, 1)]
        halves += [(0, step) for step in steps]
        rows = []
        for device in range(self.devices):
            chip, core = divmod(device, 2)
            level, near = divmod(chip, PLANE)
            position = self.ring.index(level)

            def chip_at(far, level, near=near):
                return level * PLANE + (near ^ far)

            def step_at(step, position=position):
                return self.ring[(position + step) % self.line]

            row = [chip_at(far, step_at(-step)) * 2 + (core + k) % 2 for k in range(2) for far in chips for step in steps]
            row += [chip_at(far, step) * 2 + (core + k) % 2 for k in range(2) for far in chips for step in steps]
            row += [chip_at(far, step_at(step)) for far, step in halves]
            row += [chip_at(far, step) for far, step in halves]
            row += [chip_at(far, step_at(step)) for step in reversed(steps) for far in chips]
            row.append(core)
            firsts = [chip_at(0, step) * 2 + core for step in steps]
            firsts = [9 * C // self.devices * owner for owner in firsts]
            row += [first % 128 for first in firsts]
            side = G // 2
            for first in firsts:
                for tile in range(first // 128, first // 128 + 3):
                    tap, part = divmod(tile, C // 128)
                    tap_row, tap_column = divmod(tap, 3)
                    away = (tap_row - 1) * side + tap_column - 1
                    row += [128 * part, -away % (2 * PLANE * side * side), tap_row, tap_column]
            rows.append(row)
        index = lax.axis_index("dp") * self.cores + lax.axis_index("fsdp")
        return lax.dynamic_index_in_dim(jnp.asarray(np.array(rows, np.int32)), index, 0, keepdims=False)


class Piece:
    def __init__(self, move, own, name):
        self.move = move
        self.own = own
        self.name = name
        self.rows = own.shape[0]
        self.at = STEPS
        self.found = []

    def keep(self, array, far, steps, first=0, other=None):
        for i, step in enumerate(steps):
            for core, held in enumerate((array, other)):
                self.found.append((held, first + i * self.rows, self.at + 16 * core + 4 * far + step))

    def line(self, second, third):
        with jax.named_scope(self.name + "_line"):
            one = self.move.along(self.own)
            two = self.move.along(after(one, *second) if second else one)
            three = self.move.along(after(two, *third))
        self.passed = (one, two, three)
        self.held = jnp.concatenate([self.own, one, two, three])

    def levels(self, *earlier):
        with jax.named_scope(self.name + "_levels"):
            own = after(self.own, *earlier) if earlier else self.own
            self.held = lax.all_gather(own, "dp", axis_index_groups=self.move.lines(), axis=0, tiled=True)
        self.at = LEVELS

    def settle_line(self, *earlier):
        with jax.named_scope("swap"):
            other = self.move.swap(after(self.held, *earlier) if earlier else self.held)
        self.keep(self.held, 0, range(4), other=other)

    def plane_first(self):
        half = self.rows // 2
        with jax.named_scope(self.name + "_plane"):
            first, second = self.sides = self.move.flip(self.own, 1), self.move.flip(self.own, 2)
            self.fars = (self.move.flip(first[:half], 2), self.move.flip(second[half:], 1))
            self.passed = (jnp.concatenate([self.own, first, second, *self.fars]),)

    def pass_on(self, *earlier):
        with jax.named_scope(self.name + "_line"):
            self.passed += (self.move.along(after(self.passed[-1], *earlier)),)

    def end_line(self, *earlier):
        for step, array in enumerate(after(self.passed, *earlier)):
            other = self.move.swap(array)
            for far in range(PLANE):
                self.keep(array, far, [step], first=far * self.rows, other=other)


def cross(move, pieces, fars, *earlier):
    over_first = [piece.held for piece in pieces] + [piece.second[2 * piece.rows : 4 * piece.rows] for piece in fars]
    over_second = [piece.held for piece in pieces] + [piece.first[: 2 * piece.rows] for piece in fars]
    over_first, over_second = [jnp.concatenate(parts) if len(parts) > 1 else parts[0] for parts in (over_first, over_second)]
    if earlier:
        over_first, over_second = after((over_first, over_second), *earlier)
    with jax.named_scope("_".join(piece.name for piece in pieces + fars) + "_plane"):
        first, second = move.flip(over_first, 1), move.flip(over_second, 2)
    row = 0
    for piece in pieces:
        piece.sides = (first, second, row)
        piece.first = first[row : row + 4 * piece.rows]
        piece.second = second[row : row + 4 * piece.rows]
        row += 4 * piece.rows
    for piece in fars:
        piece.far_sides = (first, second, row)
        piece.far_first = first
        row += 2 * piece.rows
    return first, second


def settle(move, pieces, fars, *earlier):
    first, second = (pieces[0].sides if pieces else fars[0].far_sides)[:2]
    if earlier:
        first, second = after((first, second), *earlier)
    with jax.named_scope("swap"):
        first_other, second_other = move.swap(first), move.swap(second)
    for piece in pieces:
        row = piece.sides[2]
        piece.first = first[row : row + 4 * piece.rows]
        piece.second = second[row : row + 4 * piece.rows]
        piece.keep(first, 1, range(4), first=row, other=first_other)
        piece.keep(second, 2, range(4), first=row, other=second_other)
    for piece in fars:
        row = piece.far_sides[2]
        piece.keep(first, 3, (2, 3), first=row, other=first_other)
        piece.keep(second, 3, (0, 1), first=row, other=second_other)


class Spread:
    def __init__(self, move, own, *earlier):
        self.move = move
        self.own = after(own, *earlier) if earlier else own
        with jax.named_scope("spread"):
            self.sides = tuple(move.flip(self.own, bits) for bits in (1, 2, 3))

    def end(self, *earlier):
        with jax.named_scope("spread_swap"):
            here = jnp.concatenate(after((self.own, *self.sides), *earlier))
            self.all = [here, self.move.swap(here)]


class Sum:
    def __init__(self, move, arrays, name, levels=False):
        self.move = move
        self.arrays = arrays
        self.name = name
        self.levels = levels

    def across(self, *earlier):
        first, second = after(tuple(self.arrays[:2]), *earlier) if earlier else self.arrays[:2]
        with jax.named_scope(self.name + "_across"):
            self.first = self.move.flip(first, 1)
            self.second = self.move.flip(second, 2)
        return self.first, self.second

    def prepare(self, *earlier):
        self.first, self.second = after((self.first, self.second), *earlier)
        with jax.named_scope(self.name + "_onward"):
            self.rests = (
                low(wide(self.arrays[2]) + wide(self.second[2:])),
                low(wide(self.arrays[3]) + wide(self.first[2:])),
            )
        self.operands = self.rests
        return self.rests

    def onward(self, *earlier):
        rests = after(self.rests, *earlier) if earlier else self.rests
        with jax.named_scope(self.name + "_onward"):
            self.rests = (self.move.flip(rests[0], 1), self.move.flip(rests[1], 2))

    def gather(self, *earlier):
        rests = after(self.rests, *earlier) if earlier else self.rests
        with jax.named_scope(self.name + "_held"):
            held = self.arrays[4]
            self.near = wide(held[:2]) + wide(self.first[:2]) + wide(rests[1])
            self.far = wide(held[2:]) + wide(self.second[:2]) + wide(rests[0])
            if self.levels:
                held = jnp.concatenate([low(self.near), low(self.far)])
                self.held = held.reshape(-1, held.shape[-1])
                return self.held
            self.far = (self.far[0], low(self.far[1]))
            return self.far

    def finish(self, *earlier):
        with jax.named_scope(self.name + "_line"):
            if self.levels:
                lines = self.move.lines()
                owned = lax.psum_scatter(self.held, "dp", axis_index_groups=lines, scatter_dimension=0, tiled=True)
                self.owned = wide(owned)
            else:
                three = self.move.along(self.far[1])
                two = self.move.along(low(self.far[0] + wide(three)))
                two = after(two, *earlier) if earlier else two
                one = self.move.along(low(self.near[1] + wide(two)))
                self.passed = (three, two, one)
                self.owned = self.near[0] + wide(one)


class LineSum:
    def __init__(self, move, arrays, name):
        self.move = move
        self.arrays = arrays
        self.name = name
        self.next = arrays[0]

    def line(self, step, *earlier):
        value = after(self.next, *earlier) if earlier else self.next
        with jax.named_scope(f"{self.name}_line{step}"):
            self.sent = self.move.along(value)

    def prepare(self, step, *earlier):
        with jax.named_scope(f"{self.name}_line{step}"):
            sent = after(self.sent, *earlier) if earlier else self.sent
            self.next = low(wide(self.arrays[step]) + wide(sent))
        return self.next

    def prepare_across(self, *earlier):
        sent = after(self.sent, *earlier) if earlier else self.sent
        with jax.named_scope(self.name + "_across"):
            held = wide(self.arrays[3]) + wide(sent)
            half = held.shape[1] // 2
            self.near, self.rest = held[:, :half], held[:, half:]
            self.operands = (low(self.near[1::2]), low(self.rest[2:]))
        return self.operands

    def across(self, *earlier):
        operands = after(self.operands, *earlier) if earlier else self.operands
        with jax.named_scope(self.name + "_across"):
            self.first = self.move.flip(operands[0], 1)
            self.second = self.move.flip(operands[1], 2)

    def prepare_onward(self, *earlier):
        self.first, self.second = after((self.first, self.second), *earlier) if earlier else (self.first, self.second)
        with jax.named_scope(self.name + "_onward"):
            self.operands = (low(self.rest[1] + wide(self.second[1])), low(self.near[2] + wide(self.first[1])))
        return self.operands

    def finish(self, *earlier):
        operands = after(self.operands, *earlier) if earlier else self.operands
        with jax.named_scope(self.name + "_onward"):
            first_rest = self.move.flip(operands[0], 1)
            second_rest = self.move.flip(operands[1], 2)
            near = self.near[0] + wide(self.first[0]) + wide(second_rest)
            rest = self.rest[0] + wide(self.second[0]) + wide(first_rest)
            self.owned = jnp.concatenate([near, rest])


def whole_matrix(array):
    blocks = Blocks()
    blocks.add(array, None, 0, 0, None, 0, 0, 0, *array.shape)
    return blocks


def halves(move, owned, matrices):
    blocks = owned.reshape(matrices, 2, -1, owned.shape[-1])
    core = lax.axis_index("fsdp")
    mine = lax.dynamic_index_in_dim(blocks, core, 1, keepdims=False)
    return mine, move.swap(lax.dynamic_index_in_dim(blocks, 1 - core, 1, keepdims=False))


def local(
    move,
    features,
    grid_live,
    pos_embed,
    w_in,
    w_mid,
    w_out,
    norm_gain,
    norm_bias,
    readout_w,
    readout_b,
    cotangent,
):
    rows, middle_rows, width = w_in.shape[1], w_mid.shape[1], readout_w.shape[1]
    cells = pos_embed.shape[0]
    half_side = G // 2
    paired = move.paired
    scales = [norm_gain.reshape(6, rows).T, norm_bias.reshape(6, rows).T, readout_b.reshape(rows, 4)]
    beside = jnp.concatenate([pos_embed.T, *scales, jnp.zeros((rows, C - cells - MISC), jnp.bfloat16)], axis=1)
    if paired:
        cut = middle_rows // 2
        stacks = [
            [w_in[0], beside, w_out[0]],
            [w_mid[0, :cut]],
            [w_mid[0, cut:], w_in[1], w_out[1]],
            [w_mid[1]],
            [readout_w[:, i * C : (i + 1) * C] for i in range(width // C)],
        ]
        one, two, three, four, top = [
            Piece(move, jnp.concatenate(stack) if len(stack) > 1 else stack[0], name)
            for stack, name in zip(stacks, ("one", "two", "three", "four", "top"))
        ]
        top.plane_first()
        one.line((), top.sides)
        two.line(one.passed[1:2], one.passed[2:])
        three.line(two.passed[1:2], two.passed[2:])
        four.levels(three.passed[1])
        cross(move, [one], [], *top.fars)
        cross(move, [two], [one], one.first)
        one.settle_line(one.first)
        settle(move, [one], [], one.first)
        cross(move, [three], [two], two.first)
        two.settle_line(two.first)
        settle(move, [two], [one], two.first)
        top.pass_on(two.first)
        cross(move, [], [three], three.first)
        three.settle_line(three.first)
        settle(move, [three], [two], three.first)
        cross(move, [four], [], three.far_first, top.passed[1])
        top.pass_on(three.far_first)
        settle(move, [], [three], three.far_first)
        lies = {
            "head_0": [(one, 0, rows, 0, 0, C), (one, rows, rows, 0, C, HEAD - C)],
            "middle_0": [(two, 0, cut, 0, 0, C), (three, 0, cut, cut, 0, C)],
            "last_0": [(one, 2 * rows, rows, 0, 0, C)],
            "first_1": [(three, cut, rows, 0, 0, C)],
            "last_1": [(three, cut + rows, rows, 0, 0, C)],
            "middle_1": [(four, 0, middle_rows, 0, 0, C)],
            "readout": [(top, i * rows, rows, 0, i * C, C) for i in range(width // C)],
        }
    else:

        def whole(own):
            return lax.all_gather(own, ("dp", "fsdp"), axis=0, tiled=True)

        first_all = whole(w_in[0])
        lies = {
            "head_0": [(first_all, 0), (whole(beside[:, : HEAD - C]), C)],
            "middle_0": [(whole(w_mid[0]), 0)],
            "last_0": [(whole(w_out[0]), 0)],
            "first_1": [(whole(w_in[1]), 0)],
            "last_1": [(whole(w_out[1]), 0)],
            "middle_1": [(whole(w_mid[1]), 0)],
            "readout": [(whole(readout_w), 0)],
        }

    def matrix(name):
        blocks = Blocks()
        if not paired:
            for array, column in lies[name]:
                blocks.add(array, None, 0, 0, None, 0, 0, column, *array.shape)
            return blocks
        stride = middle_rows if name.startswith("middle") else rows
        for piece, row, extent, to_row, to_column, columns in lies[name]:
            for array, first, place in piece.found:
                blocks.add(array, None, first + row, 0, place, stride, to_row, to_column, extent, columns)
        return blocks

    def sums_of(columns, matrices, pieces=((None, STEPPED),)):
        blocks = Blocks()
        if not paired:
            extent = sum(matrices) * move.devices
            blocks.add(shaped(1, extent, columns), 0, 0, 0, None, 0, 0, 0, extent, columns)
            return blocks
        runs, start = [], 0
        for block_rows in matrices:
            runs.append((start, 2 * block_rows, 0))
            start += move.devices * block_rows
        for cut, kind in pieces:
            taken = []
            while runs and cut != 0:
                start, stride, first = runs.pop(0)
                extent = stride - first if cut is None else min(cut, stride - first)
                taken.append((start + first, stride, extent))
                if first + extent < stride:
                    runs.insert(0, (start, stride, first + extent))
                cut = None if cut is None else cut - extent
            place = {STEPPED: OUT_STEPS, LEVELED: OUT_LEVELS, LINED: OUT_LINE}[kind]
            for count in (4, 4, 4, 4) if kind == LINED else (4, 4, 2, 2, 4):
                array = shaped(count, sum(extent for _, _, extent in taken), columns)
                for block in range(count):
                    row = 0
                    for first, stride, extent in taken:
                        blocks.add(array, block, row, 0, place, stride, first, 0, extent, columns)
                        row += extent
                    place += 1
        return blocks

    def swap(value):
        return move.swap(value) if paired else None

    def tie(value, *earlier):
        return after(value, *earlier) if paired else value

    def scattered(terms, matrices=1):
        total = wide(terms[0][0]).reshape(matrices, -1, terms[0].shape[-1])
        return lax.psum_scatter(total, ("dp", "fsdp"), scatter_dimension=1, tiled=True)

    half = 2 if paired else 1
    table = move.table()
    mid_0, last_0 = matrix("middle_0"), matrix("last_0")
    misc, pooled, stream_in, lefts_0, pre1_0, pre2_0, pre3_0, first_0, last_0 = forward_block(
        table, 0, G, None, features[0], None, matrix("head_0"), mid_0, last_0
    )
    lefts_other_0 = swap(lefts_0)
    if paired:
        settle(move, [four], [], pooled)
        cross(move, [], [four])
        top.pass_on(pooled)
        four.settle_line(pooled)
        settle(move, [], [four])
    first_1, mid_1, last_1 = matrix("first_1"), matrix("middle_1"), matrix("last_1")
    lefts_1, pre1_1, pre2_1, pre3_1, first_1, last_1 = forward_block(
        table, 1, half_side, pooled, None, misc, first_1, mid_1, last_1
    )
    first_0, last_0, first_1, last_1 = [whole_matrix(array) for array in (first_0, last_0, first_1, last_1)]
    lefts_other_1 = swap(lefts_1)
    if paired:
        top.end_line(lefts_1)
    readout_bias = misc[12:].T.reshape(1, width)
    output, grad_top, grad_readout_b, grad_logits, grad_logits_other = readout(
        table, grid_live, tie(lefts_1, lefts_other_0), readout_bias, cotangent[0], matrix("readout")
    )
    if paired:
        acts = Spread(move, lefts_1[1])
        grad_logits_other = swap(after(grad_logits_other, *acts.sides))
        grad_top = after(grad_top, *acts.sides)
    else:
        grad_logits, grad_logits_other = jnp.concatenate([grad_logits, grad_logits_other], axis=1), None
    direct_1, grads_1, grads_other_1, sums_1 = back_last(
        table, 1, half_side, grad_top, pooled, pre3_1, pre2_1, misc, last_1
    )
    if paired:
        spread = Spread(move, grads_1[1], grad_logits_other)
        grads_other_1 = tie(grads_other_1, grad_logits_other)
    grads_other_1 = swap(grads_other_1)
    readout_terms = weight_terms(
        table,
        None,
        [(lefts_1, 3, lefts_other_1, tie(grad_logits, sums_1), None, grad_logits_other, None)],
        [],
        sums_of(width // half, [rows], [(None, LEVELED)]),
    )
    if paired:
        sum_readout = Sum(move, readout_terms, "readout", levels=True)
        spread.sides = after(spread.sides, *readout_terms)
        sum_readout.across(grads_other_1, *spread.sides)
        grads_1 = tie(grads_1, *readout_terms, *spread.sides)
    else:
        middle_terms_1 = weight_terms(
            table,
            (half_side, lefts_1, lefts_other_1, grads_1, grads_other_1),
            [],
            [],
            sums_of(C // half, [middle_rows]),
        )
    grad_pooled, sums_first_1, grad_first_1, grad_first_other_1 = back_first(
        table, 1, half_side, grads_1, pre1_1, direct_1, misc, None, mid_1, first_1
    )
    direct_0, grads_0, grads_other_0, sums_0 = back_last(
        table, 0, G, grad_pooled, stream_in, pre3_0, pre2_0, misc, last_0
    )
    if paired:
        waited = [*sum_readout.prepare(sums_0), *after(spread.sides, sums_0)]
        lefts_other_0 = tie(lefts_other_0, *waited)
        grads_other_0, grad_first_other_1 = after((grads_other_0, grad_first_other_1), *waited)
        spread.end(*waited)
        acts.end(*waited)
        sum_readout.onward(*waited)
    grads_other_0, grad_first_other_1 = swap(grads_other_0), swap(grad_first_other_1)
    crossed_terms = weight_terms(
        table,
        (G, lefts_0, lefts_other_0, grads_0, grads_other_0),
        [],
        [],
        sums_of(C // half, [middle_rows]),
    )
    if paired:
        sum_middle_0 = Sum(move, crossed_terms, "middle_0")
        waited = [sum_readout.gather(*crossed_terms), *after((*spread.all, *acts.all), *crossed_terms)]
        sum_readout.finish()
        sum_middle_0.across(*waited)
        acts.all[0] = tie(acts.all[0], *waited)
        middle_terms_1 = plane_terms(table, half_side, acts.all, spread.all, middle_rows)
        grads_0 = tie(grads_0, middle_terms_1, *waited)
    rests = [sums_0, sums_first_1, sums_1, grad_readout_b.reshape(C, 4).T]
    grad_in, _, grad_first_0, grad_first_other_0, side, side_other = back_first(
        table, 0, G, grads_0, pre1_0, direct_0, misc, rests, mid_0, first_0
    )
    if paired:
        waited = [*sum_middle_0.prepare(grad_in)]
        grad_first_other_0, side_other = after((grad_first_other_0, side_other), *waited)
        side_other = swap(side_other)
        sides = [(side, side_other)]
        sum_middle_0.onward(*waited)
        with jax.named_scope("middle_1_levels"):
            owned_1 = lax.psum_scatter(
                after(middle_terms_1, *waited).reshape(-1, C),
                "dp",
                axis_index_groups=move.lines(),
                scatter_dimension=0,
                tiled=True,
            )
        lefts_other_0 = tie(lefts_other_0, *waited)
    else:
        sides = [(side, None), (side_other, None)]
    grad_first_other_0 = swap(grad_first_other_0)
    last_terms = weight_terms(
        table,
        None,
        [
            (lefts_0, 2, lefts_other_0, grads_0, 0, grads_other_0, 0),
            (lefts_1, 0, lefts_other_1, grad_first_1, 0, grad_first_other_1, None),
            (lefts_1, 2, lefts_other_1, grads_1, 0, grads_other_1, 0),
            (lefts_0, 0, lefts_other_0, grad_first_0, 0, grad_first_other_0, None),
        ],
        sides,
        sums_of(C // half, [rows] * 5),
    )
    if paired:
        sum_last = Sum(move, last_terms, "last")
        waited = sum_middle_0.gather(*last_terms)
        sum_last.across(*waited)
        sum_middle_0.finish()
        core = jnp.reshape(lax.axis_index("fsdp"), (1,))
        readout_owned = place_halves(core, halves(move, sum_readout.owned, 1))[0].reshape(rows, width)
        sum_last.prepare(readout_owned)
        sum_last.onward()
        sum_last.gather()
        middle_owned = place_halves(core, halves(move, sum_middle_0.owned, 1), owned_1[None])
        sum_last.finish(middle_owned)
        first_grad, last_grad, pos_grad, gain_grad, bias_grad, readout_grad = place_last(core, *halves(move, sum_last.owned, 5), cells)
        readout_grad = readout_grad.T
    else:
        readout_owned = scattered(readout_terms)[0]
        middle_owned = jnp.concatenate([scattered(terms) for terms in (crossed_terms, middle_terms_1)])
        last_owned = scattered(last_terms, 5)
        first_grad, last_grad = jnp.stack([last_owned[3], last_owned[1]]), jnp.stack([last_owned[0], last_owned[2]])
        pos_grad = last_owned[4, :, :cells].T
        scales = last_owned[4, :, cells : cells + MISC]
        gain_grad, bias_grad = scales[:, 0:6].T.reshape(2, 3, rows), scales[:, 6:12].T.reshape(2, 3, rows)
        readout_grad = scales[:, 12:]
    return (
        output[None],
        grad_in[None],
        pos_grad,
        first_grad,
        middle_owned,
        last_grad,
        gain_grad,
        bias_grad,
        readout_owned,
        readout_grad.reshape(-1),
    )


def solution(mesh):
    return jax.shard_map(
        functools.partial(local, Movement(mesh)),
        mesh=mesh,
        in_specs=(
            P(("dp", "fsdp"), None, None),
            P(("dp", "fsdp")),
            P(None, ("dp", "fsdp")),
            P(None, ("dp", "fsdp"), None),
            P(None, ("dp", "fsdp"), None),
            P(None, ("dp", "fsdp"), None),
            P(None, None, ("dp", "fsdp")),
            P(None, None, ("dp", "fsdp")),
            P(("dp", "fsdp"), None),
            P(("dp", "fsdp")),
            P(("dp", "fsdp"), None, None),
        ),
        out_specs=(
            P(("dp", "fsdp"), None, None),
            P(("dp", "fsdp"), None, None),
            P(None, ("dp", "fsdp")),
            P(None, ("dp", "fsdp"), None),
            P(None, ("dp", "fsdp"), None),
            P(None, ("dp", "fsdp"), None),
            P(None, None, ("dp", "fsdp")),
            P(None, None, ("dp", "fsdp")),
            P(("dp", "fsdp"), None),
            P(("dp", "fsdp")),
        ),
        check_vma=False,
    )
```

```python
import functools

import jax
import jax.numpy as jnp
import numpy as np
from jax import lax
from jax.experimental import pallas as pl
from jax.experimental.pallas import tpu as pltpu
from jax.sharding import PartitionSpec as P

C = 1024
G = 24
PLANE = 4
TILE = 256
ROWS = 144
PAD = 24
MISC = 16
HEAD = 1664
SIDE = 384
STEPS, LEVELS, OUT_STEPS, OUT_LEVELS, OUT_LINE, CORE, WINDOWS, TABLE = 0, 32, 64, 80, 96, 112, 113, 165
STEPPED, LEVELED, LINED = range(3)
COST = 4
COSTS = {"forward_block": 50}
VMEM = 60 * 1024 * 1024


def low(value):
    return value.astype(jnp.bfloat16)


def wide(value):
    return value.astype(jnp.float32)


def dot(left, right):
    return jnp.dot(left, right, preferred_element_type=jnp.float32)


def dot_rows(left, right):
    return lax.dot_general(left, right, (((1,), (1,)), ((), ())), preferred_element_type=jnp.float32)


def dot_sums(left, right):
    return lax.dot_general(left, right, (((0,), (0,)), ((), ())), preferred_element_type=jnp.float32)


def sigmoid(value):
    return 1.0 / (1.0 + jnp.exp(-value))


def centered(value):
    center = value - jnp.mean(value, axis=-1, keepdims=True)
    spread = jnp.mean(center * center, axis=-1, keepdims=True)
    scale = lax.rsqrt(spread + 1e-05)
    return center * scale, scale


def norm_back(grad, normal, scale, gain):
    inner = grad * gain
    first = jnp.mean(inner, axis=-1, keepdims=True)
    second = jnp.mean(inner * normal, axis=-1, keepdims=True)
    return scale * (inner - first - normal * second)


def silu_back(value):
    gate = sigmoid(value)
    return gate * (1.0 + value * (1.0 - gate))


def tiles(extent, size, body):
    def step(i, carry):
        body(pl.ds(pl.multiple_of(i * size, size), size))
        return carry

    lax.fori_loop(0, extent // size, step, 0)


def fold(value):
    return jnp.sum(value.reshape(-1, 8, value.shape[-1]), axis=0)


def columns_of(cells, side, lanes):
    index = lax.broadcasted_iota(jnp.int32, (cells, lanes), 0).astype(jnp.float32)
    return index - side * jnp.floor((index + 0.5) * (1.0 / side))


def beside(value, side, step):
    cells = value.shape[0]
    column = columns_of(cells, side, value.shape[1])
    inside = column < side - 1 if step > 0 else column > 0
    return jnp.where(inside, pltpu.roll(value, (cells - step) % cells, 0), 0.0)


class Blocks:
    def __init__(self):
        self.operands = []
        self.moves = []

    def operand(self, array):
        for number, known in enumerate(self.operands):
            if known is array:
                return number
        self.operands.append(array)
        return len(self.operands) - 1

    def add(self, array, block, row, column, place, stride, to_row, to_column, rows, columns):
        self.moves.append((self.operand(array), block, row, column, place, stride, to_row, to_column, rows, columns))

    @property
    def copies(self):
        return len(self.moves)

    def bind(self, refs, places, matrix, sems, to_blocks=False, base=0):
        made = []
        for number, block, row, column, place, stride, to_row, to_column, rows, columns in self.moves:
            first = to_row
            if place is not None:
                first = pl.multiple_of(places[place] * stride + to_row, 16)
            inside = matrix.at[pl.ds(first, rows), pl.ds(to_column, columns)]
            outside = refs[number] if block is None else refs[number].at[block]
            outside = outside.at[pl.ds(row, rows), pl.ds(column, columns)]
            pair = (inside, outside) if to_blocks else (outside, inside)
            made.append(pltpu.make_async_copy(*pair, sems.at[base + len(made)]))
        return made


def start(copies):
    for copy in copies:
        copy.start()


def wait(copies):
    for copy in copies:
        copy.wait()


ANY = pl.BlockSpec(memory_space=pltpu.HBM)
IN = pl.BlockSpec(memory_space=pltpu.VMEM)
SMEM = pl.BlockSpec(memory_space=pltpu.SMEM)


def call(kernel, name, ins, in_specs, outs, out_specs, scratch, flops, moved):
    short = COSTS.get(name, COST)
    return pl.pallas_call(
        kernel,
        name=name,
        out_shape=outs,
        in_specs=in_specs,
        out_specs=out_specs,
        scratch_shapes=scratch,
        compiler_params=pltpu.CompilerParams(vmem_limit_bytes=VMEM),
        cost_estimate=pl.CostEstimate(flops=int(flops) // short, bytes_accessed=int(moved) // short, transcendentals=0),
    )(*ins)


class Traffic:
    def __init__(self, sems):
        self.sems = sems
        self.used = 0
        self.sent = []

    def begin(self, source, target):
        copy = pltpu.make_async_copy(source, target, self.sems.at[self.used])
        self.used += 1
        copy.start()
        return copy

    def send(self, source, target):
        self.sent.append(self.begin(source, target))

    def load(self, blocks, refs, places, matrix):
        copies = blocks.bind(refs, places, matrix, self.sems, base=self.used)
        self.used += len(copies)
        start(copies)
        return copies

    def store(self, blocks, refs, places, matrix):
        copies = blocks.bind(refs, places, matrix, self.sems, to_blocks=True, base=self.used)
        self.used += len(copies)
        start(copies)
        self.sent += copies

    def finish(self):
        wait(self.sent)


def shaped(*shape, dtype=jnp.float32):
    return jax.ShapeDtypeStruct(shape, dtype)


def forward_block(table, number, side, stream, features, misc, w_first, w_middle, w_last):
    cells = side * side
    opening = features is not None
    n_first, n_middle, n_last = len(w_first.operands), len(w_middle.operands), len(w_last.operands)
    given = [features] if opening else [stream, misc]
    given_count = len(given)
    bf16 = jnp.bfloat16
    n_lefts = 3 if opening else 4

    def kernel(table_ref, *refs):
        refs = list(refs)
        heads = [refs.pop(0) for _ in range(given_count)]
        firsts = [refs.pop(0) for _ in range(n_first)]
        middles = [refs.pop(0) for _ in range(n_middle)]
        lasts = [refs.pop(0) for _ in range(n_last)]
        if opening:
            misc_ref, pooled_ref, u_out = refs.pop(0), refs.pop(0), refs.pop(0)
            u_ref = refs.pop(0 - 1)
        else:
            u_ref, misc_ref = heads
        lefts_out, pre1_out, pre2_out, pre3_out, wi_out, wo_out = [refs.pop(0) for _ in range(6)]
        wi, wm, wo, taps, lefts, above, below, work, pairs, pre1, pre2, pre3, sems = refs
        traffic = Traffic(sems)
        first_copies = traffic.load(w_first, firsts, table_ref, wi)
        middle_copies = traffic.load(w_middle, middles, table_ref, wm)
        last_copies = traffic.load(w_last, lasts, table_ref, wo)
        wait(first_copies)
        traffic.send(wi.at[:, pl.ds(0, C)], wi_out)
        if opening:

            def place(cut):
                turned = jnp.transpose(wide(wi[cut, C:HEAD]))
                u_ref[:, cut] = wide(heads[0][:, cut]) + turned[:cells]
                misc_ref[:, cut] = turned[cells : cells + MISC]

            tiles(C, 128, place)
            traffic.send(u_ref, u_out)

        def lower(rows):
            lefts[0, rows, :] = low(u_ref[rows, :])

        tiles(cells, ROWS, lower)

        def first(cut):
            pre1[:, cut] = dot(lefts[0], wi[:, cut])

        tiles(C, TILE, first)
        traffic.send(pre1, pre1_out)

        def norm_act(source, norm, store):
            gain = misc_ref[3 * number + norm : 3 * number + norm + 1, :]
            bias = misc_ref[6 + 3 * number + norm : 7 + 3 * number + norm, :]

            def rows_of(rows):
                normal, _ = centered(source[rows, :])
                hidden = normal * gain + bias
                store(rows, hidden * sigmoid(hidden))

            tiles(cells, ROWS, rows_of)

        def keep_first(rows, value):
            work[rows, :] = value
            lefts[1, rows, :] = low(value)

        norm_act(pre1, 0, keep_first)

        def spread(i, carry):
            cut = pl.ds(pl.multiple_of(i * 128, 128), 128)
            value = work[:, cut]
            taps[:, pl.ds(pl.multiple_of(i * 128, 128), 128)] = low(beside(value, side, -1))
            taps[:, pl.ds(pl.multiple_of(C + i * 128, 128), 128)] = low(value)
            taps[:, pl.ds(pl.multiple_of(2 * C + i * 128, 128), 128)] = low(beside(value, side, 1))
            return carry

        lax.fori_loop(0, C // 128, spread, 0)
        zeros = jnp.zeros((PAD, TILE), jnp.float32)
        for ref in (above, below):
            ref[:PAD, :] = zeros
            ref[PAD + cells :, :] = zeros
        wait(middle_copies)

        def middle(cut):
            above[PAD : PAD + cells, :] = dot(taps[...], wm[0 : 3 * C, cut])
            below[PAD : PAD + cells, :] = dot(taps[...], wm[6 * C : 9 * C, cut])
            same = dot(taps[...], wm[3 * C : 6 * C, cut])
            pre2[:, cut] = same + above[PAD - side : PAD - side + cells, :] + below[PAD + side : PAD + side + cells, :]

        tiles(C, TILE, middle)
        traffic.send(pre2, pre2_out)

        def keep_second(rows, value):
            lefts[2, rows, :] = low(value)

        norm_act(pre2, 1, keep_second)
        if opening:
            traffic.send(lefts, lefts_out)
        wait(last_copies)
        traffic.send(wo, wo_out)

        def last(cut):
            pre3[:, cut] = dot(lefts[2], wo[:, cut])

        tiles(C, TILE, last)
        traffic.send(pre3, pre3_out)
        gain = misc_ref[3 * number + 2 : 3 * number + 3, :]
        bias = misc_ref[8 + 3 * number : 9 + 3 * number, :]

        def close(rows):
            normal, _ = centered(pre3[rows, :])
            total = u_ref[rows, :] + (normal * gain + bias)
            value = total * sigmoid(total)
            if opening:
                work[rows, :] = value
            else:
                lefts[3, rows, :] = low(value)

        tiles(cells, ROWS, close)
        if opening:
            half = side // 2

            def pool(cut):
                value = work[:, cut].reshape(half, 2, side, 128)
                pairs[...] = (value[:, 0] + value[:, 1]).reshape(half * side, 128)
                pooled_ref[:, cut] = 0.25 * (
                    pairs[pl.ds(0, half * half, 2), :] + pairs[pl.ds(1, half * half, 2), :]
                )

            tiles(C, 128, pool)
        else:
            traffic.send(lefts, lefts_out)
        traffic.finish()

    outs, out_specs = [], []
    if opening:
        outs += [shaped(MISC, C), shaped(cells // 4, C), shaped(cells, C)]
        out_specs += [IN, IN, ANY]
    outs += [shaped(n_lefts, cells, C, dtype=bf16)] + [shaped(cells, C)] * 3 + [shaped(C, C, dtype=bf16)] * 2
    out_specs += [ANY] * 6
    copies = w_first.copies + w_middle.copies + w_last.copies + 7
    scratch = [
        pltpu.VMEM((C, HEAD if opening else C), bf16),
        pltpu.VMEM((9 * C, C), bf16),
        pltpu.VMEM((C, C), bf16),
        pltpu.VMEM((cells, 3 * C), bf16),
        pltpu.VMEM((n_lefts, cells, C), bf16),
        pltpu.VMEM((cells + 2 * PAD, TILE), jnp.float32),
        pltpu.VMEM((cells + 2 * PAD, TILE), jnp.float32),
        pltpu.VMEM((cells, C), jnp.float32),
        pltpu.VMEM((cells // 2, 128), jnp.float32),
        pltpu.VMEM((cells, C), jnp.float32),
        pltpu.VMEM((cells, C), jnp.float32),
        pltpu.VMEM((cells, C), jnp.float32),
        pltpu.SemaphoreType.DMA((copies,)),
    ]
    if opening:
        scratch.append(pltpu.VMEM((cells, C), jnp.float32))
    weights = w_first.operands + w_middle.operands + w_last.operands
    return call(
        kernel,
        "forward_block",
        [table] + given + weights,
        [SMEM] + [IN] * given_count + [ANY] * len(weights),
        outs,
        out_specs,
        scratch,
        2 * cells * 11 * C * C,
        22 * C * C + 20 * cells * C,
    )


def readout(table, live, lefts, bias, cotangent, weights):
    cells, columns = cotangent.shape
    n_weights = len(weights.operands)
    bf16 = jnp.bfloat16
    cut_size = 512
    half = columns // 2

    def kernel(table_ref, live_ref, lefts_ref, bias_ref, cot_ref, *refs):
        refs = list(refs)
        sources = [refs.pop(0) for _ in range(n_weights)]
        output, grad_stream, grad_bias, own, other, matrix, low_ref, sems = refs
        traffic = Traffic(sems)
        given = traffic.begin(lefts_ref.at[3], low_ref)
        copies = traffic.load(weights, sources, table_ref, matrix)
        factor = wide(live_ref[0])
        core = table_ref[CORE]
        grad_stream[...] = jnp.zeros((cells, C), jnp.float32)
        given.wait()
        wait(copies)
        for part in range(2):

            def step(cut, part=part):
                here = pl.ds(pl.multiple_of(part * half + cut.start, cut_size), cut_size)
                logits = dot(low_ref[...], matrix[:, here]) + bias_ref[:, here]
                share = 0.5 * (1.0 + lax.erf(logits * (0.5**0.5)))
                output[:, here] = low(logits * share * factor)
                slope = share + logits * (jnp.exp(-0.5 * logits * logits) * (0.5 / jnp.pi) ** 0.5)
                grad_logits = low(wide(cot_ref[:, here]) * factor * slope)
                grad_bias[:, here] = jnp.sum(wide(grad_logits), axis=0, keepdims=True)

                @pl.when(core == part)
                def _():
                    own[:, cut] = grad_logits

                @pl.when(core != part)
                def _():
                    other[:, cut] = grad_logits

                grad_stream[...] += dot_rows(grad_logits, matrix[:, here])

            tiles(half, cut_size, step)

    outs = [shaped(cells, columns, dtype=bf16), shaped(cells, C), shaped(1, columns)]
    outs += [shaped(cells, half, dtype=bf16)] * 2
    scratch = [
        pltpu.VMEM((C, columns), bf16),
        pltpu.VMEM((cells, C), bf16),
        pltpu.SemaphoreType.DMA((weights.copies + 1,)),
    ]
    return call(
        kernel,
        "readout",
        [table, live, lefts, bias, cotangent] + weights.operands,
        [SMEM] * 2 + [ANY] + [IN] * 2 + [ANY] * n_weights,
        outs,
        [IN] * 5,
        scratch,
        4 * cells * C * columns,
        2 * C * columns + 4 * cells * columns,
    )


def back_last(table, number, side, grad_out, stream, pre3, pre2, misc, w_last):
    cells = side * side
    pooled = grad_out.shape[0] != cells
    n_weights = len(w_last.operands)
    bf16 = jnp.bfloat16
    half = C // 2

    def kernel(table_ref, grad_ref, u_in, pre3_in, pre2_in, misc_ref, *refs):
        refs = list(refs)
        sources = [refs.pop(0) for _ in range(n_weights)]
        direct_out, grads, other, sums, matrix, direct, u_ref, pre3_ref, pre2_ref, work, parts, pairs, sems = refs
        traffic = Traffic(sems)
        opened = [traffic.begin(u_in, u_ref), traffic.begin(pre3_in, pre3_ref)]
        later = traffic.begin(pre2_in, pre2_ref)
        copies = traffic.load(w_last, sources, table_ref, matrix)
        parts[...] = jnp.zeros_like(parts)
        gain = misc_ref[3 * number + 2 : 3 * number + 3, :]
        bias = misc_ref[8 + 3 * number : 9 + 3 * number, :]
        if pooled:

            def spread(cut):
                value = 0.25 * grad_ref[:, cut]
                pairs[pl.ds(0, cells // 4, 2), :] = value
                pairs[pl.ds(1, cells // 4, 2), :] = value
                twice = pairs[...].reshape(side // 2, 1, side, 128)
                work[:, cut] = jnp.broadcast_to(twice, (side // 2, 2, side, 128)).reshape(cells, 128)

            tiles(C, 128, spread)
        grad_from = work if pooled else grad_ref
        wait(opened)

        def close(rows):
            normal, scale = centered(pre3_ref[rows, :])
            total = u_ref[rows, :] + (normal * gain + bias)
            inner = grad_from[rows, :] * silu_back(total)
            direct[rows, :] = inner
            parts[0:8, :] += fold(inner * normal)
            parts[8:16, :] += fold(inner)
            grads[0, rows, :] = low(norm_back(inner, normal, scale, gain))

        tiles(cells, ROWS, close)
        traffic.send(direct, direct_out)
        gain = misc_ref[3 * number + 1 : 3 * number + 2, :]
        bias = misc_ref[7 + 3 * number : 8 + 3 * number, :]
        wait(copies)

        def last(cut):
            work[:, cut] = dot_rows(grads[0], matrix[cut, :])

        tiles(C, TILE, last)
        later.wait()

        def norm(rows):
            normal, scale = centered(pre2_ref[rows, :])
            hidden = normal * gain + bias
            inner = work[rows, :] * silu_back(hidden)
            parts[16:24, :] += fold(inner * normal)
            parts[24:32, :] += fold(inner)
            grads[1, rows, :] = low(norm_back(inner, normal, scale, gain))

        tiles(cells, ROWS, norm)
        sums[...] = jnp.sum(parts[...].reshape(4, 8, C), axis=1)
        there = pl.ds(pl.multiple_of((1 - table_ref[CORE]) * half, half), half)
        for i in range(2):
            other[i] = grads[i, :, there]
        traffic.finish()

    outs = [shaped(cells, C), shaped(2, cells, C, dtype=bf16), shaped(2, cells, half, dtype=bf16), shaped(4, C)]
    f32 = jnp.float32
    scratch = [pltpu.VMEM((C, C), bf16)] + [pltpu.VMEM((cells, C), f32)] * 5
    scratch += [pltpu.VMEM((32, C), f32), pltpu.VMEM((cells // 2, 128), f32), pltpu.SemaphoreType.DMA((w_last.copies + 4,))]
    return call(
        kernel,
        "back_last",
        [table, grad_out, stream, pre3, pre2, misc] + w_last.operands,
        [SMEM, IN, ANY, ANY, ANY, IN] + [ANY] * n_weights,
        outs,
        [ANY, IN, IN, IN],
        scratch,
        2 * cells * C * C,
        2 * C * C + 24 * cells * C,
    )


def weight_terms(table, middle, products, sides, out_blocks):
    bf16 = jnp.bfloat16
    if middle is not None:
        products = [(middle[1], 1, middle[2], middle[3], 1, middle[4], 1)] + products
    pair = products[0][2] is not None
    given = []
    for left, _, left_other, right, _, right_other, _ in products:
        given += [left, right] + ([left_other, right_other] if pair else [])
    n_given = len(given)
    n_outs = len(out_blocks.operands)
    width = out_blocks.operands[0].shape[-1]
    cells_of = [product[0].shape[-2] for product in products]
    factor = 2 if pair else 1
    heights = [C] * len(products)
    if middle is not None:
        heights[0] = 9 * C
    starts = [sum(heights[:i]) for i in range(len(heights) + 1)]
    grid_side = middle[0] if middle is not None else 0
    grid_cells = grid_side * grid_side
    size = 512

    def kernel(table_ref, *refs):
        refs = list(refs)
        sources = [refs.pop(0) for _ in range(n_given)]
        beside_refs = [refs.pop(0) for _ in range(len(sides) * factor)]
        targets = [refs.pop(0) for _ in range(n_outs)]
        grad, sems = refs.pop(0), refs.pop(0)
        traffic = Traffic(sems)
        waits = []
        for (_, left_at, _, _, right_at, _, other_at), cells in zip(products, cells_of):
            left, right = refs.pop(0), refs.pop(0)
            left_in, right_in = sources.pop(0), sources.pop(0)
            copies = [traffic.begin(left_in.at[left_at], left.at[pl.ds(0, cells), :])]
            if right_at is not None:
                right_in = right_in.at[right_at]
                if pair:
                    right_in = right_in.at[:, pl.ds(pl.multiple_of(table_ref[CORE] * width, width), width)]
            copies.append(traffic.begin(right_in, right.at[pl.ds(0, cells), :]))
            if pair:
                left_in, right_in = sources.pop(0), sources.pop(0)
                copies.append(traffic.begin(left_in.at[left_at], left.at[pl.ds(cells, cells), :]))
                if other_at is not None:
                    right_in = right_in.at[other_at]
                copies.append(traffic.begin(right_in, right.at[pl.ds(cells, cells), :]))
            waits.append((copies, left, right))
        at = 0
        for side in sides:
            extent = side[0].shape[-1]
            total = beside_refs.pop(0)[...]
            if pair:
                total = low(wide(total) + wide(beside_refs.pop(0)[...]))
            grad[starts[-1] :, at : at + extent] = total
            at += extent
        if sides:
            grad[starts[-1] :, at:] = jnp.zeros((C, width - at), bf16)
        if middle is not None:
            taps, shifted, padded = refs
            copies, act, right = waits[0]
            padded[:PAD, :] = jnp.zeros((PAD, 128), jnp.float32)
            padded[PAD + grid_cells :, :] = jnp.zeros((PAD, 128), jnp.float32)
            wait(copies)
            for first in range(0, factor * grid_cells, grid_cells):
                rows = slice(first, first + grid_cells)

                def spread(i, carry, rows=rows):
                    cut = pl.ds(pl.multiple_of(i * 128, 128), 128)
                    value = wide(act[rows, cut])
                    taps[rows, cut] = low(beside(value, grid_side, -1))
                    taps[rows, pl.ds(pl.multiple_of(C + i * 128, 128), 128)] = act[rows, cut]
                    taps[rows, pl.ds(pl.multiple_of(2 * C + i * 128, 128), 128)] = low(beside(value, grid_side, 1))
                    return carry

                def shift(i, carry, rows=rows):
                    cut = pl.ds(pl.multiple_of(i * 128, 128), 128)
                    padded[PAD : PAD + grid_cells, :] = wide(right[rows, cut])
                    shifted[0, rows, cut] = low(padded[PAD + grid_side : PAD + grid_side + grid_cells, :])
                    shifted[1, rows, cut] = right[rows, cut]
                    shifted[2, rows, cut] = low(padded[PAD - grid_side : PAD - grid_side + grid_cells, :])
                    return carry

                lax.fori_loop(0, C // 128, spread, 0)
                lax.fori_loop(0, width // 128, shift, 0)
            def part(i, carry):
                cut = pl.ds(pl.multiple_of(lax.rem(i, 3 * C // size) * size, size), size)
                target = pl.ds(pl.multiple_of(i * size, size), size)
                grad[target, :] = low(dot_sums(taps[:, cut], shifted[i // (3 * C // size)]))
                return carry

            lax.fori_loop(0, 9 * C // size, part, 0)
        for number, (copies, left, right) in enumerate(waits):
            if middle is not None and number == 0:
                continue
            wait(copies)

            def part(cut, number=number, left=left, right=right):
                target = pl.ds(pl.multiple_of(starts[number] + cut.start, TILE), TILE)
                grad[target, :] = low(dot_sums(left[:, cut], right[...]))

            tiles(C, TILE, part)
        traffic.store(out_blocks, targets, table_ref, grad)
        traffic.finish()

    outs = [shaped(*array.shape, dtype=bf16) for array in out_blocks.operands]
    scratch = [
        pltpu.VMEM((starts[-1] + (C if sides else 0), width), bf16),
        pltpu.SemaphoreType.DMA((out_blocks.copies + 4 * len(products),)),
    ]
    for cells in cells_of:
        scratch += [pltpu.VMEM((factor * cells, C), bf16), pltpu.VMEM((factor * cells, width), bf16)]
    if middle is not None:
        scratch += [
            pltpu.VMEM((factor * grid_cells, 3 * C), bf16),
            pltpu.VMEM((3, factor * grid_cells, width), bf16),
            pltpu.VMEM((grid_cells + 2 * PAD, 128), jnp.float32),
        ]
    besides = [array for side in sides for array in side if array is not None]
    return call(
        kernel,
        "weight_terms",
        [table] + given + besides,
        [SMEM] + [ANY] * n_given + [IN] * len(besides),
        outs,
        [ANY] * n_outs,
        scratch,
        sum(2 * factor * cells * height * width for cells, height in zip(cells_of, heights)),
        2 * starts[-1] * width + sum(4 * factor * cells * C for cells in cells_of),
    )


def plane_terms(table, side, acts, grads, block_rows):
    cells = side * side
    total = sum(array.shape[0] for array in acts)
    bf16 = jnp.bfloat16
    blocks = 4
    span = 3 * 128

    def kernel(table_ref, *refs):
        refs = list(refs)
        act_refs = [refs.pop(0) for _ in acts]
        grad_refs = [refs.pop(0) for _ in grads]
        target, act, right, taps, terms, sems = refs
        traffic = Traffic(sems)
        copies, row = [], 0
        for source, other in zip(act_refs, grad_refs):
            rows = pl.ds(row, source.shape[0])
            copies += [traffic.begin(source, act.at[rows, :]), traffic.begin(other, right.at[rows, :])]
            row += source.shape[0]
        index = lax.broadcasted_iota(jnp.int32, (total, 128), 0).astype(jnp.float32)
        inside = index - cells * jnp.floor((index + 0.5) * (1.0 / cells))
        line = jnp.floor((inside + 0.5) * (1.0 / side))
        column = inside - side * line
        wait(copies)
        for block in range(blocks):
            for tile in range(3):
                at = WINDOWS + blocks + 4 * (3 * block + tile)
                cut = pl.ds(pl.multiple_of(table_ref[at], 128), 128)
                value = pltpu.roll(wide(act[:, cut]), table_ref[at + 1], 0)
                tap_line = line + (table_ref[at + 2] - 1).astype(jnp.float32)
                tap_column = column + (table_ref[at + 3] - 1).astype(jnp.float32)
                there = (tap_line >= 0) & (tap_line < side) & (tap_column >= 0) & (tap_column < side)
                first = block * span + tile * 128
                taps[:, first : first + 128] = low(jnp.where(there, value, 0.0))
            terms[block] = low(dot_sums(taps[:, block * span : (block + 1) * span], right[...]))
            start_row = pl.multiple_of(table_ref[WINDOWS + block], 32)
            traffic.send(terms.at[block, pl.ds(start_row, block_rows), :], target.at[block])
        traffic.finish()

    return call(
        kernel,
        "plane_terms",
        [table] + acts + grads,
        [SMEM] + [ANY] * (2 * len(acts)),
        shaped(blocks, block_rows, C, dtype=bf16),
        ANY,
        [
            pltpu.VMEM((total, C), bf16),
            pltpu.VMEM((total, C), bf16),
            pltpu.VMEM((total, blocks * span), bf16),
            pltpu.VMEM((blocks, span, C), bf16),
            pltpu.SemaphoreType.DMA((2 * len(acts) + blocks,)),
        ],
        2 * total * blocks * span * C,
        4 * total * C + 2 * blocks * block_rows * C,
    )


def back_first(table, number, side, grads, pre1, direct, misc, rests, w_middle, w_first):
    cells = side * side
    closing = rests is not None
    n_middle, n_first = len(w_middle.operands), len(w_first.operands)
    bf16 = jnp.bfloat16
    extra = rests if closing else []
    half = C // 2
    side_half = SIDE

    def kernel(table_ref, grads_in, pre1_in, direct_in, misc_ref, *refs):
        refs = list(refs)
        rest_refs = [refs.pop(0) for _ in extra]
        middles = [refs.pop(0) for _ in range(n_middle)]
        firsts = [refs.pop(0) for _ in range(n_first)]
        grad_u, sums, grad_pre1, other = [refs.pop(0) for _ in range(4)]
        turned = [refs.pop(0), refs.pop(0)] if closing else None
        wm, wi, grad_ref, pre1_ref, direct_ref, taps, above, below, work, parts, sems = refs
        traffic = Traffic(sems)
        given = traffic.begin(grads_in.at[1], grad_ref)
        middle_copies = traffic.load(w_middle, middles, table_ref, wm)
        pre1_copy = traffic.begin(pre1_in, pre1_ref)
        first_copies = traffic.load(w_first, firsts, table_ref, wi)
        direct_copy = traffic.begin(direct_in, direct_ref)
        parts[...] = jnp.zeros_like(parts)
        zeros = jnp.zeros((PAD, TILE), jnp.float32)
        for ref in (above, below):
            ref[:PAD, :] = zeros
            ref[PAD + cells :, :] = zeros
        given.wait()

        def spread(i, carry):
            cut = pl.ds(pl.multiple_of(i * 128, 128), 128)
            value = wide(grad_ref[:, cut])
            taps[:, cut] = low(beside(value, side, 1))
            taps[:, pl.ds(pl.multiple_of(C + i * 128, 128), 128)] = grad_ref[:, cut]
            taps[:, pl.ds(pl.multiple_of(2 * C + i * 128, 128), 128)] = low(beside(value, side, -1))
            return carry

        lax.fori_loop(0, C // 128, spread, 0)
        wait(middle_copies)

        def middle(i, carry):
            def row(tap):
                total = None
                for column in range(3):
                    source = pl.ds(pl.multiple_of((3 * tap + column) * C + i * TILE, TILE), TILE)
                    term = dot_rows(taps[:, column * C : (column + 1) * C], wm[source, :])
                    total = term if total is None else total + term
                return total

            above[PAD : PAD + cells, :] = row(0)
            below[PAD : PAD + cells, :] = row(2)
            cut = pl.ds(pl.multiple_of(i * TILE, TILE), TILE)
            work[:, cut] = (
                row(1) + above[PAD + side : PAD + side + cells, :] + below[PAD - side : PAD - side + cells, :]
            )
            return carry

        lax.fori_loop(0, C // TILE, middle, 0)
        gain = misc_ref[3 * number : 3 * number + 1, :]
        bias = misc_ref[6 + 3 * number : 7 + 3 * number, :]
        pre1_copy.wait()

        def norm(rows):
            normal, scale = centered(pre1_ref[rows, :])
            hidden = normal * gain + bias
            inner = work[rows, :] * silu_back(hidden)
            parts[0:8, :] += fold(inner * normal)
            parts[8:16, :] += fold(inner)
            grad_pre1[0, rows, :] = low(norm_back(inner, normal, scale, gain))

        tiles(cells, ROWS, norm)
        sums[...] = jnp.sum(parts[...].reshape(2, 8, C), axis=1)
        core = table_ref[CORE]
        other[...] = grad_pre1[0, :, pl.ds(pl.multiple_of((1 - core) * half, half), half)]
        wait(first_copies)
        direct_copy.wait()

        def first(cut):
            grad_u[:, cut] = direct_ref[:, cut] + dot_rows(grad_pre1[0], wi[cut, :])

        tiles(C, TILE, first)
        if closing:

            last_0, first_1, last_1, bias_grad = rest_refs

            def turn(cut):
                stacked = jnp.concatenate(
                    [grad_u[:, cut]]
                    + [ref[row : row + 1, cut] for ref, row in ((sums, 0), (last_0, 2), (last_0, 0))]
                    + [ref[row : row + 1, cut] for ref, row in ((first_1, 0), (last_1, 2), (last_1, 0))]
                    + [ref[row : row + 1, cut] for ref, row in ((sums, 1), (last_0, 3), (last_0, 1))]
                    + [ref[row : row + 1, cut] for ref, row in ((first_1, 1), (last_1, 3), (last_1, 1))]
                    + [bias_grad[:, cut], jnp.zeros((2 * side_half - cells - MISC, 128), jnp.float32)]
                )
                parts_of = low(jnp.transpose(stacked))
                for part in range(2):
                    piece = parts_of[:, part * side_half : (part + 1) * side_half]

                    @pl.when(core == part)
                    def _(piece=piece):
                        turned[0][cut, :] = piece

                    @pl.when(core != part)
                    def _(piece=piece):
                        turned[1][cut, :] = piece

            tiles(C, 128, turn)

    outs = [shaped(cells, C), shaped(2, C), shaped(1, cells, C, dtype=bf16), shaped(cells, half, dtype=bf16)]
    if closing:
        outs += [shaped(C, side_half, dtype=bf16)] * 2
    f32 = jnp.float32
    scratch = [
        pltpu.VMEM((9 * C, C), bf16),
        pltpu.VMEM((C, C), bf16),
        pltpu.VMEM((cells, C), bf16),
        pltpu.VMEM((cells, C), f32),
        pltpu.VMEM((cells, C), f32),
        pltpu.VMEM((cells, 3 * C), bf16),
        pltpu.VMEM((cells + 2 * PAD, TILE), f32),
        pltpu.VMEM((cells + 2 * PAD, TILE), f32),
        pltpu.VMEM((cells, C), f32),
        pltpu.VMEM((16, C), f32),
        pltpu.SemaphoreType.DMA((w_middle.copies + w_first.copies + 3,)),
    ]
    weights = w_middle.operands + w_first.operands
    return call(
        kernel,
        "back_first",
        [table, grads, pre1, direct, misc] + extra + weights,
        [SMEM] + [ANY] * 3 + [IN] * (1 + len(extra)) + [ANY] * len(weights),
        outs,
        [IN] * len(outs),
        scratch,
        2 * cells * 10 * C * C,
        20 * C * C + 24 * cells * C,
    )


def place_halves(core, pair, rest=None):
    _, rows, half = pair[0].shape
    extra = [] if rest is None else [rest]

    def kernel(core_ref, mine, other, *refs):
        target = refs[-1]
        for part in range(2):

            @pl.when(core_ref[0] == part)
            def _(part=part):
                target[0, :, part * half : (part + 1) * half] = mine[0]
                target[0, :, (1 - part) * half : (2 - part) * half] = other[0]

        if extra:
            target[1] = wide(refs[0][0])

    return call(
        kernel,
        "place_halves",
        [core, *pair] + extra,
        [SMEM] + [IN] * (2 + len(extra)),
        shaped(1 + len(extra), rows, 2 * half),
        IN,
        [],
        0,
        16 * rows * half,
    )


def place_last(core, mine, other, cells):
    _, rows, half = mine.shape

    def kernel(core_ref, mine_ref, other_ref, first, last, pos, gains, biases, bias, side):
        for part in range(2):

            @pl.when(core_ref[0] == part)
            def _(part=part):
                for target, block, number in ((last, 0, 0), (first, 1, 1), (last, 1, 2), (first, 0, 3)):
                    target[block, :, part * half : (part + 1) * half] = mine_ref[number]
                    target[block, :, (1 - part) * half : (2 - part) * half] = other_ref[number]
                side[:, part * SIDE : (part + 1) * SIDE] = mine_ref[4, :, :SIDE]
                side[:, (1 - part) * SIDE : (2 - part) * SIDE] = other_ref[4, :, :SIDE]

        pos[...] = side[:, :cells]
        turned = jnp.transpose(side[...])
        for number in range(6):
            gains[number % 3, number // 3 : number // 3 + 1, :] = turned[cells + number : cells + number + 1]
            biases[number % 3, number // 3 : number // 3 + 1, :] = turned[cells + 6 + number : cells + 7 + number]
        bias[...] = turned[cells + 12 : cells + MISC]

    return call(
        kernel,
        "place_last",
        [core, mine, other],
        [SMEM, IN, IN],
        [shaped(2, rows, 2 * half)] * 2 + [shaped(rows, cells)] + [shaped(3, 2, rows)] * 2 + [shaped(4, rows)],
        [IN] * 6,
        [pltpu.VMEM((rows, 2 * SIDE), jnp.float32)],
        0,
        32 * rows * half * 5,
    )


def after(value, *earlier):
    return lax.optimization_barrier((value, earlier))[0]


class Movement:
    def __init__(self, mesh):
        self.dp = mesh.shape["dp"]
        self.cores = mesh.shape["fsdp"]
        self.line = self.dp // PLANE
        self.devices = self.dp * self.cores
        self.ring = [0] + list(range(1, self.line, 2)) + list(range(2, self.line, 2))[::-1]
        self.paired = self.cores == 2 and self.line == 4

    def flip(self, value, bits):
        return lax.ppermute(value, "dp", [(i, i ^ bits) for i in range(self.dp)])

    def along(self, value):
        pairs = []
        for position, level in enumerate(self.ring):
            following = self.ring[(position + 1) % self.line]
            pairs += [(level * PLANE + near, following * PLANE + near) for near in range(PLANE)]
        return lax.ppermute(value, "dp", pairs)

    def swap(self, value):
        return lax.ppermute(value, "fsdp", [(0, 1), (1, 0)])

    def lines(self):
        return [[level * PLANE + near for level in range(self.line)] for near in range(PLANE)]

    def table(self):
        if not self.paired:
            return jnp.zeros((TABLE,), jnp.int32)
        steps, chips = range(self.line), range(PLANE)
        halves = [(1, 0), (1, 1), (3, 0), (3, 1), (2, 2), (2, 3), (3, 2), (3, 3), (1, 2), (1, 3), (2, 0), (2, 1)]
        halves += [(0, step) for step in steps]
        rows = []
        for device in range(self.devices):
            chip, core = divmod(device, 2)
            level, near = divmod(chip, PLANE)
            position = self.ring.index(level)

            def chip_at(far, level, near=near):
                return level * PLANE + (near ^ far)

            def step_at(step, position=position):
                return self.ring[(position + step) % self.line]

            row = [chip_at(far, step_at(-step)) * 2 + (core + k) % 2 for k in range(2) for far in chips for step in steps]
            row += [chip_at(far, step) * 2 + (core + k) % 2 for k in range(2) for far in chips for step in steps]
            row += [chip_at(far, step_at(step)) for far, step in halves]
            row += [chip_at(far, step) for far, step in halves]
            row += [chip_at(far, step_at(step)) for step in reversed(steps) for far in chips]
            row.append(core)
            firsts = [chip_at(0, step) * 2 + core for step in steps]
            firsts = [9 * C // self.devices * owner for owner in firsts]
            row += [first % 128 for first in firsts]
            side = G // 2
            for first in firsts:
                for tile in range(first // 128, first // 128 + 3):
                    tap, part = divmod(tile, C // 128)
                    tap_row, tap_column = divmod(tap, 3)
                    away = (tap_row - 1) * side + tap_column - 1
                    row += [128 * part, -away % (2 * PLANE * side * side), tap_row, tap_column]
            rows.append(row)
        index = lax.axis_index("dp") * self.cores + lax.axis_index("fsdp")
        return lax.dynamic_index_in_dim(jnp.asarray(np.array(rows, np.int32)), index, 0, keepdims=False)


class Piece:
    def __init__(self, move, own, name):
        self.move = move
        self.own = own
        self.name = name
        self.rows = own.shape[0]
        self.at = STEPS
        self.found = []

    def keep(self, array, far, steps, first=0, other=None):
        for i, step in enumerate(steps):
            for core, held in enumerate((array, other)):
                self.found.append((held, first + i * self.rows, self.at + 16 * core + 4 * far + step))

    def line(self, second=(), third=(), first=()):
        with jax.named_scope(self.name + "_line"):
            one = self.move.along(after(self.own, *first) if first else self.own)
            two = self.move.along(after(one, *second) if second else one)
            three = self.move.along(after(two, *third) if third else two)
        self.passed = (one, two, three)
        self.held = jnp.concatenate([self.own, one, two, three])

    def levels(self, *earlier):
        with jax.named_scope(self.name + "_levels"):
            own = after(self.own, *earlier) if earlier else self.own
            self.held = lax.all_gather(own, "dp", axis_index_groups=self.move.lines(), axis=0, tiled=True)
        self.at = LEVELS

    def settle_line(self, *earlier):
        with jax.named_scope("swap"):
            other = self.move.swap(after(self.held, *earlier) if earlier else self.held)
        self.keep(self.held, 0, range(4), other=other)

    def plane_first(self, *earlier):
        half = self.rows // 2
        own = after(self.own, *earlier) if earlier else self.own
        with jax.named_scope(self.name + "_plane"):
            first, second = self.sides = self.move.flip(own, 1), self.move.flip(own, 2)
            self.fars = (self.move.flip(first[:half], 2), self.move.flip(second[half:], 1))
            self.passed = (jnp.concatenate([self.own, first, second, *self.fars]),)

    def pass_on(self, *earlier):
        with jax.named_scope(self.name + "_line"):
            self.passed += (self.move.along(after(self.passed[-1], *earlier)),)

    def end_line(self, *earlier):
        for step, array in enumerate(after(self.passed, *earlier)):
            other = self.move.swap(array)
            for far in range(PLANE):
                self.keep(array, far, [step], first=far * self.rows, other=other)


def cross(move, pieces, fars, *earlier):
    over_first = [piece.held for piece in pieces] + [piece.second[2 * piece.rows : 4 * piece.rows] for piece in fars]
    over_second = [piece.held for piece in pieces] + [piece.first[: 2 * piece.rows] for piece in fars]
    over_first, over_second = [jnp.concatenate(parts) if len(parts) > 1 else parts[0] for parts in (over_first, over_second)]
    if earlier:
        over_first, over_second = after((over_first, over_second), *earlier)
    with jax.named_scope("_".join(piece.name for piece in pieces + fars) + "_plane"):
        first, second = move.flip(over_first, 1), move.flip(over_second, 2)
    row = 0
    for piece in pieces:
        piece.sides = (first, second, row)
        piece.first = first[row : row + 4 * piece.rows]
        piece.second = second[row : row + 4 * piece.rows]
        row += 4 * piece.rows
    for piece in fars:
        piece.far_sides = (first, second, row)
        piece.far_first = first
        row += 2 * piece.rows
    return first, second


def settle(move, pieces, fars, *earlier):
    first, second = (pieces[0].sides if pieces else fars[0].far_sides)[:2]
    if earlier:
        first, second = after((first, second), *earlier)
    with jax.named_scope("swap"):
        first_other, second_other = move.swap(first), move.swap(second)
    for piece in pieces:
        row = piece.sides[2]
        piece.first = first[row : row + 4 * piece.rows]
        piece.second = second[row : row + 4 * piece.rows]
        piece.keep(first, 1, range(4), first=row, other=first_other)
        piece.keep(second, 2, range(4), first=row, other=second_other)
    for piece in fars:
        row = piece.far_sides[2]
        piece.keep(first, 3, (2, 3), first=row, other=first_other)
        piece.keep(second, 3, (0, 1), first=row, other=second_other)


class Spread:
    def __init__(self, move, own, *earlier):
        self.move = move
        self.own = after(own, *earlier) if earlier else own
        with jax.named_scope("spread"):
            self.sides = tuple(move.flip(self.own, bits) for bits in (1, 2, 3))

    def end(self, *earlier):
        with jax.named_scope("spread_swap"):
            here = jnp.concatenate(after((self.own, *self.sides), *earlier))
            self.all = [here, self.move.swap(here)]


class Sum:
    def __init__(self, move, arrays, name, levels=False):
        self.move = move
        self.arrays = arrays
        self.name = name
        self.levels = levels

    def across(self, *earlier):
        first, second = after(tuple(self.arrays[:2]), *earlier) if earlier else self.arrays[:2]
        with jax.named_scope(self.name + "_across"):
            self.first = self.move.flip(first, 1)
            self.second = self.move.flip(second, 2)
        return self.first, self.second

    def prepare(self, *earlier):
        self.first, self.second = after((self.first, self.second), *earlier)
        with jax.named_scope(self.name + "_onward"):
            self.rests = (
                low(wide(self.arrays[2]) + wide(self.second[2:])),
                low(wide(self.arrays[3]) + wide(self.first[2:])),
            )
        self.operands = self.rests
        return self.rests

    def onward(self, *earlier):
        rests = after(self.rests, *earlier) if earlier else self.rests
        with jax.named_scope(self.name + "_onward"):
            self.rests = (self.move.flip(rests[0], 1), self.move.flip(rests[1], 2))

    def gather(self, *earlier):
        rests = after(self.rests, *earlier) if earlier else self.rests
        with jax.named_scope(self.name + "_held"):
            held = self.arrays[4]
            self.near = wide(held[:2]) + wide(self.first[:2]) + wide(rests[1])
            self.far = wide(held[2:]) + wide(self.second[:2]) + wide(rests[0])
            if self.levels:
                held = jnp.concatenate([low(self.near), low(self.far)])
                self.held = held.reshape(-1, held.shape[-1])
                return self.held
            self.far = (self.far[0], low(self.far[1]))
            return self.far

    def finish(self, *earlier):
        with jax.named_scope(self.name + "_line"):
            if self.levels:
                lines = self.move.lines()
                owned = lax.psum_scatter(self.held, "dp", axis_index_groups=lines, scatter_dimension=0, tiled=True)
                self.owned = wide(owned)
            else:
                three = self.move.along(self.far[1])
                two = self.move.along(low(self.far[0] + wide(three)))
                two = after(two, *earlier) if earlier else two
                one = self.move.along(low(self.near[1] + wide(two)))
                self.passed = (three, two, one)
                self.owned = self.near[0] + wide(one)


class LineSum:
    def __init__(self, move, arrays, name):
        self.move = move
        self.arrays = arrays
        self.name = name
        self.next = arrays[0]

    def line(self, step, *earlier):
        value = after(self.next, *earlier) if earlier else self.next
        with jax.named_scope(f"{self.name}_line{step}"):
            self.sent = self.move.along(value)

    def prepare(self, step, *earlier):
        with jax.named_scope(f"{self.name}_line{step}"):
            sent = after(self.sent, *earlier) if earlier else self.sent
            self.next = low(wide(self.arrays[step]) + wide(sent))
        return self.next

    def prepare_across(self, *earlier):
        sent = after(self.sent, *earlier) if earlier else self.sent
        with jax.named_scope(self.name + "_across"):
            held = wide(self.arrays[3]) + wide(sent)
            half = held.shape[1] // 2
            self.near, self.rest = held[:, :half], held[:, half:]
            self.operands = (low(self.near[1::2]), low(self.rest[2:]))
        return self.operands

    def across(self, *earlier):
        operands = after(self.operands, *earlier) if earlier else self.operands
        with jax.named_scope(self.name + "_across"):
            self.first = self.move.flip(operands[0], 1)
            self.second = self.move.flip(operands[1], 2)

    def prepare_onward(self, *earlier):
        self.first, self.second = after((self.first, self.second), *earlier) if earlier else (self.first, self.second)
        with jax.named_scope(self.name + "_onward"):
            self.operands = (low(self.rest[1] + wide(self.second[1])), low(self.near[2] + wide(self.first[1])))
        return self.operands

    def finish(self, *earlier):
        operands = after(self.operands, *earlier) if earlier else self.operands
        with jax.named_scope(self.name + "_onward"):
            first_rest = self.move.flip(operands[0], 1)
            second_rest = self.move.flip(operands[1], 2)
            near = self.near[0] + wide(self.first[0]) + wide(second_rest)
            rest = self.rest[0] + wide(self.second[0]) + wide(first_rest)
            self.owned = jnp.concatenate([near, rest])


def whole_matrix(array):
    blocks = Blocks()
    blocks.add(array, None, 0, 0, None, 0, 0, 0, *array.shape)
    return blocks


def halves(move, owned, matrices):
    blocks = owned.reshape(matrices, 2, -1, owned.shape[-1])
    core = lax.axis_index("fsdp")
    mine = lax.dynamic_index_in_dim(blocks, core, 1, keepdims=False)
    return mine, move.swap(lax.dynamic_index_in_dim(blocks, 1 - core, 1, keepdims=False))


def local(
    move,
    features,
    grid_live,
    pos_embed,
    w_in,
    w_mid,
    w_out,
    norm_gain,
    norm_bias,
    readout_w,
    readout_b,
    cotangent,
):
    rows, middle_rows, width = w_in.shape[1], w_mid.shape[1], readout_w.shape[1]
    cells = pos_embed.shape[0]
    half_side = G // 2
    paired = move.paired
    scales = [norm_gain.reshape(6, rows).T, norm_bias.reshape(6, rows).T, readout_b.reshape(rows, 4)]
    beside = jnp.concatenate([pos_embed.T, *scales, jnp.zeros((rows, C - cells - MISC), jnp.bfloat16)], axis=1)
    if paired:
        cut = middle_rows // 2
        stacks = [
            [w_in[0], beside, w_out[0]],
            [w_mid[0, :cut]],
            [w_mid[0, cut:], w_in[1], w_out[1]],
            [w_mid[1]],
            [readout_w[:, i * C : (i + 1) * C] for i in range(width // C)],
        ]
        one, two, three, four, top = [
            Piece(move, jnp.concatenate(stack) if len(stack) > 1 else stack[0], name)
            for stack, name in zip(stacks, ("one", "two", "three", "four", "top"))
        ]
        one.line()
        top.plane_first(one.passed[0])
        two.line(one.passed[1:2], one.passed[2:])
        three.line(two.passed[1:2], two.passed[2:])
        four.line(first=three.passed[2:])
        cross(move, [one], [], *top.fars)
        cross(move, [two], [one], one.first)
        one.settle_line(one.first)
        settle(move, [one], [], one.first)
        cross(move, [three], [two], two.first)
        two.settle_line(two.first)
        settle(move, [two], [one], two.first)
        top.pass_on(four.passed[1])
        cross(move, [], [three], three.first, four.passed[2])
        three.settle_line(three.first)
        settle(move, [three], [two], three.first)
        cross(move, [four], [], three.far_first)
        top.pass_on(three.far_first)
        settle(move, [], [three], three.far_first, top.passed[1])
        lies = {
            "head_0": [(one, 0, rows, 0, 0, C), (one, rows, rows, 0, C, HEAD - C)],
            "middle_0": [(two, 0, cut, 0, 0, C), (three, 0, cut, cut, 0, C)],
            "last_0": [(one, 2 * rows, rows, 0, 0, C)],
            "first_1": [(three, cut, rows, 0, 0, C)],
            "last_1": [(three, cut + rows, rows, 0, 0, C)],
            "middle_1": [(four, 0, middle_rows, 0, 0, C)],
            "readout": [(top, i * rows, rows, 0, i * C, C) for i in range(width // C)],
        }
    else:

        def whole(own):
            return lax.all_gather(own, ("dp", "fsdp"), axis=0, tiled=True)

        first_all = whole(w_in[0])
        lies = {
            "head_0": [(first_all, 0), (whole(beside[:, : HEAD - C]), C)],
            "middle_0": [(whole(w_mid[0]), 0)],
            "last_0": [(whole(w_out[0]), 0)],
            "first_1": [(whole(w_in[1]), 0)],
            "last_1": [(whole(w_out[1]), 0)],
            "middle_1": [(whole(w_mid[1]), 0)],
            "readout": [(whole(readout_w), 0)],
        }

    def matrix(name):
        blocks = Blocks()
        if not paired:
            for array, column in lies[name]:
                blocks.add(array, None, 0, 0, None, 0, 0, column, *array.shape)
            return blocks
        stride = middle_rows if name.startswith("middle") else rows
        for piece, row, extent, to_row, to_column, columns in lies[name]:
            for array, first, place in piece.found:
                blocks.add(array, None, first + row, 0, place, stride, to_row, to_column, extent, columns)
        return blocks

    def sums_of(columns, matrices, pieces=((None, STEPPED),)):
        blocks = Blocks()
        if not paired:
            extent = sum(matrices) * move.devices
            blocks.add(shaped(1, extent, columns), 0, 0, 0, None, 0, 0, 0, extent, columns)
            return blocks
        runs, start = [], 0
        for block_rows in matrices:
            runs.append((start, 2 * block_rows, 0))
            start += move.devices * block_rows
        for cut, kind in pieces:
            taken = []
            while runs and cut != 0:
                start, stride, first = runs.pop(0)
                extent = stride - first if cut is None else min(cut, stride - first)
                taken.append((start + first, stride, extent))
                if first + extent < stride:
                    runs.insert(0, (start, stride, first + extent))
                cut = None if cut is None else cut - extent
            place = {STEPPED: OUT_STEPS, LEVELED: OUT_LEVELS, LINED: OUT_LINE}[kind]
            for count in (4, 4, 4, 4) if kind == LINED else (4, 4, 2, 2, 4):
                array = shaped(count, sum(extent for _, _, extent in taken), columns)
                for block in range(count):
                    row = 0
                    for first, stride, extent in taken:
                        blocks.add(array, block, row, 0, place, stride, first, 0, extent, columns)
                        row += extent
                    place += 1
        return blocks

    def swap(value):
        return move.swap(value) if paired else None

    def tie(value, *earlier):
        return after(value, *earlier) if paired else value

    def scattered(terms, matrices=1):
        total = wide(terms[0][0]).reshape(matrices, -1, terms[0].shape[-1])
        return lax.psum_scatter(total, ("dp", "fsdp"), scatter_dimension=1, tiled=True)

    half = 2 if paired else 1
    table = move.table()
    mid_0, last_0 = matrix("middle_0"), matrix("last_0")
    misc, pooled, stream_in, lefts_0, pre1_0, pre2_0, pre3_0, first_0, last_0 = forward_block(
        table, 0, G, None, features[0], None, matrix("head_0"), mid_0, last_0
    )
    lefts_other_0 = swap(lefts_0)
    if paired:
        settle(move, [four], [], pooled)
        cross(move, [], [four], top.passed[2])
        top.pass_on(pooled)
        four.settle_line(pooled)
        settle(move, [], [four])
    first_1, mid_1, last_1 = matrix("first_1"), matrix("middle_1"), matrix("last_1")
    if paired:
        top.end_line(pooled)
        pooled = tie(pooled, top.passed[3])
    lefts_1, pre1_1, pre2_1, pre3_1, first_1, last_1 = forward_block(
        table, 1, half_side, pooled, None, misc, first_1, mid_1, last_1
    )
    first_0, last_0, first_1, last_1 = [whole_matrix(array) for array in (first_0, last_0, first_1, last_1)]
    lefts_other_1 = swap(lefts_1)
    readout_bias = misc[12:].T.reshape(1, width)
    output, grad_top, grad_readout_b, grad_logits, grad_logits_other = readout(
        table, grid_live, tie(lefts_1, lefts_other_0), readout_bias, cotangent[0], matrix("readout")
    )
    if paired:
        acts = Spread(move, lefts_1[1])
        grad_logits_other = swap(after(grad_logits_other, *acts.sides))
        grad_top = after(grad_top, *acts.sides)
    else:
        grad_logits, grad_logits_other = jnp.concatenate([grad_logits, grad_logits_other], axis=1), None
    direct_1, grads_1, grads_other_1, sums_1 = back_last(
        table, 1, half_side, grad_top, pooled, pre3_1, pre2_1, misc, last_1
    )
    if paired:
        spread = Spread(move, grads_1[1], grad_logits_other)
        grads_other_1 = tie(grads_other_1, grad_logits_other)
    grads_other_1 = swap(grads_other_1)
    readout_terms = weight_terms(
        table,
        None,
        [(lefts_1, 3, lefts_other_1, tie(grad_logits, sums_1), None, grad_logits_other, None)],
        [],
        sums_of(width // half, [rows], [(None, LEVELED)]),
    )
    if paired:
        sum_readout = Sum(move, readout_terms, "readout", levels=True)
        spread.sides = after(spread.sides, *readout_terms)
        sum_readout.across(grads_other_1, *spread.sides)
        grads_1 = tie(grads_1, *readout_terms, *spread.sides)
    else:
        middle_terms_1 = weight_terms(
            table,
            (half_side, lefts_1, lefts_other_1, grads_1, grads_other_1),
            [],
            [],
            sums_of(C // half, [middle_rows]),
        )
    grad_pooled, sums_first_1, grad_first_1, grad_first_other_1 = back_first(
        table, 1, half_side, grads_1, pre1_1, direct_1, misc, None, mid_1, first_1
    )
    direct_0, grads_0, grads_other_0, sums_0 = back_last(
        table, 0, G, grad_pooled, stream_in, pre3_0, pre2_0, misc, last_0
    )
    if paired:
        waited = [*sum_readout.prepare(sums_0), *after(spread.sides, sums_0)]
        lefts_other_0 = tie(lefts_other_0, *waited)
        grads_other_0, grad_first_other_1 = after((grads_other_0, grad_first_other_1), *waited)
        spread.end(*waited)
        acts.end(*waited)
        sum_readout.onward(*waited)
    grads_other_0, grad_first_other_1 = swap(grads_other_0), swap(grad_first_other_1)
    crossed_terms = weight_terms(
        table,
        (G, lefts_0, lefts_other_0, grads_0, grads_other_0),
        [],
        [],
        sums_of(C // half, [middle_rows]),
    )
    if paired:
        sum_middle_0 = Sum(move, crossed_terms, "middle_0")
        waited = [sum_readout.gather(*crossed_terms), *after((*spread.all, *acts.all), *crossed_terms)]
        sum_readout.finish()
        sum_middle_0.across(*waited)
        acts.all[0] = tie(acts.all[0], *waited)
        middle_terms_1 = plane_terms(table, half_side, acts.all, spread.all, middle_rows)
        grads_0 = tie(grads_0, middle_terms_1, *waited)
    rests = [sums_0, sums_first_1, sums_1, grad_readout_b.reshape(C, 4).T]
    grad_in, _, grad_first_0, grad_first_other_0, side, side_other = back_first(
        table, 0, G, grads_0, pre1_0, direct_0, misc, rests, mid_0, first_0
    )
    if paired:
        waited = [*sum_middle_0.prepare(grad_in)]
        grad_first_other_0, side_other = after((grad_first_other_0, side_other), *waited)
        side_other = swap(side_other)
        sides = [(side, side_other)]
        sum_middle_0.onward(*waited)
        with jax.named_scope("middle_1_levels"):
            owned_1 = lax.psum_scatter(
                middle_terms_1.reshape(-1, C),
                "dp",
                axis_index_groups=move.lines(),
                scatter_dimension=0,
                tiled=True,
            )
        lefts_other_0 = tie(lefts_other_0, *waited)
    else:
        sides = [(side, None), (side_other, None)]
    grad_first_other_0 = swap(grad_first_other_0)
    last_terms = weight_terms(
        table,
        None,
        [
            (lefts_0, 2, lefts_other_0, grads_0, 0, grads_other_0, 0),
            (lefts_1, 0, lefts_other_1, grad_first_1, 0, grad_first_other_1, None),
            (lefts_1, 2, lefts_other_1, grads_1, 0, grads_other_1, 0),
            (lefts_0, 0, lefts_other_0, grad_first_0, 0, grad_first_other_0, None),
        ],
        sides,
        sums_of(C // half, [rows] * 5),
    )
    if paired:
        sum_last = Sum(move, last_terms, "last")
        waited = sum_middle_0.gather(*last_terms)
        sum_last.across(*waited)
        sum_middle_0.finish()
        core = jnp.reshape(lax.axis_index("fsdp"), (1,))
        readout_owned = place_halves(core, halves(move, sum_readout.owned, 1))[0].reshape(rows, width)
        sum_last.prepare(readout_owned)
        sum_last.onward()
        sum_last.gather()
        middle_owned = place_halves(core, halves(move, sum_middle_0.owned, 1), owned_1[None])
        sum_last.finish(middle_owned)
        first_grad, last_grad, pos_grad, gain_grad, bias_grad, readout_grad = place_last(core, *halves(move, sum_last.owned, 5), cells)
        readout_grad = readout_grad.T
        pos_grad = pos_grad.T
        gain_grad, bias_grad = jnp.swapaxes(gain_grad, 0, 1), jnp.swapaxes(bias_grad, 0, 1)
    else:
        readout_owned = scattered(readout_terms)[0]
        middle_owned = jnp.concatenate([scattered(terms) for terms in (crossed_terms, middle_terms_1)])
        last_owned = scattered(last_terms, 5)
        first_grad, last_grad = jnp.stack([last_owned[3], last_owned[1]]), jnp.stack([last_owned[0], last_owned[2]])
        pos_grad = last_owned[4, :, :cells].T
        scales = last_owned[4, :, cells : cells + MISC]
        gain_grad, bias_grad = scales[:, 0:6].T.reshape(2, 3, rows), scales[:, 6:12].T.reshape(2, 3, rows)
        readout_grad = scales[:, 12:]
    return (
        output[None],
        grad_in[None],
        pos_grad,
        first_grad,
        middle_owned,
        last_grad,
        gain_grad,
        bias_grad,
        readout_owned,
        readout_grad.reshape(-1),
    )


def solution(mesh):
    return jax.shard_map(
        functools.partial(local, Movement(mesh)),
        mesh=mesh,
        in_specs=(
            P(("dp", "fsdp"), None, None),
            P(("dp", "fsdp")),
            P(None, ("dp", "fsdp")),
            P(None, ("dp", "fsdp"), None),
            P(None, ("dp", "fsdp"), None),
            P(None, ("dp", "fsdp"), None),
            P(None, None, ("dp", "fsdp")),
            P(None, None, ("dp", "fsdp")),
            P(("dp", "fsdp"), None),
            P(("dp", "fsdp")),
            P(("dp", "fsdp"), None, None),
        ),
        out_specs=(
            P(("dp", "fsdp"), None, None),
            P(("dp", "fsdp"), None, None),
            P(None, ("dp", "fsdp")),
            P(None, ("dp", "fsdp"), None),
            P(None, ("dp", "fsdp"), None),
            P(None, ("dp", "fsdp"), None),
            P(None, None, ("dp", "fsdp")),
            P(None, None, ("dp", "fsdp")),
            P(("dp", "fsdp"), None),
            P(("dp", "fsdp")),
        ),
        check_vma=False,
    )
```

```python
import functools

import jax
import jax.numpy as jnp
import numpy as np
from jax import lax
from jax.experimental import pallas as pl
from jax.experimental.pallas import tpu as pltpu
from jax.sharding import PartitionSpec as P

C = 1024
G = 24
PLANE = 4
TILE = 256
ROWS = 144
PAD = 24
MISC = 16
HEAD = 1664
SIDE = 384
STEPS, LEVELS, OUT_STEPS, OUT_LEVELS, OUT_LINE, CORE, WINDOWS, TABLE = 0, 32, 64, 80, 96, 112, 113, 165
STEPPED, LEVELED, LINED = range(3)
COST = 4
COSTS = {"forward_block": 50}
VMEM = 60 * 1024 * 1024


def low(value):
    return value.astype(jnp.bfloat16)


def wide(value):
    return value.astype(jnp.float32)


def dot(left, right):
    return jnp.dot(left, right, preferred_element_type=jnp.float32)


def dot_rows(left, right):
    return lax.dot_general(left, right, (((1,), (1,)), ((), ())), preferred_element_type=jnp.float32)


def dot_sums(left, right):
    return lax.dot_general(left, right, (((0,), (0,)), ((), ())), preferred_element_type=jnp.float32)


def sigmoid(value):
    return 1.0 / (1.0 + jnp.exp(-value))


def centered(value):
    center = value - jnp.mean(value, axis=-1, keepdims=True)
    spread = jnp.mean(center * center, axis=-1, keepdims=True)
    scale = lax.rsqrt(spread + 1e-05)
    return center * scale, scale


def norm_back(grad, normal, scale, gain):
    inner = grad * gain
    first = jnp.mean(inner, axis=-1, keepdims=True)
    second = jnp.mean(inner * normal, axis=-1, keepdims=True)
    return scale * (inner - first - normal * second)


def silu_back(value):
    gate = sigmoid(value)
    return gate * (1.0 + value * (1.0 - gate))


def tiles(extent, size, body):
    def step(i, carry):
        body(pl.ds(pl.multiple_of(i * size, size), size))
        return carry

    lax.fori_loop(0, extent // size, step, 0)


def fold(value):
    return jnp.sum(value.reshape(-1, 8, value.shape[-1]), axis=0)


def columns_of(cells, side, lanes):
    index = lax.broadcasted_iota(jnp.int32, (cells, lanes), 0).astype(jnp.float32)
    return index - side * jnp.floor((index + 0.5) * (1.0 / side))


def beside(value, side, step):
    cells = value.shape[0]
    column = columns_of(cells, side, value.shape[1])
    inside = column < side - 1 if step > 0 else column > 0
    return jnp.where(inside, pltpu.roll(value, (cells - step) % cells, 0), 0.0)


class Blocks:
    def __init__(self):
        self.operands = []
        self.moves = []

    def operand(self, array):
        for number, known in enumerate(self.operands):
            if known is array:
                return number
        self.operands.append(array)
        return len(self.operands) - 1

    def add(self, array, block, row, column, place, stride, to_row, to_column, rows, columns):
        self.moves.append((self.operand(array), block, row, column, place, stride, to_row, to_column, rows, columns))

    @property
    def copies(self):
        return len(self.moves)

    def firsts(self, places):
        return [
            to_row + (places[place] * stride if place is not None else jnp.int32(0))
            for _, _, _, _, place, stride, to_row, _, _, _ in self.moves
        ]

    def ends(self, places):
        return [
            to_row + rows + (places[place] * stride if place is not None else 0)
            for _, _, _, _, place, stride, to_row, _, rows, _ in self.moves
        ]

    def bind(self, refs, places, matrix, sems, to_blocks=False, base=0):
        made = []
        for number, block, row, column, place, stride, to_row, to_column, rows, columns in self.moves:
            first = to_row
            if place is not None:
                first = pl.multiple_of(places[place] * stride + to_row, 16)
            inside = matrix.at[pl.ds(first, rows), pl.ds(to_column, columns)]
            outside = refs[number] if block is None else refs[number].at[block]
            outside = outside.at[pl.ds(row, rows), pl.ds(column, columns)]
            pair = (inside, outside) if to_blocks else (outside, inside)
            made.append(pltpu.make_async_copy(*pair, sems.at[base + len(made)]))
        return made


def start(copies):
    for copy in copies:
        copy.start()


def wait(copies):
    for copy in copies:
        copy.wait()


ANY = pl.BlockSpec(memory_space=pltpu.HBM)
IN = pl.BlockSpec(memory_space=pltpu.VMEM)
SMEM = pl.BlockSpec(memory_space=pltpu.SMEM)


def call(kernel, name, ins, in_specs, outs, out_specs, scratch, flops, moved):
    short = COSTS.get(name, COST)
    return pl.pallas_call(
        kernel,
        name=name,
        out_shape=outs,
        in_specs=in_specs,
        out_specs=out_specs,
        scratch_shapes=scratch,
        compiler_params=pltpu.CompilerParams(vmem_limit_bytes=VMEM),
        cost_estimate=pl.CostEstimate(flops=int(flops) // short, bytes_accessed=int(moved) // short, transcendentals=0),
    )(*ins)


class Traffic:
    def __init__(self, sems):
        self.sems = sems
        self.used = 0
        self.sent = []

    def begin(self, source, target):
        copy = pltpu.make_async_copy(source, target, self.sems.at[self.used])
        self.used += 1
        copy.start()
        return copy

    def send(self, source, target):
        self.sent.append(self.begin(source, target))

    def load(self, blocks, refs, places, matrix):
        copies = blocks.bind(refs, places, matrix, self.sems, base=self.used)
        self.used += len(copies)
        start(copies)
        return copies

    def plan(self, blocks, refs, places, matrix):
        copies = blocks.bind(refs, places, matrix, self.sems, to_blocks=True, base=self.used)
        self.used += len(copies)
        self.sent += copies
        return copies

    def plan_in(self, blocks, refs, places, matrix):
        copies = blocks.bind(refs, places, matrix, self.sems, base=self.used)
        self.used += len(copies)
        return copies

    def store(self, blocks, refs, places, matrix):
        start(self.plan(blocks, refs, places, matrix))

    def finish(self):
        wait(self.sent)


def shaped(*shape, dtype=jnp.float32):
    return jax.ShapeDtypeStruct(shape, dtype)


def forward_block(table, number, side, stream, features, misc, w_first, w_middle, w_last):
    cells = side * side
    opening = features is not None
    n_first, n_middle, n_last = len(w_first.operands), len(w_middle.operands), len(w_last.operands)
    given = [features] if opening else [stream, misc]
    given_count = len(given)
    bf16 = jnp.bfloat16
    n_lefts = 3 if opening else 4

    def kernel(table_ref, *refs):
        refs = list(refs)
        heads = [refs.pop(0) for _ in range(given_count)]
        firsts = [refs.pop(0) for _ in range(n_first)]
        middles = [refs.pop(0) for _ in range(n_middle)]
        lasts = [refs.pop(0) for _ in range(n_last)]
        if opening:
            misc_ref, pooled_ref, u_out = refs.pop(0), refs.pop(0), refs.pop(0)
            u_ref = refs.pop(0 - 1)
        else:
            u_ref, misc_ref = heads
        lefts_out, pre1_out, pre2_out, pre3_out, wi_out, wo_out = [refs.pop(0) for _ in range(6)]
        wi, wm, wo, taps, lefts, above, below, work, pairs, pre1, pre2, pre3, sems = refs
        traffic = Traffic(sems)
        first_copies = traffic.load(w_first, firsts, table_ref, wi)
        middle_copies = traffic.load(w_middle, middles, table_ref, wm)
        last_copies = traffic.load(w_last, lasts, table_ref, wo)
        wait(first_copies)
        traffic.send(wi.at[:, pl.ds(0, C)], wi_out)
        if opening:

            def place(cut):
                turned = jnp.transpose(wide(wi[cut, C:HEAD]))
                u_ref[:, cut] = wide(heads[0][:, cut]) + turned[:cells]
                misc_ref[:, cut] = turned[cells : cells + MISC]

            tiles(C, 128, place)
            traffic.send(u_ref, u_out)

        def lower(rows):
            lefts[0, rows, :] = low(u_ref[rows, :])

        tiles(cells, ROWS, lower)

        def first(cut):
            pre1[:, cut] = dot(lefts[0], wi[:, cut])

        tiles(C, TILE, first)
        traffic.send(pre1, pre1_out)

        def norm_act(source, norm, store):
            gain = misc_ref[3 * number + norm : 3 * number + norm + 1, :]
            bias = misc_ref[6 + 3 * number + norm : 7 + 3 * number + norm, :]

            def rows_of(rows):
                normal, _ = centered(source[rows, :])
                hidden = normal * gain + bias
                store(rows, hidden * sigmoid(hidden))

            tiles(cells, ROWS, rows_of)

        def keep_first(rows, value):
            work[rows, :] = value
            lefts[1, rows, :] = low(value)

        norm_act(pre1, 0, keep_first)

        def spread(i, carry):
            cut = pl.ds(pl.multiple_of(i * 128, 128), 128)
            value = work[:, cut]
            taps[:, pl.ds(pl.multiple_of(i * 128, 128), 128)] = low(beside(value, side, -1))
            taps[:, pl.ds(pl.multiple_of(C + i * 128, 128), 128)] = low(value)
            taps[:, pl.ds(pl.multiple_of(2 * C + i * 128, 128), 128)] = low(beside(value, side, 1))
            return carry

        lax.fori_loop(0, C // 128, spread, 0)
        zeros = jnp.zeros((PAD, TILE), jnp.float32)
        for ref in (above, below):
            ref[:PAD, :] = zeros
            ref[PAD + cells :, :] = zeros
        wait(middle_copies)

        def middle(cut):
            above[PAD : PAD + cells, :] = dot(taps[...], wm[0 : 3 * C, cut])
            below[PAD : PAD + cells, :] = dot(taps[...], wm[6 * C : 9 * C, cut])
            same = dot(taps[...], wm[3 * C : 6 * C, cut])
            pre2[:, cut] = same + above[PAD - side : PAD - side + cells, :] + below[PAD + side : PAD + side + cells, :]

        tiles(C, TILE, middle)
        traffic.send(pre2, pre2_out)

        def keep_second(rows, value):
            lefts[2, rows, :] = low(value)

        norm_act(pre2, 1, keep_second)
        if opening:
            traffic.send(lefts, lefts_out)
        wait(last_copies)
        traffic.send(wo, wo_out)

        def last(cut):
            pre3[:, cut] = dot(lefts[2], wo[:, cut])

        tiles(C, TILE, last)
        traffic.send(pre3, pre3_out)
        gain = misc_ref[3 * number + 2 : 3 * number + 3, :]
        bias = misc_ref[8 + 3 * number : 9 + 3 * number, :]

        def close(rows):
            normal, _ = centered(pre3[rows, :])
            total = u_ref[rows, :] + (normal * gain + bias)
            value = total * sigmoid(total)
            if opening:
                work[rows, :] = value
            else:
                lefts[3, rows, :] = low(value)

        tiles(cells, ROWS, close)
        if opening:
            half = side // 2

            def pool(cut):
                value = work[:, cut].reshape(half, 2, side, 128)
                pairs[...] = (value[:, 0] + value[:, 1]).reshape(half * side, 128)
                pooled_ref[:, cut] = 0.25 * (
                    pairs[pl.ds(0, half * half, 2), :] + pairs[pl.ds(1, half * half, 2), :]
                )

            tiles(C, 128, pool)
        else:
            traffic.send(lefts, lefts_out)
        traffic.finish()

    outs, out_specs = [], []
    if opening:
        outs += [shaped(MISC, C), shaped(cells // 4, C), shaped(cells, C)]
        out_specs += [IN, IN, ANY]
    outs += [shaped(n_lefts, cells, C, dtype=bf16)] + [shaped(cells, C)] * 3 + [shaped(C, C, dtype=bf16)] * 2
    out_specs += [ANY] * 6
    copies = w_first.copies + w_middle.copies + w_last.copies + 7
    scratch = [
        pltpu.VMEM((C, HEAD if opening else C), bf16),
        pltpu.VMEM((9 * C, C), bf16),
        pltpu.VMEM((C, C), bf16),
        pltpu.VMEM((cells, 3 * C), bf16),
        pltpu.VMEM((n_lefts, cells, C), bf16),
        pltpu.VMEM((cells + 2 * PAD, TILE), jnp.float32),
        pltpu.VMEM((cells + 2 * PAD, TILE), jnp.float32),
        pltpu.VMEM((cells, C), jnp.float32),
        pltpu.VMEM((cells // 2, 128), jnp.float32),
        pltpu.VMEM((cells, C), jnp.float32),
        pltpu.VMEM((cells, C), jnp.float32),
        pltpu.VMEM((cells, C), jnp.float32),
        pltpu.SemaphoreType.DMA((copies,)),
    ]
    if opening:
        scratch.append(pltpu.VMEM((cells, C), jnp.float32))
    weights = w_first.operands + w_middle.operands + w_last.operands
    return call(
        kernel,
        "forward_block",
        [table] + given + weights,
        [SMEM] + [IN] * given_count + [ANY] * len(weights),
        outs,
        out_specs,
        scratch,
        2 * cells * 11 * C * C,
        22 * C * C + 20 * cells * C,
    )


def readout(table, live, lefts, bias, cotangent, weights):
    cells, columns = cotangent.shape
    n_weights = len(weights.operands)
    bf16 = jnp.bfloat16
    cut_size = 512
    half = columns // 2

    def kernel(table_ref, live_ref, lefts_ref, bias_ref, cot_ref, *refs):
        refs = list(refs)
        sources = [refs.pop(0) for _ in range(n_weights)]
        output, grad_stream, grad_bias, own, other, matrix, low_ref, sems = refs
        traffic = Traffic(sems)
        given = traffic.begin(lefts_ref.at[3], low_ref)
        copies = traffic.load(weights, sources, table_ref, matrix)
        factor = wide(live_ref[0])
        core = table_ref[CORE]
        grad_stream[...] = jnp.zeros((cells, C), jnp.float32)
        given.wait()
        wait(copies)
        for part in range(2):

            def step(cut, part=part):
                here = pl.ds(pl.multiple_of(part * half + cut.start, cut_size), cut_size)
                logits = dot(low_ref[...], matrix[:, here]) + bias_ref[:, here]
                share = 0.5 * (1.0 + lax.erf(logits * (0.5**0.5)))
                output[:, here] = low(logits * share * factor)
                slope = share + logits * (jnp.exp(-0.5 * logits * logits) * (0.5 / jnp.pi) ** 0.5)
                grad_logits = low(wide(cot_ref[:, here]) * factor * slope)
                grad_bias[:, here] = jnp.sum(wide(grad_logits), axis=0, keepdims=True)

                @pl.when(core == part)
                def _():
                    own[:, cut] = grad_logits

                @pl.when(core != part)
                def _():
                    other[:, cut] = grad_logits

                grad_stream[...] += dot_rows(grad_logits, matrix[:, here])

            tiles(half, cut_size, step)

    outs = [shaped(cells, columns, dtype=bf16), shaped(cells, C), shaped(1, columns)]
    outs += [shaped(cells, half, dtype=bf16)] * 2
    scratch = [
        pltpu.VMEM((C, columns), bf16),
        pltpu.VMEM((cells, C), bf16),
        pltpu.SemaphoreType.DMA((weights.copies + 1,)),
    ]
    return call(
        kernel,
        "readout",
        [table, live, lefts, bias, cotangent] + weights.operands,
        [SMEM] * 2 + [ANY] + [IN] * 2 + [ANY] * n_weights,
        outs,
        [IN] * 5,
        scratch,
        4 * cells * C * columns,
        2 * C * columns + 4 * cells * columns,
    )


def back_last(table, number, side, grad_out, stream, pre3, pre2, misc, w_last):
    cells = side * side
    pooled = grad_out.shape[0] != cells
    n_weights = len(w_last.operands)
    bf16 = jnp.bfloat16
    half = C // 2

    def kernel(table_ref, grad_ref, u_in, pre3_in, pre2_in, misc_ref, *refs):
        refs = list(refs)
        sources = [refs.pop(0) for _ in range(n_weights)]
        direct_out, grads, other, sums, matrix, direct, u_ref, pre3_ref, pre2_ref, work, parts, pairs, sems = refs
        traffic = Traffic(sems)
        opened = [traffic.begin(u_in, u_ref), traffic.begin(pre3_in, pre3_ref)]
        later = traffic.begin(pre2_in, pre2_ref)
        copies = traffic.load(w_last, sources, table_ref, matrix)
        parts[...] = jnp.zeros_like(parts)
        gain = misc_ref[3 * number + 2 : 3 * number + 3, :]
        bias = misc_ref[8 + 3 * number : 9 + 3 * number, :]
        if pooled:

            def spread(cut):
                value = 0.25 * grad_ref[:, cut]
                pairs[pl.ds(0, cells // 4, 2), :] = value
                pairs[pl.ds(1, cells // 4, 2), :] = value
                twice = pairs[...].reshape(side // 2, 1, side, 128)
                work[:, cut] = jnp.broadcast_to(twice, (side // 2, 2, side, 128)).reshape(cells, 128)

            tiles(C, 128, spread)
        grad_from = work if pooled else grad_ref
        wait(opened)

        def close(rows):
            normal, scale = centered(pre3_ref[rows, :])
            total = u_ref[rows, :] + (normal * gain + bias)
            inner = grad_from[rows, :] * silu_back(total)
            direct[rows, :] = inner
            parts[0:8, :] += fold(inner * normal)
            parts[8:16, :] += fold(inner)
            grads[0, rows, :] = low(norm_back(inner, normal, scale, gain))

        tiles(cells, ROWS, close)
        traffic.send(direct, direct_out)
        gain = misc_ref[3 * number + 1 : 3 * number + 2, :]
        bias = misc_ref[7 + 3 * number : 8 + 3 * number, :]
        wait(copies)

        def last(cut):
            work[:, cut] = dot_rows(grads[0], matrix[cut, :])

        tiles(C, TILE, last)
        later.wait()

        def norm(rows):
            normal, scale = centered(pre2_ref[rows, :])
            hidden = normal * gain + bias
            inner = work[rows, :] * silu_back(hidden)
            parts[16:24, :] += fold(inner * normal)
            parts[24:32, :] += fold(inner)
            grads[1, rows, :] = low(norm_back(inner, normal, scale, gain))

        tiles(cells, ROWS, norm)
        sums[...] = jnp.sum(parts[...].reshape(4, 8, C), axis=1)
        there = pl.ds(pl.multiple_of((1 - table_ref[CORE]) * half, half), half)
        for i in range(2):
            other[i] = grads[i, :, there]
        traffic.finish()

    outs = [shaped(cells, C), shaped(2, cells, C, dtype=bf16), shaped(2, cells, half, dtype=bf16), shaped(4, C)]
    f32 = jnp.float32
    scratch = [pltpu.VMEM((C, C), bf16)] + [pltpu.VMEM((cells, C), f32)] * 5
    scratch += [pltpu.VMEM((32, C), f32), pltpu.VMEM((cells // 2, 128), f32), pltpu.SemaphoreType.DMA((w_last.copies + 4,))]
    return call(
        kernel,
        "back_last",
        [table, grad_out, stream, pre3, pre2, misc] + w_last.operands,
        [SMEM, IN, ANY, ANY, ANY, IN] + [ANY] * n_weights,
        outs,
        [ANY, IN, IN, IN],
        scratch,
        2 * cells * C * C,
        2 * C * C + 24 * cells * C,
    )


def weight_terms(table, middle, products, sides, out_blocks):
    bf16 = jnp.bfloat16
    if middle is not None:
        products = [(middle[1], 1, middle[2], middle[3], 1, middle[4], 1)] + products
    pair = products[0][2] is not None
    given = []
    for left, _, left_other, right, _, right_other, _ in products:
        given += [left, right] + ([left_other, right_other] if pair else [])
    n_given = len(given)
    n_outs = len(out_blocks.operands)
    width = out_blocks.operands[0].shape[-1]
    cells_of = [product[0].shape[-2] for product in products]
    factor = 2 if pair else 1
    heights = [C] * len(products)
    if middle is not None:
        heights[0] = 9 * C
    starts = [sum(heights[:i]) for i in range(len(heights) + 1)]
    grid_side = middle[0] if middle is not None else 0
    grid_cells = grid_side * grid_side
    size = 512

    def kernel(table_ref, *refs):
        refs = list(refs)
        sources = [refs.pop(0) for _ in range(n_given)]
        beside_refs = [refs.pop(0) for _ in range(len(sides) * factor)]
        targets = [refs.pop(0) for _ in range(n_outs)]
        grad, sems = refs.pop(0), refs.pop(0)
        traffic = Traffic(sems)
        waits = []
        for (_, left_at, _, _, right_at, _, other_at), cells in zip(products, cells_of):
            left, right = refs.pop(0), refs.pop(0)
            left_in, right_in = sources.pop(0), sources.pop(0)
            copies = [traffic.begin(left_in.at[left_at], left.at[pl.ds(0, cells), :])]
            if right_at is not None:
                right_in = right_in.at[right_at]
                if pair:
                    right_in = right_in.at[:, pl.ds(pl.multiple_of(table_ref[CORE] * width, width), width)]
            copies.append(traffic.begin(right_in, right.at[pl.ds(0, cells), :]))
            if pair:
                left_in, right_in = sources.pop(0), sources.pop(0)
                copies.append(traffic.begin(left_in.at[left_at], left.at[pl.ds(cells, cells), :]))
                if other_at is not None:
                    right_in = right_in.at[other_at]
                copies.append(traffic.begin(right_in, right.at[pl.ds(cells, cells), :]))
            waits.append((copies, left, right))
        at = 0
        for side in sides:
            extent = side[0].shape[-1]
            total = beside_refs.pop(0)[...]
            if pair:
                total = low(wide(total) + wide(beside_refs.pop(0)[...]))
            grad[starts[-1] :, at : at + extent] = total
            at += extent
        if sides:
            grad[starts[-1] :, at:] = jnp.zeros((C, width - at), bf16)
        if middle is not None:
            taps, shifted, padded = refs
            copies, act, right = waits[0]
            padded[:PAD, :] = jnp.zeros((PAD, 128), jnp.float32)
            padded[PAD + grid_cells :, :] = jnp.zeros((PAD, 128), jnp.float32)
            wait(copies)
            for first in range(0, factor * grid_cells, grid_cells):
                rows = slice(first, first + grid_cells)

                def spread(i, carry, rows=rows):
                    cut = pl.ds(pl.multiple_of(i * 128, 128), 128)
                    value = wide(act[rows, cut])
                    taps[rows, cut] = low(beside(value, grid_side, -1))
                    taps[rows, pl.ds(pl.multiple_of(C + i * 128, 128), 128)] = act[rows, cut]
                    taps[rows, pl.ds(pl.multiple_of(2 * C + i * 128, 128), 128)] = low(beside(value, grid_side, 1))
                    return carry

                def shift(i, carry, rows=rows):
                    cut = pl.ds(pl.multiple_of(i * 128, 128), 128)
                    padded[PAD : PAD + grid_cells, :] = wide(right[rows, cut])
                    shifted[0, rows, cut] = low(padded[PAD + grid_side : PAD + grid_side + grid_cells, :])
                    shifted[1, rows, cut] = right[rows, cut]
                    shifted[2, rows, cut] = low(padded[PAD - grid_side : PAD - grid_side + grid_cells, :])
                    return carry

                lax.fori_loop(0, C // 128, spread, 0)
                lax.fori_loop(0, width // 128, shift, 0)
            stage = 3 * C // size
            out_copies = traffic.plan(out_blocks, targets, table_ref, grad)
            ends = out_blocks.ends(table_ref)

            def part(i, carry):
                cut = pl.ds(pl.multiple_of(lax.rem(i, stage) * size, size), size)
                target = pl.ds(pl.multiple_of(i * size, size), size)
                grad[target, :] = low(dot_sums(taps[:, cut], shifted[i // stage]))

                @pl.when(lax.rem(i, stage) == stage - 1)
                def _():
                    ready = (i + 1) * size
                    for copy, end in zip(out_copies, ends):

                        @pl.when((end <= ready) & (end > ready - 3 * C))
                        def _(copy=copy):
                            copy.start()

                return carry

            lax.fori_loop(0, 9 * C // size, part, 0)
        for number, (copies, left, right) in enumerate(waits):
            if middle is not None and number == 0:
                continue
            wait(copies)

            def part(cut, number=number, left=left, right=right):
                target = pl.ds(pl.multiple_of(starts[number] + cut.start, TILE), TILE)
                grad[target, :] = low(dot_sums(left[:, cut], right[...]))

            tiles(C, TILE, part)
        if middle is None:
            traffic.store(out_blocks, targets, table_ref, grad)
        traffic.finish()

    outs = [shaped(*array.shape, dtype=bf16) for array in out_blocks.operands]
    scratch = [
        pltpu.VMEM((starts[-1] + (C if sides else 0), width), bf16),
        pltpu.SemaphoreType.DMA((out_blocks.copies + 4 * len(products),)),
    ]
    for cells in cells_of:
        scratch += [pltpu.VMEM((factor * cells, C), bf16), pltpu.VMEM((factor * cells, width), bf16)]
    if middle is not None:
        scratch += [
            pltpu.VMEM((factor * grid_cells, 3 * C), bf16),
            pltpu.VMEM((3, factor * grid_cells, width), bf16),
            pltpu.VMEM((grid_cells + 2 * PAD, 128), jnp.float32),
        ]
    besides = [array for side in sides for array in side if array is not None]
    return call(
        kernel,
        "weight_terms",
        [table] + given + besides,
        [SMEM] + [ANY] * n_given + [IN] * len(besides),
        outs,
        [ANY] * n_outs,
        scratch,
        sum(2 * factor * cells * height * width for cells, height in zip(cells_of, heights)),
        2 * starts[-1] * width + sum(4 * factor * cells * C for cells in cells_of),
    )


def plane_terms(table, side, acts, grads, block_rows):
    cells = side * side
    total = sum(array.shape[0] for array in acts)
    bf16 = jnp.bfloat16
    blocks = 4
    span = 3 * 128

    def kernel(table_ref, *refs):
        refs = list(refs)
        act_refs = [refs.pop(0) for _ in acts]
        grad_refs = [refs.pop(0) for _ in grads]
        target, act, right, taps, terms, sems = refs
        traffic = Traffic(sems)
        copies, row = [], 0
        for source, other in zip(act_refs, grad_refs):
            rows = pl.ds(row, source.shape[0])
            copies += [traffic.begin(source, act.at[rows, :]), traffic.begin(other, right.at[rows, :])]
            row += source.shape[0]
        index = lax.broadcasted_iota(jnp.int32, (total, 128), 0).astype(jnp.float32)
        inside = index - cells * jnp.floor((index + 0.5) * (1.0 / cells))
        line = jnp.floor((inside + 0.5) * (1.0 / side))
        column = inside - side * line
        wait(copies)
        for block in range(blocks):
            for tile in range(3):
                at = WINDOWS + blocks + 4 * (3 * block + tile)
                cut = pl.ds(pl.multiple_of(table_ref[at], 128), 128)
                value = pltpu.roll(wide(act[:, cut]), table_ref[at + 1], 0)
                tap_line = line + (table_ref[at + 2] - 1).astype(jnp.float32)
                tap_column = column + (table_ref[at + 3] - 1).astype(jnp.float32)
                there = (tap_line >= 0) & (tap_line < side) & (tap_column >= 0) & (tap_column < side)
                first = block * span + tile * 128
                taps[:, first : first + 128] = low(jnp.where(there, value, 0.0))
            terms[block] = low(dot_sums(taps[:, block * span : (block + 1) * span], right[...]))
            start_row = pl.multiple_of(table_ref[WINDOWS + block], 32)
            traffic.send(terms.at[block, pl.ds(start_row, block_rows), :], target.at[block])
        traffic.finish()

    return call(
        kernel,
        "plane_terms",
        [table] + acts + grads,
        [SMEM] + [ANY] * (2 * len(acts)),
        shaped(blocks, block_rows, C, dtype=bf16),
        ANY,
        [
            pltpu.VMEM((total, C), bf16),
            pltpu.VMEM((total, C), bf16),
            pltpu.VMEM((total, blocks * span), bf16),
            pltpu.VMEM((blocks, span, C), bf16),
            pltpu.SemaphoreType.DMA((2 * len(acts) + blocks,)),
        ],
        2 * total * blocks * span * C,
        4 * total * C + 2 * blocks * block_rows * C,
    )


def back_first(table, number, side, grads, pre1, direct, misc, rests, w_middle, w_first):
    cells = side * side
    closing = rests is not None
    n_middle, n_first = len(w_middle.operands), len(w_first.operands)
    bf16 = jnp.bfloat16
    extra = rests if closing else []
    half = C // 2
    side_half = SIDE

    def kernel(table_ref, grads_in, pre1_in, direct_in, misc_ref, *refs):
        refs = list(refs)
        rest_refs = [refs.pop(0) for _ in extra]
        middles = [refs.pop(0) for _ in range(n_middle)]
        firsts = [refs.pop(0) for _ in range(n_first)]
        grad_u, sums, grad_pre1, other = [refs.pop(0) for _ in range(4)]
        turned = [refs.pop(0), refs.pop(0)] if closing else None
        wm, wi, grad_ref, pre1_ref, direct_ref, taps, above, work, parts, sems = refs
        traffic = Traffic(sems)
        given = traffic.begin(grads_in.at[1], grad_ref)
        middle_copies = traffic.plan_in(w_middle, middles, table_ref, wm)
        stages = [lax.div(first, 3 * C) for first in w_middle.firsts(table_ref)]

        def of_stage(stage, act):
            for copy, own in zip(middle_copies, stages):

                @pl.when(own == stage)
                def _(copy=copy):
                    act(copy)

        for stage in range(3):
            of_stage(stage, lambda copy: copy.start())
        pre1_copy = traffic.begin(pre1_in, pre1_ref)
        first_copies = traffic.load(w_first, firsts, table_ref, wi)
        direct_copy = traffic.begin(direct_in, direct_ref)
        parts[...] = jnp.zeros_like(parts)
        zeros = jnp.zeros((PAD, TILE), jnp.float32)
        above[:PAD, :] = zeros
        above[PAD + cells :, :] = zeros
        given.wait()

        def spread(i, carry):
            cut = pl.ds(pl.multiple_of(i * 128, 128), 128)
            value = wide(grad_ref[:, cut])
            taps[:, cut] = low(beside(value, side, 1))
            taps[:, pl.ds(pl.multiple_of(C + i * 128, 128), 128)] = grad_ref[:, cut]
            taps[:, pl.ds(pl.multiple_of(2 * C + i * 128, 128), 128)] = low(beside(value, side, -1))
            return carry

        lax.fori_loop(0, C // 128, spread, 0)
        for tap in range(3):
            of_stage(tap, lambda copy: copy.wait())

            def middle(i, carry, tap=tap):
                cut = pl.ds(pl.multiple_of(i * TILE, TILE), TILE)
                total = None
                for column in range(3):
                    source = pl.ds(pl.multiple_of((3 * tap + column) * C + i * TILE, TILE), TILE)
                    term = dot_rows(taps[:, column * C : (column + 1) * C], wm[source, :])
                    total = term if total is None else total + term
                if tap == 1:
                    work[:, cut] += total
                else:
                    shift = side if tap == 0 else -side
                    above[PAD : PAD + cells, :] = total
                    moved = above[PAD + shift : PAD + shift + cells, :]
                    if tap == 0:
                        work[:, cut] = moved
                    else:
                        work[:, cut] += moved
                return carry

            lax.fori_loop(0, C // TILE, middle, 0)
        gain = misc_ref[3 * number : 3 * number + 1, :]
        bias = misc_ref[6 + 3 * number : 7 + 3 * number, :]
        pre1_copy.wait()

        def norm(rows):
            normal, scale = centered(pre1_ref[rows, :])
            hidden = normal * gain + bias
            inner = work[rows, :] * silu_back(hidden)
            parts[0:8, :] += fold(inner * normal)
            parts[8:16, :] += fold(inner)
            grad_pre1[0, rows, :] = low(norm_back(inner, normal, scale, gain))

        tiles(cells, ROWS, norm)
        sums[...] = jnp.sum(parts[...].reshape(2, 8, C), axis=1)
        core = table_ref[CORE]
        other[...] = grad_pre1[0, :, pl.ds(pl.multiple_of((1 - core) * half, half), half)]
        wait(first_copies)
        direct_copy.wait()

        def first(cut):
            grad_u[:, cut] = direct_ref[:, cut] + dot_rows(grad_pre1[0], wi[cut, :])

        tiles(C, TILE, first)
        if closing:

            last_0, first_1, last_1, bias_grad = rest_refs

            def turn(cut):
                stacked = jnp.concatenate(
                    [grad_u[:, cut]]
                    + [ref[row : row + 1, cut] for ref, row in ((sums, 0), (last_0, 2), (last_0, 0))]
                    + [ref[row : row + 1, cut] for ref, row in ((first_1, 0), (last_1, 2), (last_1, 0))]
                    + [ref[row : row + 1, cut] for ref, row in ((sums, 1), (last_0, 3), (last_0, 1))]
                    + [ref[row : row + 1, cut] for ref, row in ((first_1, 1), (last_1, 3), (last_1, 1))]
                    + [bias_grad[:, cut], jnp.zeros((2 * side_half - cells - MISC, 128), jnp.float32)]
                )
                parts_of = low(jnp.transpose(stacked))
                for part in range(2):
                    piece = parts_of[:, part * side_half : (part + 1) * side_half]

                    @pl.when(core == part)
                    def _(piece=piece):
                        turned[0][cut, :] = piece

                    @pl.when(core != part)
                    def _(piece=piece):
                        turned[1][cut, :] = piece

            tiles(C, 128, turn)

    outs = [shaped(cells, C), shaped(2, C), shaped(1, cells, C, dtype=bf16), shaped(cells, half, dtype=bf16)]
    if closing:
        outs += [shaped(C, side_half, dtype=bf16)] * 2
    f32 = jnp.float32
    scratch = [
        pltpu.VMEM((9 * C, C), bf16),
        pltpu.VMEM((C, C), bf16),
        pltpu.VMEM((cells, C), bf16),
        pltpu.VMEM((cells, C), f32),
        pltpu.VMEM((cells, C), f32),
        pltpu.VMEM((cells, 3 * C), bf16),
        pltpu.VMEM((cells + 2 * PAD, TILE), f32),
        pltpu.VMEM((cells, C), f32),
        pltpu.VMEM((16, C), f32),
        pltpu.SemaphoreType.DMA((w_middle.copies + w_first.copies + 3,)),
    ]
    weights = w_middle.operands + w_first.operands
    return call(
        kernel,
        "back_first",
        [table, grads, pre1, direct, misc] + extra + weights,
        [SMEM] + [ANY] * 3 + [IN] * (1 + len(extra)) + [ANY] * len(weights),
        outs,
        [IN] * len(outs),
        scratch,
        2 * cells * 10 * C * C,
        20 * C * C + 24 * cells * C,
    )


def place_halves(core, pair, rest=None):
    _, rows, half = pair[0].shape
    extra = [] if rest is None else [rest]

    def kernel(core_ref, mine, other, *refs):
        target = refs[-1]
        for part in range(2):

            @pl.when(core_ref[0] == part)
            def _(part=part):
                target[0, :, part * half : (part + 1) * half] = mine[0]
                target[0, :, (1 - part) * half : (2 - part) * half] = other[0]

        if extra:
            target[1] = wide(refs[0][0])

    return call(
        kernel,
        "place_halves",
        [core, *pair] + extra,
        [SMEM] + [IN] * (2 + len(extra)),
        shaped(1 + len(extra), rows, 2 * half),
        IN,
        [],
        0,
        16 * rows * half,
    )


def place_last(core, mine, other, cells):
    _, rows, half = mine.shape

    def kernel(core_ref, mine_ref, other_ref, first, last, pos, gains, biases, bias, side):
        for part in range(2):

            @pl.when(core_ref[0] == part)
            def _(part=part):
                for target, block, number in ((last, 0, 0), (first, 1, 1), (last, 1, 2), (first, 0, 3)):
                    target[block, :, part * half : (part + 1) * half] = mine_ref[number]
                    target[block, :, (1 - part) * half : (2 - part) * half] = other_ref[number]
                side[:, part * SIDE : (part + 1) * SIDE] = mine_ref[4, :, :SIDE]
                side[:, (1 - part) * SIDE : (2 - part) * SIDE] = other_ref[4, :, :SIDE]

        pos[...] = side[:, :cells]
        turned = jnp.transpose(side[...])
        for number in range(6):
            gains[number % 3, number // 3 : number // 3 + 1, :] = turned[cells + number : cells + number + 1]
            biases[number % 3, number // 3 : number // 3 + 1, :] = turned[cells + 6 + number : cells + 7 + number]
        bias[...] = turned[cells + 12 : cells + MISC]

    return call(
        kernel,
        "place_last",
        [core, mine, other],
        [SMEM, IN, IN],
        [shaped(2, rows, 2 * half)] * 2 + [shaped(rows, cells)] + [shaped(3, 2, rows)] * 2 + [shaped(4, rows)],
        [IN] * 6,
        [pltpu.VMEM((rows, 2 * SIDE), jnp.float32)],
        0,
        32 * rows * half * 5,
    )


def after(value, *earlier):
    return lax.optimization_barrier((value, earlier))[0]


class Movement:
    def __init__(self, mesh):
        self.dp = mesh.shape["dp"]
        self.cores = mesh.shape["fsdp"]
        self.line = self.dp // PLANE
        self.devices = self.dp * self.cores
        self.ring = [0] + list(range(1, self.line, 2)) + list(range(2, self.line, 2))[::-1]
        self.paired = self.cores == 2 and self.line == 4

    def flip(self, value, bits):
        return lax.ppermute(value, "dp", [(i, i ^ bits) for i in range(self.dp)])

    def along(self, value):
        pairs = []
        for position, level in enumerate(self.ring):
            following = self.ring[(position + 1) % self.line]
            pairs += [(level * PLANE + near, following * PLANE + near) for near in range(PLANE)]
        return lax.ppermute(value, "dp", pairs)

    def swap(self, value):
        return lax.ppermute(value, "fsdp", [(0, 1), (1, 0)])

    def lines(self):
        return [[level * PLANE + near for level in range(self.line)] for near in range(PLANE)]

    def table(self):
        if not self.paired:
            return jnp.zeros((TABLE,), jnp.int32)
        steps, chips = range(self.line), range(PLANE)
        halves = [(1, 0), (1, 1), (3, 0), (3, 1), (2, 2), (2, 3), (3, 2), (3, 3), (1, 2), (1, 3), (2, 0), (2, 1)]
        halves += [(0, step) for step in steps]
        rows = []
        for device in range(self.devices):
            chip, core = divmod(device, 2)
            level, near = divmod(chip, PLANE)
            position = self.ring.index(level)

            def chip_at(far, level, near=near):
                return level * PLANE + (near ^ far)

            def step_at(step, position=position):
                return self.ring[(position + step) % self.line]

            row = [chip_at(far, step_at(-step)) * 2 + (core + k) % 2 for k in range(2) for far in chips for step in steps]
            row += [chip_at(far, step) * 2 + (core + k) % 2 for k in range(2) for far in chips for step in steps]
            row += [chip_at(far, step_at(step)) for far, step in halves]
            row += [chip_at(far, step) for far, step in halves]
            row += [chip_at(far, step_at(step)) for step in reversed(steps) for far in chips]
            row.append(core)
            firsts = [chip_at(0, step) * 2 + core for step in steps]
            firsts = [9 * C // self.devices * owner for owner in firsts]
            row += [first % 128 for first in firsts]
            side = G // 2
            for first in firsts:
                for tile in range(first // 128, first // 128 + 3):
                    tap, part = divmod(tile, C // 128)
                    tap_row, tap_column = divmod(tap, 3)
                    away = (tap_row - 1) * side + tap_column - 1
                    row += [128 * part, -away % (2 * PLANE * side * side), tap_row, tap_column]
            rows.append(row)
        index = lax.axis_index("dp") * self.cores + lax.axis_index("fsdp")
        return lax.dynamic_index_in_dim(jnp.asarray(np.array(rows, np.int32)), index, 0, keepdims=False)


class Piece:
    def __init__(self, move, own, name):
        self.move = move
        self.own = own
        self.name = name
        self.rows = own.shape[0]
        self.at = STEPS
        self.found = []

    def keep(self, array, far, steps, first=0, other=None):
        for i, step in enumerate(steps):
            for core, held in enumerate((array, other)):
                self.found.append((held, first + i * self.rows, self.at + 16 * core + 4 * far + step))

    def line(self, second=(), third=(), first=()):
        with jax.named_scope(self.name + "_line"):
            one = self.move.along(after(self.own, *first) if first else self.own)
            two = self.move.along(after(one, *second) if second else one)
            three = self.move.along(after(two, *third) if third else two)
        self.passed = (one, two, three)
        self.held = jnp.concatenate([self.own, one, two, three])

    def levels(self, *earlier):
        with jax.named_scope(self.name + "_levels"):
            own = after(self.own, *earlier) if earlier else self.own
            self.held = lax.all_gather(own, "dp", axis_index_groups=self.move.lines(), axis=0, tiled=True)
        self.at = LEVELS

    def settle_line(self, *earlier):
        with jax.named_scope("swap"):
            other = self.move.swap(after(self.held, *earlier) if earlier else self.held)
        self.keep(self.held, 0, range(4), other=other)

    def plane_first(self, *earlier):
        half = self.rows // 2
        own = after(self.own, *earlier) if earlier else self.own
        with jax.named_scope(self.name + "_plane"):
            first, second = self.sides = self.move.flip(own, 1), self.move.flip(own, 2)
            self.fars = (self.move.flip(first[:half], 2), self.move.flip(second[half:], 1))
            self.passed = (jnp.concatenate([self.own, first, second, *self.fars]),)

    def pass_on(self, *earlier):
        with jax.named_scope(self.name + "_line"):
            self.passed += (self.move.along(after(self.passed[-1], *earlier)),)

    def end_line(self, *earlier):
        for step, array in enumerate(after(self.passed, *earlier)):
            other = self.move.swap(array)
            for far in range(PLANE):
                self.keep(array, far, [step], first=far * self.rows, other=other)


def cross(move, pieces, fars, *earlier):
    over_first = [piece.held for piece in pieces] + [piece.second[2 * piece.rows : 4 * piece.rows] for piece in fars]
    over_second = [piece.held for piece in pieces] + [piece.first[: 2 * piece.rows] for piece in fars]
    over_first, over_second = [jnp.concatenate(parts) if len(parts) > 1 else parts[0] for parts in (over_first, over_second)]
    if earlier:
        over_first, over_second = after((over_first, over_second), *earlier)
    with jax.named_scope("_".join(piece.name for piece in pieces + fars) + "_plane"):
        first, second = move.flip(over_first, 1), move.flip(over_second, 2)
    row = 0
    for piece in pieces:
        piece.sides = (first, second, row)
        piece.first = first[row : row + 4 * piece.rows]
        piece.second = second[row : row + 4 * piece.rows]
        row += 4 * piece.rows
    for piece in fars:
        piece.far_sides = (first, second, row)
        piece.far_first = first
        row += 2 * piece.rows
    return first, second


def settle(move, pieces, fars, *earlier):
    first, second = (pieces[0].sides if pieces else fars[0].far_sides)[:2]
    if earlier:
        first, second = after((first, second), *earlier)
    with jax.named_scope("swap"):
        first_other, second_other = move.swap(first), move.swap(second)
    for piece in pieces:
        row = piece.sides[2]
        piece.first = first[row : row + 4 * piece.rows]
        piece.second = second[row : row + 4 * piece.rows]
        piece.keep(first, 1, range(4), first=row, other=first_other)
        piece.keep(second, 2, range(4), first=row, other=second_other)
    for piece in fars:
        row = piece.far_sides[2]
        piece.keep(first, 3, (2, 3), first=row, other=first_other)
        piece.keep(second, 3, (0, 1), first=row, other=second_other)


class Spread:
    def __init__(self, move, own, *earlier):
        self.move = move
        self.own = after(own, *earlier) if earlier else own
        with jax.named_scope("spread"):
            self.sides = tuple(move.flip(self.own, bits) for bits in (1, 2, 3))

    def end(self, *earlier):
        with jax.named_scope("spread_swap"):
            here = jnp.concatenate(after((self.own, *self.sides), *earlier))
            self.all = [here, self.move.swap(here)]


class Sum:
    def __init__(self, move, arrays, name, levels=False):
        self.move = move
        self.arrays = arrays
        self.name = name
        self.levels = levels

    def across(self, *earlier):
        first, second = after(tuple(self.arrays[:2]), *earlier) if earlier else self.arrays[:2]
        with jax.named_scope(self.name + "_across"):
            self.first = self.move.flip(first, 1)
            self.second = self.move.flip(second, 2)
        return self.first, self.second

    def prepare(self, *earlier):
        self.first, self.second = after((self.first, self.second), *earlier)
        with jax.named_scope(self.name + "_onward"):
            self.rests = (
                low(wide(self.arrays[2]) + wide(self.second[2:])),
                low(wide(self.arrays[3]) + wide(self.first[2:])),
            )
        self.operands = self.rests
        return self.rests

    def onward(self, *earlier):
        rests = after(self.rests, *earlier) if earlier else self.rests
        with jax.named_scope(self.name + "_onward"):
            self.rests = (self.move.flip(rests[0], 1), self.move.flip(rests[1], 2))

    def gather(self, *earlier):
        rests = after(self.rests, *earlier) if earlier else self.rests
        with jax.named_scope(self.name + "_held"):
            held = self.arrays[4]
            self.near = wide(held[:2]) + wide(self.first[:2]) + wide(rests[1])
            self.far = wide(held[2:]) + wide(self.second[:2]) + wide(rests[0])
            if self.levels:
                held = jnp.concatenate([low(self.near), low(self.far)])
                self.held = held.reshape(-1, held.shape[-1])
                return self.held
            self.far = (self.far[0], low(self.far[1]))
            return self.far

    def finish(self, *earlier):
        with jax.named_scope(self.name + "_line"):
            if self.levels:
                lines = self.move.lines()
                owned = lax.psum_scatter(self.held, "dp", axis_index_groups=lines, scatter_dimension=0, tiled=True)
                self.owned = wide(owned)
            else:
                three = self.move.along(self.far[1])
                two = self.move.along(low(self.far[0] + wide(three)))
                two = after(two, *earlier) if earlier else two
                one = self.move.along(low(self.near[1] + wide(two)))
                self.passed = (three, two, one)
                self.owned = self.near[0] + wide(one)


class LineSum:
    def __init__(self, move, arrays, name):
        self.move = move
        self.arrays = arrays
        self.name = name
        self.next = arrays[0]

    def line(self, step, *earlier):
        value = after(self.next, *earlier) if earlier else self.next
        with jax.named_scope(f"{self.name}_line{step}"):
            self.sent = self.move.along(value)

    def prepare(self, step, *earlier):
        with jax.named_scope(f"{self.name}_line{step}"):
            sent = after(self.sent, *earlier) if earlier else self.sent
            self.next = low(wide(self.arrays[step]) + wide(sent))
        return self.next

    def prepare_across(self, *earlier):
        sent = after(self.sent, *earlier) if earlier else self.sent
        with jax.named_scope(self.name + "_across"):
            held = wide(self.arrays[3]) + wide(sent)
            half = held.shape[1] // 2
            self.near, self.rest = held[:, :half], held[:, half:]
            self.operands = (low(self.near[1::2]), low(self.rest[2:]))
        return self.operands

    def across(self, *earlier):
        operands = after(self.operands, *earlier) if earlier else self.operands
        with jax.named_scope(self.name + "_across"):
            self.first = self.move.flip(operands[0], 1)
            self.second = self.move.flip(operands[1], 2)

    def prepare_onward(self, *earlier):
        self.first, self.second = after((self.first, self.second), *earlier) if earlier else (self.first, self.second)
        with jax.named_scope(self.name + "_onward"):
            self.operands = (low(self.rest[1] + wide(self.second[1])), low(self.near[2] + wide(self.first[1])))
        return self.operands

    def finish(self, *earlier):
        operands = after(self.operands, *earlier) if earlier else self.operands
        with jax.named_scope(self.name + "_onward"):
            first_rest = self.move.flip(operands[0], 1)
            second_rest = self.move.flip(operands[1], 2)
            near = self.near[0] + wide(self.first[0]) + wide(second_rest)
            rest = self.rest[0] + wide(self.second[0]) + wide(first_rest)
            self.owned = jnp.concatenate([near, rest])


def whole_matrix(array):
    blocks = Blocks()
    blocks.add(array, None, 0, 0, None, 0, 0, 0, *array.shape)
    return blocks


def halves(move, owned, matrices):
    blocks = owned.reshape(matrices, 2, -1, owned.shape[-1])
    core = lax.axis_index("fsdp")
    mine = lax.dynamic_index_in_dim(blocks, core, 1, keepdims=False)
    return mine, move.swap(lax.dynamic_index_in_dim(blocks, 1 - core, 1, keepdims=False))


def local(
    move,
    features,
    grid_live,
    pos_embed,
    w_in,
    w_mid,
    w_out,
    norm_gain,
    norm_bias,
    readout_w,
    readout_b,
    cotangent,
):
    rows, middle_rows, width = w_in.shape[1], w_mid.shape[1], readout_w.shape[1]
    cells = pos_embed.shape[0]
    half_side = G // 2
    paired = move.paired
    scales = [norm_gain.reshape(6, rows).T, norm_bias.reshape(6, rows).T, readout_b.reshape(rows, 4)]
    beside = jnp.concatenate([pos_embed.T, *scales, jnp.zeros((rows, C - cells - MISC), jnp.bfloat16)], axis=1)
    if paired:
        cut = middle_rows // 2
        stacks = [
            [w_in[0], beside, w_out[0]],
            [w_mid[0, :cut]],
            [w_mid[0, cut:], w_in[1], w_out[1]],
            [w_mid[1]],
            [readout_w[:, i * C : (i + 1) * C] for i in range(width // C)],
        ]
        one, two, three, four, top = [
            Piece(move, jnp.concatenate(stack) if len(stack) > 1 else stack[0], name)
            for stack, name in zip(stacks, ("one", "two", "three", "four", "top"))
        ]
        one.line()
        top.plane_first(one.passed[0])
        two.line(one.passed[1:2], one.passed[2:])
        three.line(two.passed[1:2], two.passed[2:])
        four.line(first=three.passed[2:])
        cross(move, [one], [], *top.fars)
        cross(move, [two], [one], one.first)
        one.settle_line(one.first)
        settle(move, [one], [], one.first)
        cross(move, [three], [two], two.first)
        two.settle_line(two.first)
        settle(move, [two], [one], two.first)
        top.pass_on(four.passed[1])
        cross(move, [], [three], three.first, four.held)
        three.settle_line(three.first)
        settle(move, [three], [two], three.first)
        cross(move, [four], [], three.far_first)
        top.pass_on(three.far_first)
        settle(move, [], [three], three.far_first, top.passed[1])
        lies = {
            "head_0": [(one, 0, rows, 0, 0, C), (one, rows, rows, 0, C, HEAD - C)],
            "middle_0": [(two, 0, cut, 0, 0, C), (three, 0, cut, cut, 0, C)],
            "last_0": [(one, 2 * rows, rows, 0, 0, C)],
            "first_1": [(three, cut, rows, 0, 0, C)],
            "last_1": [(three, cut + rows, rows, 0, 0, C)],
            "middle_1": [(four, 0, middle_rows, 0, 0, C)],
            "readout": [(top, i * rows, rows, 0, i * C, C) for i in range(width // C)],
        }
    else:

        def whole(own):
            return lax.all_gather(own, ("dp", "fsdp"), axis=0, tiled=True)

        first_all = whole(w_in[0])
        lies = {
            "head_0": [(first_all, 0), (whole(beside[:, : HEAD - C]), C)],
            "middle_0": [(whole(w_mid[0]), 0)],
            "last_0": [(whole(w_out[0]), 0)],
            "first_1": [(whole(w_in[1]), 0)],
            "last_1": [(whole(w_out[1]), 0)],
            "middle_1": [(whole(w_mid[1]), 0)],
            "readout": [(whole(readout_w), 0)],
        }

    def matrix(name):
        blocks = Blocks()
        if not paired:
            for array, column in lies[name]:
                blocks.add(array, None, 0, 0, None, 0, 0, column, *array.shape)
            return blocks
        stride = middle_rows if name.startswith("middle") else rows
        for piece, row, extent, to_row, to_column, columns in lies[name]:
            for array, first, place in piece.found:
                blocks.add(array, None, first + row, 0, place, stride, to_row, to_column, extent, columns)
        return blocks

    def sums_of(columns, matrices, pieces=((None, STEPPED),)):
        blocks = Blocks()
        if not paired:
            extent = sum(matrices) * move.devices
            blocks.add(shaped(1, extent, columns), 0, 0, 0, None, 0, 0, 0, extent, columns)
            return blocks
        runs, start = [], 0
        for block_rows in matrices:
            runs.append((start, 2 * block_rows, 0))
            start += move.devices * block_rows
        for cut, kind in pieces:
            taken = []
            while runs and cut != 0:
                start, stride, first = runs.pop(0)
                extent = stride - first if cut is None else min(cut, stride - first)
                taken.append((start + first, stride, extent))
                if first + extent < stride:
                    runs.insert(0, (start, stride, first + extent))
                cut = None if cut is None else cut - extent
            place = {STEPPED: OUT_STEPS, LEVELED: OUT_LEVELS, LINED: OUT_LINE}[kind]
            for count in (4, 4, 4, 4) if kind == LINED else (4, 4, 2, 2, 4):
                array = shaped(count, sum(extent for _, _, extent in taken), columns)
                for block in range(count):
                    row = 0
                    for first, stride, extent in taken:
                        blocks.add(array, block, row, 0, place, stride, first, 0, extent, columns)
                        row += extent
                    place += 1
        return blocks

    def swap(value):
        return move.swap(value) if paired else None

    def tie(value, *earlier):
        return after(value, *earlier) if paired else value

    def scattered(terms, matrices=1):
        total = wide(terms[0][0]).reshape(matrices, -1, terms[0].shape[-1])
        return lax.psum_scatter(total, ("dp", "fsdp"), scatter_dimension=1, tiled=True)

    half = 2 if paired else 1
    table = move.table()
    mid_0, last_0 = matrix("middle_0"), matrix("last_0")
    misc, pooled, stream_in, lefts_0, pre1_0, pre2_0, pre3_0, first_0, last_0 = forward_block(
        table, 0, G, None, features[0], None, matrix("head_0"), mid_0, last_0
    )
    lefts_other_0 = swap(lefts_0)
    if paired:
        settle(move, [four], [], pooled)
        cross(move, [], [four], top.passed[2])
        top.pass_on(pooled)
        four.settle_line(pooled)
        settle(move, [], [four])
    readout_bias = misc[12:].T.reshape(1, width)
    first_1, mid_1, last_1 = matrix("first_1"), matrix("middle_1"), matrix("last_1")
    if paired:
        top.end_line(pooled)
        pooled = tie(pooled, top.passed[3], readout_bias)
    lefts_1, pre1_1, pre2_1, pre3_1, first_1, last_1 = forward_block(
        table, 1, half_side, pooled, None, misc, first_1, mid_1, last_1
    )
    first_0, last_0, first_1, last_1 = [whole_matrix(array) for array in (first_0, last_0, first_1, last_1)]
    lefts_other_1 = swap(lefts_1)
    output, grad_top, grad_readout_b, grad_logits, grad_logits_other = readout(
        table, grid_live, tie(lefts_1, lefts_other_0), readout_bias, cotangent[0], matrix("readout")
    )
    if paired:
        acts = Spread(move, lefts_1[1])
        grad_logits_other = swap(after(grad_logits_other, *acts.sides))
        grad_top = after(grad_top, *acts.sides)
    else:
        grad_logits, grad_logits_other = jnp.concatenate([grad_logits, grad_logits_other], axis=1), None
    direct_1, grads_1, grads_other_1, sums_1 = back_last(
        table, 1, half_side, grad_top, pooled, pre3_1, pre2_1, misc, last_1
    )
    if paired:
        grads_other_1 = tie(grads_other_1, grad_logits_other)
    grads_other_1 = swap(grads_other_1)
    readout_terms = weight_terms(
        table,
        None,
        [(lefts_1, 3, lefts_other_1, tie(grad_logits, sums_1), None, grad_logits_other, None)],
        [],
        sums_of(width // half, [rows], [(None, LEVELED)]),
    )
    if paired:
        sum_readout = Sum(move, readout_terms, "readout", levels=True)
        spread = Spread(move, grads_1[1], *readout_terms)
        sum_readout.across(grads_other_1)
        grads_1 = tie(grads_1, *readout_terms, grads_other_1)
    else:
        middle_terms_1 = weight_terms(
            table,
            (half_side, lefts_1, lefts_other_1, grads_1, grads_other_1),
            [],
            [],
            sums_of(C // half, [middle_rows]),
        )
    grad_pooled, sums_first_1, grad_first_1, grad_first_other_1 = back_first(
        table, 1, half_side, grads_1, pre1_1, direct_1, misc, None, mid_1, first_1
    )
    direct_0, grads_0, grads_other_0, sums_0 = back_last(
        table, 0, G, grad_pooled, stream_in, pre3_0, pre2_0, misc, last_0
    )
    if paired:
        waited = [*sum_readout.prepare(sums_0), *after(spread.sides, sums_0)]
        lefts_other_0 = tie(lefts_other_0, *waited)
        grads_other_0, grad_first_other_1 = after((grads_other_0, grad_first_other_1), *waited)
        spread.end(*waited)
        acts.end(*waited)
        sum_readout.onward(*waited)
    grads_other_0, grad_first_other_1 = swap(grads_other_0), swap(grad_first_other_1)
    crossed_terms = weight_terms(
        table,
        (G, lefts_0, lefts_other_0, grads_0, grads_other_0),
        [],
        [],
        sums_of(C // half, [middle_rows]),
    )
    if paired:
        sum_middle_0 = Sum(move, crossed_terms, "middle_0")
        waited = [sum_readout.gather(*crossed_terms), *after((*spread.all, *acts.all), *crossed_terms)]
        sum_readout.finish()
        sum_middle_0.across(*waited)
        acts.all[0] = tie(acts.all[0], *waited)
        middle_terms_1 = plane_terms(table, half_side, acts.all, spread.all, middle_rows)
        grads_0 = tie(grads_0, middle_terms_1, *waited)
    rests = [sums_0, sums_first_1, sums_1, grad_readout_b.reshape(C, 4).T]
    grad_in, _, grad_first_0, grad_first_other_0, side, side_other = back_first(
        table, 0, G, grads_0, pre1_0, direct_0, misc, rests, mid_0, first_0
    )
    if paired:
        waited = [*sum_middle_0.prepare(grad_in)]
        grad_first_other_0, side_other = after((grad_first_other_0, side_other), *waited)
        side_other = swap(side_other)
        sides = [(side, side_other)]
        sum_middle_0.onward(*waited)
        with jax.named_scope("middle_1_levels"):
            owned_1 = lax.psum_scatter(
                middle_terms_1.reshape(-1, C),
                "dp",
                axis_index_groups=move.lines(),
                scatter_dimension=0,
                tiled=True,
            )
        lefts_other_0 = tie(lefts_other_0, *waited)
    else:
        sides = [(side, None), (side_other, None)]
    grad_first_other_0 = swap(grad_first_other_0)
    last_terms = weight_terms(
        table,
        None,
        [
            (lefts_0, 2, lefts_other_0, grads_0, 0, grads_other_0, 0),
            (lefts_1, 0, lefts_other_1, grad_first_1, 0, grad_first_other_1, None),
            (lefts_1, 2, lefts_other_1, grads_1, 0, grads_other_1, 0),
            (lefts_0, 0, lefts_other_0, grad_first_0, 0, grad_first_other_0, None),
        ],
        sides,
        sums_of(C // half, [rows] * 5),
    )
    if paired:
        sum_last = Sum(move, last_terms, "last")
        waited = sum_middle_0.gather(*last_terms)
        sum_last.across(*waited)
        sum_middle_0.finish()
        core = jnp.reshape(lax.axis_index("fsdp"), (1,))
        readout_owned = place_halves(core, halves(move, sum_readout.owned, 1))[0].reshape(rows, width)
        sum_last.prepare(readout_owned)
        sum_last.onward()
        sum_last.gather()
        middle_owned = place_halves(core, halves(move, sum_middle_0.owned, 1), owned_1[None])
        sum_last.finish(middle_owned)
        first_grad, last_grad, pos_grad, gain_grad, bias_grad, readout_grad = place_last(core, *halves(move, sum_last.owned, 5), cells)
        readout_grad = readout_grad.T
        pos_grad = pos_grad.T
        gain_grad, bias_grad = jnp.swapaxes(gain_grad, 0, 1), jnp.swapaxes(bias_grad, 0, 1)
    else:
        readout_owned = scattered(readout_terms)[0]
        middle_owned = jnp.concatenate([scattered(terms) for terms in (crossed_terms, middle_terms_1)])
        last_owned = scattered(last_terms, 5)
        first_grad, last_grad = jnp.stack([last_owned[3], last_owned[1]]), jnp.stack([last_owned[0], last_owned[2]])
        pos_grad = last_owned[4, :, :cells].T
        scales = last_owned[4, :, cells : cells + MISC]
        gain_grad, bias_grad = scales[:, 0:6].T.reshape(2, 3, rows), scales[:, 6:12].T.reshape(2, 3, rows)
        readout_grad = scales[:, 12:]
    return (
        output[None],
        grad_in[None],
        pos_grad,
        first_grad,
        middle_owned,
        last_grad,
        gain_grad,
        bias_grad,
        readout_owned,
        readout_grad.reshape(-1),
    )


def solution(mesh):
    return jax.shard_map(
        functools.partial(local, Movement(mesh)),
        mesh=mesh,
        in_specs=(
            P(("dp", "fsdp"), None, None),
            P(("dp", "fsdp")),
            P(None, ("dp", "fsdp")),
            P(None, ("dp", "fsdp"), None),
            P(None, ("dp", "fsdp"), None),
            P(None, ("dp", "fsdp"), None),
            P(None, None, ("dp", "fsdp")),
            P(None, None, ("dp", "fsdp")),
            P(("dp", "fsdp"), None),
            P(("dp", "fsdp")),
            P(("dp", "fsdp"), None, None),
        ),
        out_specs=(
            P(("dp", "fsdp"), None, None),
            P(("dp", "fsdp"), None, None),
            P(None, ("dp", "fsdp")),
            P(None, ("dp", "fsdp"), None),
            P(None, ("dp", "fsdp"), None),
            P(None, ("dp", "fsdp"), None),
            P(None, None, ("dp", "fsdp")),
            P(None, None, ("dp", "fsdp")),
            P(("dp", "fsdp"), None),
            P(("dp", "fsdp")),
        ),
        check_vma=False,
    )
```

```python
import functools

import jax
import jax.numpy as jnp
import numpy as np
from jax import lax
from jax.experimental import pallas as pl
from jax.experimental.pallas import tpu as pltpu
from jax.sharding import PartitionSpec as P

C = 1024
G = 24
PLANE = 4
TILE = 256
ROWS = 144
PAD = 24
MISC = 16
HEAD = 1664
SIDE = 384
STEPS, LEVELS, OUT_STEPS, OUT_LEVELS, OUT_LINE, CORE, WINDOWS, TABLE = 0, 32, 64, 80, 96, 112, 113, 165
STEPPED, LEVELED, LINED = range(3)
COST = 4
COSTS = {"forward_block": 50}
VMEM = 60 * 1024 * 1024


def low(value):
    return value.astype(jnp.bfloat16)


def wide(value):
    return value.astype(jnp.float32)


def dot(left, right):
    return jnp.dot(left, right, preferred_element_type=jnp.float32)


def dot_rows(left, right):
    return lax.dot_general(left, right, (((1,), (1,)), ((), ())), preferred_element_type=jnp.float32)


def dot_sums(left, right):
    return lax.dot_general(left, right, (((0,), (0,)), ((), ())), preferred_element_type=jnp.float32)


def sigmoid(value):
    return 1.0 / (1.0 + jnp.exp(-value))


def centered(value):
    center = value - jnp.mean(value, axis=-1, keepdims=True)
    spread = jnp.mean(center * center, axis=-1, keepdims=True)
    scale = lax.rsqrt(spread + 1e-05)
    return center * scale, scale


def norm_back(grad, normal, scale, gain):
    inner = grad * gain
    first = jnp.mean(inner, axis=-1, keepdims=True)
    second = jnp.mean(inner * normal, axis=-1, keepdims=True)
    return scale * (inner - first - normal * second)


def silu_back(value):
    gate = sigmoid(value)
    return gate * (1.0 + value * (1.0 - gate))


def tiles(extent, size, body):
    def step(i, carry):
        body(pl.ds(pl.multiple_of(i * size, size), size))
        return carry

    lax.fori_loop(0, extent // size, step, 0)


def fold(value):
    return jnp.sum(value.reshape(-1, 8, value.shape[-1]), axis=0)


def columns_of(cells, side, lanes):
    index = lax.broadcasted_iota(jnp.int32, (cells, lanes), 0).astype(jnp.float32)
    return index - side * jnp.floor((index + 0.5) * (1.0 / side))


def beside(value, side, step):
    cells = value.shape[0]
    column = columns_of(cells, side, value.shape[1])
    inside = column < side - 1 if step > 0 else column > 0
    return jnp.where(inside, pltpu.roll(value, (cells - step) % cells, 0), 0.0)


class Blocks:
    def __init__(self):
        self.operands = []
        self.moves = []

    def operand(self, array):
        for number, known in enumerate(self.operands):
            if known is array:
                return number
        self.operands.append(array)
        return len(self.operands) - 1

    def add(self, array, block, row, column, place, stride, to_row, to_column, rows, columns):
        self.moves.append((self.operand(array), block, row, column, place, stride, to_row, to_column, rows, columns))

    @property
    def copies(self):
        return len(self.moves)

    def firsts(self, places):
        return [
            to_row + (places[place] * stride if place is not None else jnp.int32(0))
            for _, _, _, _, place, stride, to_row, _, _, _ in self.moves
        ]

    def ends(self, places):
        return [
            to_row + rows + (places[place] * stride if place is not None else 0)
            for _, _, _, _, place, stride, to_row, _, rows, _ in self.moves
        ]

    def bind(self, refs, places, matrix, sems, to_blocks=False, base=0):
        made = []
        for number, block, row, column, place, stride, to_row, to_column, rows, columns in self.moves:
            first = to_row
            if place is not None:
                first = pl.multiple_of(places[place] * stride + to_row, 16)
            inside = matrix.at[pl.ds(first, rows), pl.ds(to_column, columns)]
            outside = refs[number] if block is None else refs[number].at[block]
            outside = outside.at[pl.ds(row, rows), pl.ds(column, columns)]
            pair = (inside, outside) if to_blocks else (outside, inside)
            made.append(pltpu.make_async_copy(*pair, sems.at[base + len(made)]))
        return made


def start(copies):
    for copy in copies:
        copy.start()


def wait(copies):
    for copy in copies:
        copy.wait()


ANY = pl.BlockSpec(memory_space=pltpu.HBM)
IN = pl.BlockSpec(memory_space=pltpu.VMEM)
SMEM = pl.BlockSpec(memory_space=pltpu.SMEM)


def call(kernel, name, ins, in_specs, outs, out_specs, scratch, flops, moved):
    short = COSTS.get(name, COST)
    return pl.pallas_call(
        kernel,
        name=name,
        out_shape=outs,
        in_specs=in_specs,
        out_specs=out_specs,
        scratch_shapes=scratch,
        compiler_params=pltpu.CompilerParams(vmem_limit_bytes=VMEM),
        cost_estimate=pl.CostEstimate(flops=int(flops) // short, bytes_accessed=int(moved) // short, transcendentals=0),
    )(*ins)


class Traffic:
    def __init__(self, sems):
        self.sems = sems
        self.used = 0
        self.sent = []

    def begin(self, source, target):
        copy = pltpu.make_async_copy(source, target, self.sems.at[self.used])
        self.used += 1
        copy.start()
        return copy

    def send(self, source, target):
        self.sent.append(self.begin(source, target))

    def load(self, blocks, refs, places, matrix):
        copies = blocks.bind(refs, places, matrix, self.sems, base=self.used)
        self.used += len(copies)
        start(copies)
        return copies

    def plan(self, blocks, refs, places, matrix):
        copies = blocks.bind(refs, places, matrix, self.sems, to_blocks=True, base=self.used)
        self.used += len(copies)
        self.sent += copies
        return copies

    def plan_in(self, blocks, refs, places, matrix):
        copies = blocks.bind(refs, places, matrix, self.sems, base=self.used)
        self.used += len(copies)
        return copies

    def store(self, blocks, refs, places, matrix):
        start(self.plan(blocks, refs, places, matrix))

    def finish(self):
        wait(self.sent)


def shaped(*shape, dtype=jnp.float32):
    return jax.ShapeDtypeStruct(shape, dtype)


def forward_block(table, number, side, stream, features, misc, w_first, w_middle, w_last):
    cells = side * side
    opening = features is not None
    n_first, n_middle, n_last = len(w_first.operands), len(w_middle.operands), len(w_last.operands)
    given = [features] if opening else [stream, misc]
    given_count = len(given)
    bf16 = jnp.bfloat16
    n_lefts = 3 if opening else 4

    def kernel(table_ref, *refs):
        refs = list(refs)
        heads = [refs.pop(0) for _ in range(given_count)]
        firsts = [refs.pop(0) for _ in range(n_first)]
        middles = [refs.pop(0) for _ in range(n_middle)]
        lasts = [refs.pop(0) for _ in range(n_last)]
        if opening:
            misc_ref, pooled_ref, u_out = refs.pop(0), refs.pop(0), refs.pop(0)
            u_ref = refs.pop(0 - 1)
        else:
            u_ref, misc_ref = heads
        lefts_out, pre1_out, pre2_out, pre3_out, wi_out, wo_out = [refs.pop(0) for _ in range(6)]
        wi, wm, wo, taps, lefts, above, below, work, pairs, pre1, pre2, pre3, sems = refs
        traffic = Traffic(sems)
        first_copies = traffic.load(w_first, firsts, table_ref, wi)
        middle_copies = traffic.plan_in(w_middle, middles, table_ref, wm)
        stages = [lax.div(first, 3 * C) for first in w_middle.firsts(table_ref)]

        def of_stage(stage, act):
            for copy, own in zip(middle_copies, stages):

                @pl.when(own == stage)
                def _(copy=copy):
                    act(copy)

        for stage in range(3):
            of_stage(stage, lambda copy: copy.start())
        last_copies = traffic.load(w_last, lasts, table_ref, wo)
        wait(first_copies)
        traffic.send(wi.at[:, pl.ds(0, C)], wi_out)
        if opening:

            def place(cut):
                turned = jnp.transpose(wide(wi[cut, C:HEAD]))
                u_ref[:, cut] = wide(heads[0][:, cut]) + turned[:cells]
                misc_ref[:, cut] = turned[cells : cells + MISC]

            tiles(C, 128, place)
            traffic.send(u_ref, u_out)

        def lower(rows):
            lefts[0, rows, :] = low(u_ref[rows, :])

        tiles(cells, ROWS, lower)

        def first(cut):
            pre1[:, cut] = dot(lefts[0], wi[:, cut])

        tiles(C, TILE, first)
        traffic.send(pre1, pre1_out)

        def norm_act(source, norm, store):
            gain = misc_ref[3 * number + norm : 3 * number + norm + 1, :]
            bias = misc_ref[6 + 3 * number + norm : 7 + 3 * number + norm, :]

            def rows_of(rows):
                normal, _ = centered(source[rows, :])
                hidden = normal * gain + bias
                store(rows, hidden * sigmoid(hidden))

            tiles(cells, ROWS, rows_of)

        def keep_first(rows, value):
            work[rows, :] = value
            lefts[1, rows, :] = low(value)

        norm_act(pre1, 0, keep_first)

        def spread(i, carry):
            cut = pl.ds(pl.multiple_of(i * 128, 128), 128)
            value = work[:, cut]
            taps[:, pl.ds(pl.multiple_of(i * 128, 128), 128)] = low(beside(value, side, -1))
            taps[:, pl.ds(pl.multiple_of(C + i * 128, 128), 128)] = low(value)
            taps[:, pl.ds(pl.multiple_of(2 * C + i * 128, 128), 128)] = low(beside(value, side, 1))
            return carry

        lax.fori_loop(0, C // 128, spread, 0)
        zeros = jnp.zeros((PAD, TILE), jnp.float32)
        for ref in (above, below):
            ref[:PAD, :] = zeros
            ref[PAD + cells :, :] = zeros
        for tap in range(3):
            of_stage(tap, lambda copy: copy.wait())

            def middle(cut, tap=tap):
                total = dot(taps[...], wm[3 * C * tap : 3 * C * (tap + 1), cut])
                if tap == 1:
                    pre2[:, cut] += total
                else:
                    shift = -side if tap == 0 else side
                    above[PAD : PAD + cells, :] = total
                    moved = above[PAD + shift : PAD + shift + cells, :]
                    if tap == 0:
                        pre2[:, cut] = moved
                    else:
                        pre2[:, cut] += moved

            tiles(C, TILE, middle)
        traffic.send(pre2, pre2_out)

        def keep_second(rows, value):
            lefts[2, rows, :] = low(value)

        norm_act(pre2, 1, keep_second)
        if opening:
            traffic.send(lefts, lefts_out)
        wait(last_copies)
        traffic.send(wo, wo_out)

        def last(cut):
            pre3[:, cut] = dot(lefts[2], wo[:, cut])

        tiles(C, TILE, last)
        traffic.send(pre3, pre3_out)
        gain = misc_ref[3 * number + 2 : 3 * number + 3, :]
        bias = misc_ref[8 + 3 * number : 9 + 3 * number, :]

        def close(rows):
            normal, _ = centered(pre3[rows, :])
            total = u_ref[rows, :] + (normal * gain + bias)
            value = total * sigmoid(total)
            if opening:
                work[rows, :] = value
            else:
                lefts[3, rows, :] = low(value)

        tiles(cells, ROWS, close)
        if opening:
            half = side // 2

            def pool(cut):
                value = work[:, cut].reshape(half, 2, side, 128)
                pairs[...] = (value[:, 0] + value[:, 1]).reshape(half * side, 128)
                pooled_ref[:, cut] = 0.25 * (
                    pairs[pl.ds(0, half * half, 2), :] + pairs[pl.ds(1, half * half, 2), :]
                )

            tiles(C, 128, pool)
        else:
            traffic.send(lefts, lefts_out)
        traffic.finish()

    outs, out_specs = [], []
    if opening:
        outs += [shaped(MISC, C), shaped(cells // 4, C), shaped(cells, C)]
        out_specs += [IN, IN, ANY]
    outs += [shaped(n_lefts, cells, C, dtype=bf16)] + [shaped(cells, C)] * 3 + [shaped(C, C, dtype=bf16)] * 2
    out_specs += [ANY] * 6
    copies = w_first.copies + w_middle.copies + w_last.copies + 7
    scratch = [
        pltpu.VMEM((C, HEAD if opening else C), bf16),
        pltpu.VMEM((9 * C, C), bf16),
        pltpu.VMEM((C, C), bf16),
        pltpu.VMEM((cells, 3 * C), bf16),
        pltpu.VMEM((n_lefts, cells, C), bf16),
        pltpu.VMEM((cells + 2 * PAD, TILE), jnp.float32),
        pltpu.VMEM((cells + 2 * PAD, TILE), jnp.float32),
        pltpu.VMEM((cells, C), jnp.float32),
        pltpu.VMEM((cells // 2, 128), jnp.float32),
        pltpu.VMEM((cells, C), jnp.float32),
        pltpu.VMEM((cells, C), jnp.float32),
        pltpu.VMEM((cells, C), jnp.float32),
        pltpu.SemaphoreType.DMA((copies,)),
    ]
    if opening:
        scratch.append(pltpu.VMEM((cells, C), jnp.float32))
    weights = w_first.operands + w_middle.operands + w_last.operands
    return call(
        kernel,
        "forward_block",
        [table] + given + weights,
        [SMEM] + [IN] * given_count + [ANY] * len(weights),
        outs,
        out_specs,
        scratch,
        2 * cells * 11 * C * C,
        22 * C * C + 20 * cells * C,
    )


def readout(table, live, lefts, bias, cotangent, weights):
    cells, columns = cotangent.shape
    n_weights = len(weights.operands)
    bf16 = jnp.bfloat16
    cut_size = 512
    half = columns // 2

    def kernel(table_ref, live_ref, lefts_ref, bias_ref, cot_ref, *refs):
        refs = list(refs)
        sources = [refs.pop(0) for _ in range(n_weights)]
        output, grad_stream, grad_bias, own, other, matrix, low_ref, sems = refs
        traffic = Traffic(sems)
        given = traffic.begin(lefts_ref.at[3], low_ref)
        copies = traffic.load(weights, sources, table_ref, matrix)
        factor = wide(live_ref[0])
        core = table_ref[CORE]
        grad_stream[...] = jnp.zeros((cells, C), jnp.float32)
        given.wait()
        for part in range(2):
            middle = (len(copies) + 1) // 2
            wait(copies[middle:] if part else copies[:middle])

            def step(cut, part=part):
                here = pl.ds(pl.multiple_of(part * half + cut.start, cut_size), cut_size)
                logits = dot(low_ref[...], matrix[:, here]) + bias_ref[:, here]
                share = 0.5 * (1.0 + lax.erf(logits * (0.5**0.5)))
                output[:, here] = low(logits * share * factor)
                slope = share + logits * (jnp.exp(-0.5 * logits * logits) * (0.5 / jnp.pi) ** 0.5)
                grad_logits = low(wide(cot_ref[:, here]) * factor * slope)
                grad_bias[:, here] = jnp.sum(wide(grad_logits), axis=0, keepdims=True)

                @pl.when(core == part)
                def _():
                    own[:, cut] = grad_logits

                @pl.when(core != part)
                def _():
                    other[:, cut] = grad_logits

                grad_stream[...] += dot_rows(grad_logits, matrix[:, here])

            tiles(half, cut_size, step)

    outs = [shaped(cells, columns, dtype=bf16), shaped(cells, C), shaped(1, columns)]
    outs += [shaped(cells, half, dtype=bf16)] * 2
    scratch = [
        pltpu.VMEM((C, columns), bf16),
        pltpu.VMEM((cells, C), bf16),
        pltpu.SemaphoreType.DMA((weights.copies + 1,)),
    ]
    return call(
        kernel,
        "readout",
        [table, live, lefts, bias, cotangent] + weights.operands,
        [SMEM] * 2 + [ANY] + [IN] * 2 + [ANY] * n_weights,
        outs,
        [IN] * 5,
        scratch,
        4 * cells * C * columns,
        2 * C * columns + 4 * cells * columns,
    )


def back_last(table, number, side, grad_out, stream, pre3, pre2, misc, w_last):
    cells = side * side
    pooled = grad_out.shape[0] != cells
    n_weights = len(w_last.operands)
    bf16 = jnp.bfloat16
    half = C // 2

    def kernel(table_ref, grad_ref, u_in, pre3_in, pre2_in, misc_ref, *refs):
        refs = list(refs)
        sources = [refs.pop(0) for _ in range(n_weights)]
        direct_out, grads, other, sums, matrix, direct, u_ref, pre3_ref, pre2_ref, work, parts, pairs, sems = refs
        traffic = Traffic(sems)
        opened = [traffic.begin(u_in, u_ref), traffic.begin(pre3_in, pre3_ref)]
        later = traffic.begin(pre2_in, pre2_ref)
        copies = traffic.load(w_last, sources, table_ref, matrix)
        parts[...] = jnp.zeros_like(parts)
        gain = misc_ref[3 * number + 2 : 3 * number + 3, :]
        bias = misc_ref[8 + 3 * number : 9 + 3 * number, :]
        if pooled:

            def spread(cut):
                value = 0.25 * grad_ref[:, cut]
                pairs[pl.ds(0, cells // 4, 2), :] = value
                pairs[pl.ds(1, cells // 4, 2), :] = value
                twice = pairs[...].reshape(side // 2, 1, side, 128)
                work[:, cut] = jnp.broadcast_to(twice, (side // 2, 2, side, 128)).reshape(cells, 128)

            tiles(C, 128, spread)
        grad_from = work if pooled else grad_ref
        wait(opened)

        def close(rows):
            normal, scale = centered(pre3_ref[rows, :])
            total = u_ref[rows, :] + (normal * gain + bias)
            inner = grad_from[rows, :] * silu_back(total)
            direct[rows, :] = inner
            parts[0:8, :] += fold(inner * normal)
            parts[8:16, :] += fold(inner)
            grads[0, rows, :] = low(norm_back(inner, normal, scale, gain))

        tiles(cells, ROWS, close)
        traffic.send(direct, direct_out)
        gain = misc_ref[3 * number + 1 : 3 * number + 2, :]
        bias = misc_ref[7 + 3 * number : 8 + 3 * number, :]
        wait(copies)

        def last(cut):
            work[:, cut] = dot_rows(grads[0], matrix[cut, :])

        tiles(C, TILE, last)
        later.wait()

        def norm(rows):
            normal, scale = centered(pre2_ref[rows, :])
            hidden = normal * gain + bias
            inner = work[rows, :] * silu_back(hidden)
            parts[16:24, :] += fold(inner * normal)
            parts[24:32, :] += fold(inner)
            grads[1, rows, :] = low(norm_back(inner, normal, scale, gain))

        tiles(cells, ROWS, norm)
        sums[...] = jnp.sum(parts[...].reshape(4, 8, C), axis=1)
        there = pl.ds(pl.multiple_of((1 - table_ref[CORE]) * half, half), half)
        for i in range(2):
            other[i] = grads[i, :, there]
        traffic.finish()

    outs = [shaped(cells, C), shaped(2, cells, C, dtype=bf16), shaped(2, cells, half, dtype=bf16), shaped(4, C)]
    f32 = jnp.float32
    scratch = [pltpu.VMEM((C, C), bf16)] + [pltpu.VMEM((cells, C), f32)] * 5
    scratch += [pltpu.VMEM((32, C), f32), pltpu.VMEM((cells // 2, 128), f32), pltpu.SemaphoreType.DMA((w_last.copies + 4,))]
    return call(
        kernel,
        "back_last",
        [table, grad_out, stream, pre3, pre2, misc] + w_last.operands,
        [SMEM, IN, ANY, ANY, ANY, IN] + [ANY] * n_weights,
        outs,
        [ANY, IN, IN, IN],
        scratch,
        2 * cells * C * C,
        2 * C * C + 24 * cells * C,
    )


def weight_terms(table, middle, products, sides, out_blocks):
    bf16 = jnp.bfloat16
    if middle is not None:
        products = [(middle[1], 1, middle[2], middle[3], 1, middle[4], 1)] + products
    pair = products[0][2] is not None
    given = []
    for left, _, left_other, right, _, right_other, _ in products:
        given += [left, right] + ([left_other, right_other] if pair else [])
    n_given = len(given)
    n_outs = len(out_blocks.operands)
    width = out_blocks.operands[0].shape[-1]
    cells_of = [product[0].shape[-2] for product in products]
    factor = 2 if pair else 1
    heights = [C] * len(products)
    if middle is not None:
        heights[0] = 9 * C
    starts = [sum(heights[:i]) for i in range(len(heights) + 1)]
    grid_side = middle[0] if middle is not None else 0
    grid_cells = grid_side * grid_side
    size = 512

    def kernel(table_ref, *refs):
        refs = list(refs)
        sources = [refs.pop(0) for _ in range(n_given)]
        beside_refs = [refs.pop(0) for _ in range(len(sides) * factor)]
        targets = [refs.pop(0) for _ in range(n_outs)]
        grad, sems = refs.pop(0), refs.pop(0)
        traffic = Traffic(sems)
        waits = []
        for (_, left_at, _, _, right_at, _, other_at), cells in zip(products, cells_of):
            left, right = refs.pop(0), refs.pop(0)
            left_in, right_in = sources.pop(0), sources.pop(0)
            copies = [traffic.begin(left_in.at[left_at], left.at[pl.ds(0, cells), :])]
            if right_at is not None:
                right_in = right_in.at[right_at]
                if pair:
                    right_in = right_in.at[:, pl.ds(pl.multiple_of(table_ref[CORE] * width, width), width)]
            copies.append(traffic.begin(right_in, right.at[pl.ds(0, cells), :]))
            if pair:
                left_in, right_in = sources.pop(0), sources.pop(0)
                copies.append(traffic.begin(left_in.at[left_at], left.at[pl.ds(cells, cells), :]))
                if other_at is not None:
                    right_in = right_in.at[other_at]
                copies.append(traffic.begin(right_in, right.at[pl.ds(cells, cells), :]))
            waits.append((copies, left, right))
        at = 0
        for side in sides:
            extent = side[0].shape[-1]
            total = beside_refs.pop(0)[...]
            if pair:
                total = low(wide(total) + wide(beside_refs.pop(0)[...]))
            grad[starts[-1] :, at : at + extent] = total
            at += extent
        if sides:
            grad[starts[-1] :, at:] = jnp.zeros((C, width - at), bf16)
        if middle is not None:
            taps, shifted, padded = refs
            copies, act, right = waits[0]
            padded[:PAD, :] = jnp.zeros((PAD, 128), jnp.float32)
            padded[PAD + grid_cells :, :] = jnp.zeros((PAD, 128), jnp.float32)
            wait(copies)
            for first in range(0, factor * grid_cells, grid_cells):
                rows = slice(first, first + grid_cells)

                def spread(i, carry, rows=rows):
                    cut = pl.ds(pl.multiple_of(i * 128, 128), 128)
                    value = wide(act[rows, cut])
                    taps[rows, cut] = low(beside(value, grid_side, -1))
                    taps[rows, pl.ds(pl.multiple_of(C + i * 128, 128), 128)] = act[rows, cut]
                    taps[rows, pl.ds(pl.multiple_of(2 * C + i * 128, 128), 128)] = low(beside(value, grid_side, 1))
                    return carry

                def shift(i, carry, rows=rows):
                    cut = pl.ds(pl.multiple_of(i * 128, 128), 128)
                    padded[PAD : PAD + grid_cells, :] = wide(right[rows, cut])
                    shifted[0, rows, cut] = low(padded[PAD + grid_side : PAD + grid_side + grid_cells, :])
                    shifted[1, rows, cut] = right[rows, cut]
                    shifted[2, rows, cut] = low(padded[PAD - grid_side : PAD - grid_side + grid_cells, :])
                    return carry

                lax.fori_loop(0, C // 128, spread, 0)
                lax.fori_loop(0, width // 128, shift, 0)
            stage = 3 * C // size
            out_copies = traffic.plan(out_blocks, targets, table_ref, grad)
            ends = out_blocks.ends(table_ref)

            def part(i, carry):
                cut = pl.ds(pl.multiple_of(lax.rem(i, stage) * size, size), size)
                target = pl.ds(pl.multiple_of(i * size, size), size)
                grad[target, :] = low(dot_sums(taps[:, cut], shifted[i // stage]))

                @pl.when(lax.rem(i, stage) == stage - 1)
                def _():
                    ready = (i + 1) * size
                    for copy, end in zip(out_copies, ends):

                        @pl.when((end <= ready) & (end > ready - 3 * C))
                        def _(copy=copy):
                            copy.start()

                return carry

            lax.fori_loop(0, 9 * C // size, part, 0)
        for number, (copies, left, right) in enumerate(waits):
            if middle is not None and number == 0:
                continue
            wait(copies)

            def part(cut, number=number, left=left, right=right):
                target = pl.ds(pl.multiple_of(starts[number] + cut.start, TILE), TILE)
                grad[target, :] = low(dot_sums(left[:, cut], right[...]))

            tiles(C, TILE, part)
        if middle is None:
            traffic.store(out_blocks, targets, table_ref, grad)
        traffic.finish()

    outs = [shaped(*array.shape, dtype=bf16) for array in out_blocks.operands]
    scratch = [
        pltpu.VMEM((starts[-1] + (C if sides else 0), width), bf16),
        pltpu.SemaphoreType.DMA((out_blocks.copies + 4 * len(products),)),
    ]
    for cells in cells_of:
        scratch += [pltpu.VMEM((factor * cells, C), bf16), pltpu.VMEM((factor * cells, width), bf16)]
    if middle is not None:
        scratch += [
            pltpu.VMEM((factor * grid_cells, 3 * C), bf16),
            pltpu.VMEM((3, factor * grid_cells, width), bf16),
            pltpu.VMEM((grid_cells + 2 * PAD, 128), jnp.float32),
        ]
    besides = [array for side in sides for array in side if array is not None]
    return call(
        kernel,
        "weight_terms",
        [table] + given + besides,
        [SMEM] + [ANY] * n_given + [IN] * len(besides),
        outs,
        [ANY] * n_outs,
        scratch,
        sum(2 * factor * cells * height * width for cells, height in zip(cells_of, heights)),
        2 * starts[-1] * width + sum(4 * factor * cells * C for cells in cells_of),
    )


def plane_terms(table, side, acts, grads, block_rows):
    cells = side * side
    total = sum(array.shape[0] for array in acts)
    bf16 = jnp.bfloat16
    blocks = 4
    span = 3 * 128

    def kernel(table_ref, *refs):
        refs = list(refs)
        act_refs = [refs.pop(0) for _ in acts]
        grad_refs = [refs.pop(0) for _ in grads]
        target, act, right, taps, terms, sems = refs
        traffic = Traffic(sems)
        copies, row = [], 0
        for source, other in zip(act_refs, grad_refs):
            rows = pl.ds(row, source.shape[0])
            copies += [traffic.begin(source, act.at[rows, :]), traffic.begin(other, right.at[rows, :])]
            row += source.shape[0]
        index = lax.broadcasted_iota(jnp.int32, (total, 128), 0).astype(jnp.float32)
        inside = index - cells * jnp.floor((index + 0.5) * (1.0 / cells))
        line = jnp.floor((inside + 0.5) * (1.0 / side))
        column = inside - side * line
        wait(copies)
        for block in range(blocks):
            for tile in range(3):
                at = WINDOWS + blocks + 4 * (3 * block + tile)
                cut = pl.ds(pl.multiple_of(table_ref[at], 128), 128)
                value = pltpu.roll(wide(act[:, cut]), table_ref[at + 1], 0)
                tap_line = line + (table_ref[at + 2] - 1).astype(jnp.float32)
                tap_column = column + (table_ref[at + 3] - 1).astype(jnp.float32)
                there = (tap_line >= 0) & (tap_line < side) & (tap_column >= 0) & (tap_column < side)
                first = block * span + tile * 128
                taps[:, first : first + 128] = low(jnp.where(there, value, 0.0))
            terms[block] = low(dot_sums(taps[:, block * span : (block + 1) * span], right[...]))
            start_row = pl.multiple_of(table_ref[WINDOWS + block], 32)
            traffic.send(terms.at[block, pl.ds(start_row, block_rows), :], target.at[block])
        traffic.finish()

    return call(
        kernel,
        "plane_terms",
        [table] + acts + grads,
        [SMEM] + [ANY] * (2 * len(acts)),
        shaped(blocks, block_rows, C, dtype=bf16),
        ANY,
        [
            pltpu.VMEM((total, C), bf16),
            pltpu.VMEM((total, C), bf16),
            pltpu.VMEM((total, blocks * span), bf16),
            pltpu.VMEM((blocks, span, C), bf16),
            pltpu.SemaphoreType.DMA((2 * len(acts) + blocks,)),
        ],
        2 * total * blocks * span * C,
        4 * total * C + 2 * blocks * block_rows * C,
    )


def back_first(table, number, side, grads, pre1, direct, misc, rests, w_middle, w_first):
    cells = side * side
    closing = rests is not None
    n_middle, n_first = len(w_middle.operands), len(w_first.operands)
    bf16 = jnp.bfloat16
    extra = rests if closing else []
    half = C // 2
    side_half = SIDE

    def kernel(table_ref, grads_in, pre1_in, direct_in, misc_ref, *refs):
        refs = list(refs)
        rest_refs = [refs.pop(0) for _ in extra]
        middles = [refs.pop(0) for _ in range(n_middle)]
        firsts = [refs.pop(0) for _ in range(n_first)]
        grad_u, sums, grad_pre1, other = [refs.pop(0) for _ in range(4)]
        turned = [refs.pop(0), refs.pop(0)] if closing else None
        wm, wi, grad_ref, pre1_ref, direct_ref, taps, above, work, parts, sems = refs
        traffic = Traffic(sems)
        given = traffic.begin(grads_in.at[1], grad_ref)
        middle_copies = traffic.plan_in(w_middle, middles, table_ref, wm)
        stages = [lax.div(first, 3 * C) for first in w_middle.firsts(table_ref)]

        def of_stage(stage, act):
            for copy, own in zip(middle_copies, stages):

                @pl.when(own == stage)
                def _(copy=copy):
                    act(copy)

        for stage in range(3):
            of_stage(stage, lambda copy: copy.start())
        pre1_copy = traffic.begin(pre1_in, pre1_ref)
        first_copies = traffic.load(w_first, firsts, table_ref, wi)
        direct_copy = traffic.begin(direct_in, direct_ref)
        parts[...] = jnp.zeros_like(parts)
        zeros = jnp.zeros((PAD, TILE), jnp.float32)
        above[:PAD, :] = zeros
        above[PAD + cells :, :] = zeros
        given.wait()

        def spread(i, carry):
            cut = pl.ds(pl.multiple_of(i * 128, 128), 128)
            value = wide(grad_ref[:, cut])
            taps[:, cut] = low(beside(value, side, 1))
            taps[:, pl.ds(pl.multiple_of(C + i * 128, 128), 128)] = grad_ref[:, cut]
            taps[:, pl.ds(pl.multiple_of(2 * C + i * 128, 128), 128)] = low(beside(value, side, -1))
            return carry

        lax.fori_loop(0, C // 128, spread, 0)
        for tap in range(3):
            of_stage(tap, lambda copy: copy.wait())

            def middle(i, carry, tap=tap):
                cut = pl.ds(pl.multiple_of(i * TILE, TILE), TILE)
                total = None
                for column in range(3):
                    source = pl.ds(pl.multiple_of((3 * tap + column) * C + i * TILE, TILE), TILE)
                    term = dot_rows(taps[:, column * C : (column + 1) * C], wm[source, :])
                    total = term if total is None else total + term
                if tap == 1:
                    work[:, cut] += total
                else:
                    shift = side if tap == 0 else -side
                    above[PAD : PAD + cells, :] = total
                    moved = above[PAD + shift : PAD + shift + cells, :]
                    if tap == 0:
                        work[:, cut] = moved
                    else:
                        work[:, cut] += moved
                return carry

            lax.fori_loop(0, C // TILE, middle, 0)
        gain = misc_ref[3 * number : 3 * number + 1, :]
        bias = misc_ref[6 + 3 * number : 7 + 3 * number, :]
        pre1_copy.wait()

        def norm(rows):
            normal, scale = centered(pre1_ref[rows, :])
            hidden = normal * gain + bias
            inner = work[rows, :] * silu_back(hidden)
            parts[0:8, :] += fold(inner * normal)
            parts[8:16, :] += fold(inner)
            grad_pre1[0, rows, :] = low(norm_back(inner, normal, scale, gain))

        tiles(cells, ROWS, norm)
        sums[...] = jnp.sum(parts[...].reshape(2, 8, C), axis=1)
        core = table_ref[CORE]
        other[...] = grad_pre1[0, :, pl.ds(pl.multiple_of((1 - core) * half, half), half)]
        wait(first_copies)
        direct_copy.wait()

        def first(cut):
            grad_u[:, cut] = direct_ref[:, cut] + dot_rows(grad_pre1[0], wi[cut, :])

        tiles(C, TILE, first)
        if closing:

            last_0, first_1, last_1, bias_grad = rest_refs

            def turn(cut):
                stacked = jnp.concatenate(
                    [grad_u[:, cut]]
                    + [ref[row : row + 1, cut] for ref, row in ((sums, 0), (last_0, 2), (last_0, 0))]
                    + [ref[row : row + 1, cut] for ref, row in ((first_1, 0), (last_1, 2), (last_1, 0))]
                    + [ref[row : row + 1, cut] for ref, row in ((sums, 1), (last_0, 3), (last_0, 1))]
                    + [ref[row : row + 1, cut] for ref, row in ((first_1, 1), (last_1, 3), (last_1, 1))]
                    + [bias_grad[:, cut], jnp.zeros((2 * side_half - cells - MISC, 128), jnp.float32)]
                )
                parts_of = low(jnp.transpose(stacked))
                for part in range(2):
                    piece = parts_of[:, part * side_half : (part + 1) * side_half]

                    @pl.when(core == part)
                    def _(piece=piece):
                        turned[0][cut, :] = piece

                    @pl.when(core != part)
                    def _(piece=piece):
                        turned[1][cut, :] = piece

            tiles(C, 128, turn)

    outs = [shaped(cells, C), shaped(2, C), shaped(1, cells, C, dtype=bf16), shaped(cells, half, dtype=bf16)]
    if closing:
        outs += [shaped(C, side_half, dtype=bf16)] * 2
    f32 = jnp.float32
    scratch = [
        pltpu.VMEM((9 * C, C), bf16),
        pltpu.VMEM((C, C), bf16),
        pltpu.VMEM((cells, C), bf16),
        pltpu.VMEM((cells, C), f32),
        pltpu.VMEM((cells, C), f32),
        pltpu.VMEM((cells, 3 * C), bf16),
        pltpu.VMEM((cells + 2 * PAD, TILE), f32),
        pltpu.VMEM((cells, C), f32),
        pltpu.VMEM((16, C), f32),
        pltpu.SemaphoreType.DMA((w_middle.copies + w_first.copies + 3,)),
    ]
    weights = w_middle.operands + w_first.operands
    return call(
        kernel,
        "back_first",
        [table, grads, pre1, direct, misc] + extra + weights,
        [SMEM] + [ANY] * 3 + [IN] * (1 + len(extra)) + [ANY] * len(weights),
        outs,
        [IN] * len(outs),
        scratch,
        2 * cells * 10 * C * C,
        20 * C * C + 24 * cells * C,
    )


def place_halves(core, pair, rest=None):
    _, rows, half = pair[0].shape
    extra = [] if rest is None else [rest]

    def kernel(core_ref, mine, other, *refs):
        target = refs[-1]
        for part in range(2):

            @pl.when(core_ref[0] == part)
            def _(part=part):
                target[0, :, part * half : (part + 1) * half] = mine[0]
                target[0, :, (1 - part) * half : (2 - part) * half] = other[0]

        if extra:
            target[1] = wide(refs[0][0])

    return call(
        kernel,
        "place_halves",
        [core, *pair] + extra,
        [SMEM] + [IN] * (2 + len(extra)),
        shaped(1 + len(extra), rows, 2 * half),
        IN,
        [],
        0,
        16 * rows * half,
    )


def place_last(core, mine, other, cells):
    _, rows, half = mine.shape

    def kernel(core_ref, mine_ref, other_ref, first, last, pos, gains, biases, bias, side):
        for part in range(2):

            @pl.when(core_ref[0] == part)
            def _(part=part):
                for target, block, number in ((last, 0, 0), (first, 1, 1), (last, 1, 2), (first, 0, 3)):
                    target[block, :, part * half : (part + 1) * half] = mine_ref[number]
                    target[block, :, (1 - part) * half : (2 - part) * half] = other_ref[number]
                side[:, part * SIDE : (part + 1) * SIDE] = mine_ref[4, :, :SIDE]
                side[:, (1 - part) * SIDE : (2 - part) * SIDE] = other_ref[4, :, :SIDE]

        pos[...] = side[:, :cells]
        turned = jnp.transpose(side[...])
        for number in range(6):
            gains[number % 3, number // 3 : number // 3 + 1, :] = turned[cells + number : cells + number + 1]
            biases[number % 3, number // 3 : number // 3 + 1, :] = turned[cells + 6 + number : cells + 7 + number]
        bias[...] = turned[cells + 12 : cells + MISC]

    return call(
        kernel,
        "place_last",
        [core, mine, other],
        [SMEM, IN, IN],
        [shaped(2, rows, 2 * half)] * 2 + [shaped(rows, cells)] + [shaped(3, 2, rows)] * 2 + [shaped(4, rows)],
        [IN] * 6,
        [pltpu.VMEM((rows, 2 * SIDE), jnp.float32)],
        0,
        32 * rows * half * 5,
    )


def after(value, *earlier):
    return lax.optimization_barrier((value, earlier))[0]


class Movement:
    def __init__(self, mesh):
        self.dp = mesh.shape["dp"]
        self.cores = mesh.shape["fsdp"]
        self.line = self.dp // PLANE
        self.devices = self.dp * self.cores
        self.ring = [0] + list(range(1, self.line, 2)) + list(range(2, self.line, 2))[::-1]
        self.paired = self.cores == 2 and self.line == 4

    def flip(self, value, bits):
        return lax.ppermute(value, "dp", [(i, i ^ bits) for i in range(self.dp)])

    def along(self, value):
        pairs = []
        for position, level in enumerate(self.ring):
            following = self.ring[(position + 1) % self.line]
            pairs += [(level * PLANE + near, following * PLANE + near) for near in range(PLANE)]
        return lax.ppermute(value, "dp", pairs)

    def swap(self, value):
        return lax.ppermute(value, "fsdp", [(0, 1), (1, 0)])

    def lines(self):
        return [[level * PLANE + near for level in range(self.line)] for near in range(PLANE)]

    def table(self):
        if not self.paired:
            return jnp.zeros((TABLE,), jnp.int32)
        steps, chips = range(self.line), range(PLANE)
        halves = [(1, 0), (1, 1), (3, 0), (3, 1), (2, 2), (2, 3), (3, 2), (3, 3), (1, 2), (1, 3), (2, 0), (2, 1)]
        halves += [(0, step) for step in steps]
        rows = []
        for device in range(self.devices):
            chip, core = divmod(device, 2)
            level, near = divmod(chip, PLANE)
            position = self.ring.index(level)

            def chip_at(far, level, near=near):
                return level * PLANE + (near ^ far)

            def step_at(step, position=position):
                return self.ring[(position + step) % self.line]

            row = [chip_at(far, step_at(-step)) * 2 + (core + k) % 2 for k in range(2) for far in chips for step in steps]
            row += [chip_at(far, step) * 2 + (core + k) % 2 for k in range(2) for far in chips for step in steps]
            row += [chip_at(far, step_at(step)) for far, step in halves]
            row += [chip_at(far, step) for far, step in halves]
            row += [chip_at(far, step_at(step)) for step in reversed(steps) for far in chips]
            row.append(core)
            firsts = [chip_at(0, step) * 2 + core for step in steps]
            firsts = [9 * C // self.devices * owner for owner in firsts]
            row += [first % 128 for first in firsts]
            side = G // 2
            for first in firsts:
                for tile in range(first // 128, first // 128 + 3):
                    tap, part = divmod(tile, C // 128)
                    tap_row, tap_column = divmod(tap, 3)
                    away = (tap_row - 1) * side + tap_column - 1
                    row += [128 * part, -away % (2 * PLANE * side * side), tap_row, tap_column]
            rows.append(row)
        index = lax.axis_index("dp") * self.cores + lax.axis_index("fsdp")
        return lax.dynamic_index_in_dim(jnp.asarray(np.array(rows, np.int32)), index, 0, keepdims=False)


class Piece:
    def __init__(self, move, own, name):
        self.move = move
        self.own = own
        self.name = name
        self.rows = own.shape[0]
        self.at = STEPS
        self.found = []

    def keep(self, array, far, steps, first=0, other=None):
        for i, step in enumerate(steps):
            for core, held in enumerate((array, other)):
                self.found.append((held, first + i * self.rows, self.at + 16 * core + 4 * far + step))

    def line(self, second=(), third=(), first=()):
        with jax.named_scope(self.name + "_line"):
            one = self.move.along(after(self.own, *first) if first else self.own)
            two = self.move.along(after(one, *second) if second else one)
            three = self.move.along(after(two, *third) if third else two)
        self.passed = (one, two, three)
        self.held = jnp.concatenate([self.own, one, two, three])

    def levels(self, *earlier):
        with jax.named_scope(self.name + "_levels"):
            own = after(self.own, *earlier) if earlier else self.own
            self.held = lax.all_gather(own, "dp", axis_index_groups=self.move.lines(), axis=0, tiled=True)
        self.at = LEVELS

    def settle_line(self, *earlier):
        with jax.named_scope("swap"):
            other = self.move.swap(after(self.held, *earlier) if earlier else self.held)
        self.keep(self.held, 0, range(4), other=other)

    def plane_first(self, *earlier):
        half = self.rows // 2
        own = after(self.own, *earlier) if earlier else self.own
        with jax.named_scope(self.name + "_plane"):
            first, second = self.sides = self.move.flip(own, 1), self.move.flip(own, 2)
            self.fars = (self.move.flip(first[:half], 2), self.move.flip(second[half:], 1))
            self.passed = (jnp.concatenate([self.own, first, second, *self.fars]),)

    def pass_on(self, *earlier):
        with jax.named_scope(self.name + "_line"):
            self.passed += (self.move.along(after(self.passed[-1], *earlier)),)

    def end_line(self, *earlier):
        for step, array in enumerate(after(self.passed, *earlier)):
            other = self.move.swap(array)
            for far in range(PLANE):
                self.keep(array, far, [step], first=far * self.rows, other=other)


def cross(move, pieces, fars, *earlier):
    over_first = [piece.held for piece in pieces] + [piece.second[2 * piece.rows : 4 * piece.rows] for piece in fars]
    over_second = [piece.held for piece in pieces] + [piece.first[: 2 * piece.rows] for piece in fars]
    over_first, over_second = [jnp.concatenate(parts) if len(parts) > 1 else parts[0] for parts in (over_first, over_second)]
    if earlier:
        over_first, over_second = after((over_first, over_second), *earlier)
    with jax.named_scope("_".join(piece.name for piece in pieces + fars) + "_plane"):
        first, second = move.flip(over_first, 1), move.flip(over_second, 2)
    row = 0
    for piece in pieces:
        piece.sides = (first, second, row)
        piece.first = first[row : row + 4 * piece.rows]
        piece.second = second[row : row + 4 * piece.rows]
        row += 4 * piece.rows
    for piece in fars:
        piece.far_sides = (first, second, row)
        piece.far_first = first
        row += 2 * piece.rows
    return first, second


def settle(move, pieces, fars, *earlier):
    first, second = (pieces[0].sides if pieces else fars[0].far_sides)[:2]
    if earlier:
        first, second = after((first, second), *earlier)
    with jax.named_scope("swap"):
        first_other, second_other = move.swap(first), move.swap(second)
    for piece in pieces:
        row = piece.sides[2]
        piece.first = first[row : row + 4 * piece.rows]
        piece.second = second[row : row + 4 * piece.rows]
        piece.keep(first, 1, range(4), first=row, other=first_other)
        piece.keep(second, 2, range(4), first=row, other=second_other)
    for piece in fars:
        row = piece.far_sides[2]
        piece.keep(first, 3, (2, 3), first=row, other=first_other)
        piece.keep(second, 3, (0, 1), first=row, other=second_other)


class Spread:
    def __init__(self, move, own, *earlier):
        self.move = move
        self.own = after(own, *earlier) if earlier else own
        with jax.named_scope("spread"):
            self.sides = tuple(move.flip(self.own, bits) for bits in (1, 2, 3))

    def end(self, *earlier):
        with jax.named_scope("spread_swap"):
            here = jnp.concatenate(after((self.own, *self.sides), *earlier))
            self.all = [here, self.move.swap(here)]


class Sum:
    def __init__(self, move, arrays, name, levels=False):
        self.move = move
        self.arrays = arrays
        self.name = name
        self.levels = levels

    def across(self, *earlier):
        first, second = after(tuple(self.arrays[:2]), *earlier) if earlier else self.arrays[:2]
        with jax.named_scope(self.name + "_across"):
            self.first = self.move.flip(first, 1)
            self.second = self.move.flip(second, 2)
        return self.first, self.second

    def prepare(self, *earlier):
        self.first, self.second = after((self.first, self.second), *earlier)
        with jax.named_scope(self.name + "_onward"):
            self.rests = (
                low(wide(self.arrays[2]) + wide(self.second[2:])),
                low(wide(self.arrays[3]) + wide(self.first[2:])),
            )
        self.operands = self.rests
        return self.rests

    def onward(self, *earlier):
        rests = after(self.rests, *earlier) if earlier else self.rests
        with jax.named_scope(self.name + "_onward"):
            self.rests = (self.move.flip(rests[0], 1), self.move.flip(rests[1], 2))

    def gather(self, *earlier):
        rests = after(self.rests, *earlier) if earlier else self.rests
        with jax.named_scope(self.name + "_held"):
            held = self.arrays[4]
            self.near = wide(held[:2]) + wide(self.first[:2]) + wide(rests[1])
            self.far = wide(held[2:]) + wide(self.second[:2]) + wide(rests[0])
            if self.levels:
                held = jnp.concatenate([low(self.near), low(self.far)])
                self.held = held.reshape(-1, held.shape[-1])
                return self.held
            self.far = (self.far[0], low(self.far[1]))
            return self.far

    def finish(self, *earlier):
        with jax.named_scope(self.name + "_line"):
            if self.levels:
                lines = self.move.lines()
                owned = lax.psum_scatter(self.held, "dp", axis_index_groups=lines, scatter_dimension=0, tiled=True)
                self.owned = wide(owned)
            else:
                three = self.move.along(self.far[1])
                two = self.move.along(low(self.far[0] + wide(three)))
                two = after(two, *earlier) if earlier else two
                one = self.move.along(low(self.near[1] + wide(two)))
                self.passed = (three, two, one)
                self.owned = self.near[0] + wide(one)


class LineSum:
    def __init__(self, move, arrays, name):
        self.move = move
        self.arrays = arrays
        self.name = name
        self.next = arrays[0]

    def line(self, step, *earlier):
        value = after(self.next, *earlier) if earlier else self.next
        with jax.named_scope(f"{self.name}_line{step}"):
            self.sent = self.move.along(value)

    def prepare(self, step, *earlier):
        with jax.named_scope(f"{self.name}_line{step}"):
            sent = after(self.sent, *earlier) if earlier else self.sent
            self.next = low(wide(self.arrays[step]) + wide(sent))
        return self.next

    def prepare_across(self, *earlier):
        sent = after(self.sent, *earlier) if earlier else self.sent
        with jax.named_scope(self.name + "_across"):
            held = wide(self.arrays[3]) + wide(sent)
            half = held.shape[1] // 2
            self.near, self.rest = held[:, :half], held[:, half:]
            self.operands = (low(self.near[1::2]), low(self.rest[2:]))
        return self.operands

    def across(self, *earlier):
        operands = after(self.operands, *earlier) if earlier else self.operands
        with jax.named_scope(self.name + "_across"):
            self.first = self.move.flip(operands[0], 1)
            self.second = self.move.flip(operands[1], 2)

    def prepare_onward(self, *earlier):
        self.first, self.second = after((self.first, self.second), *earlier) if earlier else (self.first, self.second)
        with jax.named_scope(self.name + "_onward"):
            self.operands = (low(self.rest[1] + wide(self.second[1])), low(self.near[2] + wide(self.first[1])))
        return self.operands

    def finish(self, *earlier):
        operands = after(self.operands, *earlier) if earlier else self.operands
        with jax.named_scope(self.name + "_onward"):
            first_rest = self.move.flip(operands[0], 1)
            second_rest = self.move.flip(operands[1], 2)
            near = self.near[0] + wide(self.first[0]) + wide(second_rest)
            rest = self.rest[0] + wide(self.second[0]) + wide(first_rest)
            self.owned = jnp.concatenate([near, rest])


def whole_matrix(array):
    blocks = Blocks()
    blocks.add(array, None, 0, 0, None, 0, 0, 0, *array.shape)
    return blocks


def halves(move, owned, matrices):
    blocks = owned.reshape(matrices, 2, -1, owned.shape[-1])
    core = lax.axis_index("fsdp")
    mine = lax.dynamic_index_in_dim(blocks, core, 1, keepdims=False)
    return mine, move.swap(lax.dynamic_index_in_dim(blocks, 1 - core, 1, keepdims=False))


def local(
    move,
    features,
    grid_live,
    pos_embed,
    w_in,
    w_mid,
    w_out,
    norm_gain,
    norm_bias,
    readout_w,
    readout_b,
    cotangent,
):
    rows, middle_rows, width = w_in.shape[1], w_mid.shape[1], readout_w.shape[1]
    cells = pos_embed.shape[0]
    half_side = G // 2
    paired = move.paired
    scales = [norm_gain.reshape(6, rows).T, norm_bias.reshape(6, rows).T, readout_b.reshape(rows, 4)]
    beside = jnp.concatenate([pos_embed.T, *scales, jnp.zeros((rows, C - cells - MISC), jnp.bfloat16)], axis=1)
    if paired:
        cut = middle_rows // 2
        stacks = [
            [w_in[0], beside, w_out[0]],
            [w_mid[0, :cut]],
            [w_mid[0, cut:], w_in[1], w_out[1]],
            [w_mid[1]],
            [readout_w[:, i * C : (i + 1) * C] for i in range(width // C)],
        ]
        one, two, three, four, top = [
            Piece(move, jnp.concatenate(stack) if len(stack) > 1 else stack[0], name)
            for stack, name in zip(stacks, ("one", "two", "three", "four", "top"))
        ]
        one.line()
        top.plane_first(one.passed[0])
        two.line(one.passed[1:2], one.passed[2:])
        three.line(two.passed[1:2], two.passed[2:])
        four.line(first=three.passed[2:])
        cross(move, [one], [], *top.fars)
        cross(move, [two], [one], one.first)
        one.settle_line(one.first)
        settle(move, [one], [], one.first)
        cross(move, [three], [two], two.first)
        two.settle_line(two.first)
        settle(move, [two], [one], two.first)
        top.pass_on(four.passed[1])
        cross(move, [], [three], three.first, four.held)
        three.settle_line(three.first)
        settle(move, [three], [two], three.first)
        cross(move, [four], [], three.far_first)
        top.pass_on(three.far_first)
        settle(move, [], [three], three.far_first, top.passed[1])
        lies = {
            "head_0": [(one, 0, rows, 0, 0, C), (one, rows, rows, 0, C, HEAD - C)],
            "middle_0": [(two, 0, cut, 0, 0, C), (three, 0, cut, cut, 0, C)],
            "last_0": [(one, 2 * rows, rows, 0, 0, C)],
            "first_1": [(three, cut, rows, 0, 0, C)],
            "last_1": [(three, cut + rows, rows, 0, 0, C)],
            "middle_1": [(four, 0, middle_rows, 0, 0, C)],
            "readout": [(top, i * rows, rows, 0, i * C, C) for i in range(width // C)],
        }
    else:

        def whole(own):
            return lax.all_gather(own, ("dp", "fsdp"), axis=0, tiled=True)

        first_all = whole(w_in[0])
        lies = {
            "head_0": [(first_all, 0), (whole(beside[:, : HEAD - C]), C)],
            "middle_0": [(whole(w_mid[0]), 0)],
            "last_0": [(whole(w_out[0]), 0)],
            "first_1": [(whole(w_in[1]), 0)],
            "last_1": [(whole(w_out[1]), 0)],
            "middle_1": [(whole(w_mid[1]), 0)],
            "readout": [(whole(readout_w), 0)],
        }

    def matrix(name):
        blocks = Blocks()
        if not paired:
            for array, column in lies[name]:
                blocks.add(array, None, 0, 0, None, 0, 0, column, *array.shape)
            return blocks
        stride = middle_rows if name.startswith("middle") else rows
        for piece, row, extent, to_row, to_column, columns in lies[name]:
            for array, first, place in piece.found:
                blocks.add(array, None, first + row, 0, place, stride, to_row, to_column, extent, columns)
        return blocks

    def sums_of(columns, matrices, pieces=((None, STEPPED),)):
        blocks = Blocks()
        if not paired:
            extent = sum(matrices) * move.devices
            blocks.add(shaped(1, extent, columns), 0, 0, 0, None, 0, 0, 0, extent, columns)
            return blocks
        runs, start = [], 0
        for block_rows in matrices:
            runs.append((start, 2 * block_rows, 0))
            start += move.devices * block_rows
        for cut, kind in pieces:
            taken = []
            while runs and cut != 0:
                start, stride, first = runs.pop(0)
                extent = stride - first if cut is None else min(cut, stride - first)
                taken.append((start + first, stride, extent))
                if first + extent < stride:
                    runs.insert(0, (start, stride, first + extent))
                cut = None if cut is None else cut - extent
            place = {STEPPED: OUT_STEPS, LEVELED: OUT_LEVELS, LINED: OUT_LINE}[kind]
            for count in (4, 4, 4, 4) if kind == LINED else (4, 4, 2, 2, 4):
                array = shaped(count, sum(extent for _, _, extent in taken), columns)
                for block in range(count):
                    row = 0
                    for first, stride, extent in taken:
                        blocks.add(array, block, row, 0, place, stride, first, 0, extent, columns)
                        row += extent
                    place += 1
        return blocks

    def swap(value):
        return move.swap(value) if paired else None

    def tie(value, *earlier):
        return after(value, *earlier) if paired else value

    def scattered(terms, matrices=1):
        total = wide(terms[0][0]).reshape(matrices, -1, terms[0].shape[-1])
        return lax.psum_scatter(total, ("dp", "fsdp"), scatter_dimension=1, tiled=True)

    half = 2 if paired else 1
    table = move.table()
    mid_0, last_0 = matrix("middle_0"), matrix("last_0")
    misc, pooled, stream_in, lefts_0, pre1_0, pre2_0, pre3_0, first_0, last_0 = forward_block(
        table, 0, G, None, features[0], None, matrix("head_0"), mid_0, last_0
    )
    lefts_other_0 = swap(lefts_0)
    if paired:
        settle(move, [four], [], pooled)
        cross(move, [], [four], top.passed[2])
        top.pass_on(pooled)
        four.settle_line(pooled)
        settle(move, [], [four])
    readout_bias = misc[12:].T.reshape(1, width)
    first_1, mid_1, last_1 = matrix("first_1"), matrix("middle_1"), matrix("last_1")
    if paired:
        top.end_line(pooled)
        pooled = tie(pooled, top.passed[3], readout_bias)
    lefts_1, pre1_1, pre2_1, pre3_1, first_1, last_1 = forward_block(
        table, 1, half_side, pooled, None, misc, first_1, mid_1, last_1
    )
    first_0, last_0, first_1, last_1 = [whole_matrix(array) for array in (first_0, last_0, first_1, last_1)]
    lefts_other_1 = swap(lefts_1)
    output, grad_top, grad_readout_b, grad_logits, grad_logits_other = readout(
        table, grid_live, tie(lefts_1, lefts_other_0), readout_bias, cotangent[0], matrix("readout")
    )
    if paired:
        acts = Spread(move, lefts_1[1])
        grad_logits_other = swap(after(grad_logits_other, *acts.sides))
        grad_top = after(grad_top, *acts.sides)
    else:
        grad_logits, grad_logits_other = jnp.concatenate([grad_logits, grad_logits_other], axis=1), None
    direct_1, grads_1, grads_other_1, sums_1 = back_last(
        table, 1, half_side, grad_top, pooled, pre3_1, pre2_1, misc, last_1
    )
    if paired:
        grads_other_1 = tie(grads_other_1, grad_logits_other)
    grads_other_1 = swap(grads_other_1)
    readout_terms = weight_terms(
        table,
        None,
        [(lefts_1, 3, lefts_other_1, tie(grad_logits, sums_1), None, grad_logits_other, None)],
        [],
        sums_of(width // half, [rows], [(None, LEVELED)]),
    )
    if paired:
        sum_readout = Sum(move, readout_terms, "readout", levels=True)
        spread = Spread(move, grads_1[1], *readout_terms)
        sum_readout.across(grads_other_1)
        grads_1 = tie(grads_1, *readout_terms, grads_other_1)
    else:
        middle_terms_1 = weight_terms(
            table,
            (half_side, lefts_1, lefts_other_1, grads_1, grads_other_1),
            [],
            [],
            sums_of(C // half, [middle_rows]),
        )
    grad_pooled, sums_first_1, grad_first_1, grad_first_other_1 = back_first(
        table, 1, half_side, grads_1, pre1_1, direct_1, misc, None, mid_1, first_1
    )
    direct_0, grads_0, grads_other_0, sums_0 = back_last(
        table, 0, G, grad_pooled, stream_in, pre3_0, pre2_0, misc, last_0
    )
    if paired:
        waited = [*sum_readout.prepare(sums_0), *after(spread.sides, sums_0)]
        lefts_other_0 = tie(lefts_other_0, *waited)
        grads_other_0, grad_first_other_1 = after((grads_other_0, grad_first_other_1), *waited)
        spread.end(*waited)
        acts.end(*waited)
        sum_readout.onward(*waited)
    grads_other_0, grad_first_other_1 = swap(grads_other_0), swap(grad_first_other_1)
    crossed_terms = weight_terms(
        table,
        (G, lefts_0, lefts_other_0, grads_0, grads_other_0),
        [],
        [],
        sums_of(C // half, [middle_rows]),
    )
    if paired:
        sum_middle_0 = Sum(move, crossed_terms, "middle_0")
        waited = [sum_readout.gather(*crossed_terms), *after((*spread.all, *acts.all), *crossed_terms)]
        sum_readout.finish()
        sum_middle_0.across(*waited)
        acts.all[0] = tie(acts.all[0], *waited)
        middle_terms_1 = plane_terms(table, half_side, acts.all, spread.all, middle_rows)
        grads_0 = tie(grads_0, middle_terms_1, *waited)
    rests = [sums_0, sums_first_1, sums_1, grad_readout_b.reshape(C, 4).T]
    grad_in, _, grad_first_0, grad_first_other_0, side, side_other = back_first(
        table, 0, G, grads_0, pre1_0, direct_0, misc, rests, mid_0, first_0
    )
    if paired:
        waited = [*sum_middle_0.prepare(grad_in)]
        grad_first_other_0, side_other = after((grad_first_other_0, side_other), *waited)
        side_other = swap(side_other)
        sides = [(side, side_other)]
        sum_middle_0.onward(*waited)
        with jax.named_scope("middle_1_levels"):
            owned_1 = lax.psum_scatter(
                middle_terms_1.reshape(-1, C),
                "dp",
                axis_index_groups=move.lines(),
                scatter_dimension=0,
                tiled=True,
            )
        lefts_other_0 = tie(lefts_other_0, *waited)
    else:
        sides = [(side, None), (side_other, None)]
    grad_first_other_0 = swap(grad_first_other_0)
    last_terms = weight_terms(
        table,
        None,
        [
            (lefts_0, 2, lefts_other_0, grads_0, 0, grads_other_0, 0),
            (lefts_1, 0, lefts_other_1, grad_first_1, 0, grad_first_other_1, None),
            (lefts_1, 2, lefts_other_1, grads_1, 0, grads_other_1, 0),
            (lefts_0, 0, lefts_other_0, grad_first_0, 0, grad_first_other_0, None),
        ],
        sides,
        sums_of(C // half, [rows] * 5),
    )
    if paired:
        sum_last = Sum(move, last_terms, "last")
        waited = sum_middle_0.gather(*last_terms)
        sum_last.across(*waited)
        sum_middle_0.finish()
        core = jnp.reshape(lax.axis_index("fsdp"), (1,))
        readout_owned = place_halves(core, halves(move, sum_readout.owned, 1))[0].reshape(rows, width)
        sum_last.prepare(readout_owned)
        sum_last.onward()
        sum_last.gather()
        middle_owned = place_halves(core, halves(move, sum_middle_0.owned, 1), owned_1[None])
        sum_last.finish(middle_owned)
        first_grad, last_grad, pos_grad, gain_grad, bias_grad, readout_grad = place_last(core, *halves(move, sum_last.owned, 5), cells)
        readout_grad = readout_grad.T
        pos_grad = pos_grad.T
        gain_grad, bias_grad = jnp.swapaxes(gain_grad, 0, 1), jnp.swapaxes(bias_grad, 0, 1)
    else:
        readout_owned = scattered(readout_terms)[0]
        middle_owned = jnp.concatenate([scattered(terms) for terms in (crossed_terms, middle_terms_1)])
        last_owned = scattered(last_terms, 5)
        first_grad, last_grad = jnp.stack([last_owned[3], last_owned[1]]), jnp.stack([last_owned[0], last_owned[2]])
        pos_grad = last_owned[4, :, :cells].T
        scales = last_owned[4, :, cells : cells + MISC]
        gain_grad, bias_grad = scales[:, 0:6].T.reshape(2, 3, rows), scales[:, 6:12].T.reshape(2, 3, rows)
        readout_grad = scales[:, 12:]
    return (
        output[None],
        grad_in[None],
        pos_grad,
        first_grad,
        middle_owned,
        last_grad,
        gain_grad,
        bias_grad,
        readout_owned,
        readout_grad.reshape(-1),
    )


def solution(mesh):
    return jax.shard_map(
        functools.partial(local, Movement(mesh)),
        mesh=mesh,
        in_specs=(
            P(("dp", "fsdp"), None, None),
            P(("dp", "fsdp")),
            P(None, ("dp", "fsdp")),
            P(None, ("dp", "fsdp"), None),
            P(None, ("dp", "fsdp"), None),
            P(None, ("dp", "fsdp"), None),
            P(None, None, ("dp", "fsdp")),
            P(None, None, ("dp", "fsdp")),
            P(("dp", "fsdp"), None),
            P(("dp", "fsdp")),
            P(("dp", "fsdp"), None, None),
        ),
        out_specs=(
            P(("dp", "fsdp"), None, None),
            P(("dp", "fsdp"), None, None),
            P(None, ("dp", "fsdp")),
            P(None, ("dp", "fsdp"), None),
            P(None, ("dp", "fsdp"), None),
            P(None, ("dp", "fsdp"), None),
            P(None, None, ("dp", "fsdp")),
            P(None, None, ("dp", "fsdp")),
            P(("dp", "fsdp"), None),
            P(("dp", "fsdp")),
        ),
        check_vma=False,
    )
```
